32 devices in a mesh: dp: 8 (over y, x, core), expert: 4 (over z).
Axes of the slice: x: 2, y: 2, z: 4, core: 2. Of those that a mesh axis runs over, the one named last changes fastest.
Arguments:
- tokens: bfloat16 [16384, 768], P(('dp', 'expert')), may hold values from -6 to 6
- query_weight: bfloat16 [768, 768], P('dp'), may hold values from -0.21875 to 0.21875
- key_weight: bfloat16 [768, 768], P('dp'), may hold values from -0.21875 to 0.21875
- value_weight: bfloat16 [768, 768], P('dp'), may hold values from -0.21875 to 0.21875
- project_weight: bfloat16 [768, 768], P('dp'), may hold values from -0.875 to 0.875
- router_weight: bfloat16 [768, 8], P('dp'), may hold values from -0.21875 to 0.21875
- prenorm_gain: bfloat16 [768], P('dp'), may hold values from 0.5 to 1.5
- midnorm_gain: bfloat16 [768], P('dp'), may hold values from 0.5 to 1.5
- bias_table: bfloat16 [32, 12], P('dp'), may hold values from -5 to 5
- up_weight: bfloat16 [8, 768, 3072], P('expert', None, 'dp'), may hold values from -0.21875 to 0.21875
- down_weight: bfloat16 [8, 3072, 768], P('expert', 'dp'), may hold values from -0.109375 to 0.109375
- routes: int32 [16384, 2], P(('dp', 'expert')), may hold values from 0 to 7, all different within a row; in each aligned block of 512 rows (0 to 511, 512 to 1023, ...) at most 192 rows name the same one
- bucket_index: int32 [512], replicated, may hold values from 0 to 31
- cotangent: bfloat16 [16384, 768], P(('dp', 'expert')), may hold values from -6 to 6
Outputs:
- layer_out: bfloat16 [16384, 768], P(('dp', 'expert'))
- inputs_grad: bfloat16 [16384, 768], P(('dp', 'expert'))
- query_grad: float32 [768, 768], P('dp')
- key_grad: float32 [768, 768], P('dp')
- value_grad: float32 [768, 768], P('dp')
- project_grad: float32 [768, 768], P('dp')
- router_grad: float32 [768, 8], P('dp')
- prenorm_grad: float32 [768], P('dp')
- midnorm_grad: float32 [768], P('dp')
- table_grad: float32 [32, 12], P('dp')
- up_grad: float32 [8, 768, 3072], P('expert', None, 'dp')
- down_grad: float32 [8, 3072, 768], P('expert', 'dp')
The draws below stay inside these ranges and needn't reach their ends.
Inputs may be any that keep to these rules, and one draw needn't show every extreme that they name: `routes`: among the 512 rows of one sequence no expert is named more than 192 times, and in every draw some expert is named exactly 192 times in some sequence; the two experts of a token differ.
All inputs are finite; a program needn't handle non-finite values.
Results may differ from the reference program's by a relative error of at most 0.019.
Values may be sent and summed in bfloat16 or wider, within the bound.
A program may use at most 256 MiB of HBM per device.

```python
import math
import jax
import jax.numpy as jnp
import numpy as np
from jax import lax

D = 768
HEADS = 12
HEAD_DIM = 64
FF = 3072
BUCKETS = 32
SEQ = 512
EXPERTS = 8
CAP = 192
TOKENS = 16384


def with_ends(values, key, low, top_value):
    index_at = [jax.random.randint(jax.random.fold_in(key, axis), (), 0, length) for axis, length in enumerate(values.shape)]
    longest = values.shape.index(max(values.shape))
    neighbour = index_at[:longest] + [(index_at[longest] + 1) % values.shape[longest]] + index_at[longest + 1:]
    return values.at[tuple(index_at)].set(low).at[tuple(neighbour)].set(top_value)


def level_of(stream_key, extent, cuts, low, top_value):
    level = 1.0
    for axis_at, parts in cuts:
        draws = jax.random.uniform(jax.random.fold_in(jax.random.fold_in(stream_key, 6), axis_at), (parts,), jnp.float32, low / len(cuts), top_value / len(cuts))
        level = level * jnp.repeat(jnp.exp(draws), extent[axis_at] // parts).reshape((-1,) + (1,) * (len(extent) - 1 - axis_at))
    return level


def deal_out(stream_key, own, number, rows, number_of, top, limit, lean):
    order = jax.random.permutation(stream_key, number_of)
    heavy_load, common = load_shares(number_of, rows * top, limit, lean, True), load_shares(number_of, rows * top, limit, lean, False)
    places = jnp.arange(number_of)

    def named(lengths, offset_by):
        used = int((lengths > 0).sum())
        fixed = max(1, used // 4)
        shifted = fixed + (places - fixed + offset_by * (used - fixed)) % max(1, number_of - fixed)
        return jnp.zeros((number_of,), jnp.int32).at[order[jnp.where(places < fixed, places, shifted)]].set(jnp.asarray(lengths, jnp.int32))

    lengths = jnp.where(number % 4 == 0, named(heavy_load, number // 4), named(common, number - number // 4 - 1))
    mixed = jax.random.permutation(jax.random.fold_in(own, 3), number_of)
    giver, sink = mixed[0:number_of // 2 * 2:2], mixed[1:number_of // 2 * 2:2]
    room = jnp.minimum(lengths[giver] - 1, limit - lengths[sink]) // 2
    room = jnp.where((giver == order[0]) | (sink == order[0]) | (lengths[sink] == 0), 0, jnp.maximum(room, 0))
    shifted = jax.random.randint(jax.random.fold_in(own, 4), (number_of // 2,), 0, 1 << 20) % (room + 1)
    lengths = lengths.at[giver].add(-shifted).at[sink].add(shifted)
    members = jnp.searchsorted(jnp.cumsum(lengths), jnp.arange(rows * top), side="right").astype(jnp.int32)
    grid = members.reshape(top, rows).T
    grid = grid[jax.random.permutation(jax.random.fold_in(own, 1), rows)]
    offset_by = jax.random.randint(jax.random.fold_in(own, 2), (rows, 1), 0, top)
    return jnp.take_along_axis(grid, (jnp.arange(top)[None, :] + offset_by) % top, axis=1)


def load_shares(amount, total, bound, lean, full):
    weights = [(1 << 20) // math.isqrt(rank ** lean) + 1 for rank in range(1, amount + 1)]
    largest = bound if full else min(bound, max(-(-total // amount), total * weights[0] // sum(weights)))
    least = 1 if total - largest >= amount - 1 else 0
    given, rest = [largest] + [least] * (amount - 1), total - largest - least * (amount - 1)
    while rest > 0:
        free = [i for i in range(1, amount) if given[i] < largest] or [i for i in range(1, amount) if given[i] < bound]
        pool, remaining = sum([weights[i] for i in free]), rest
        for i in free:
            addition = min(bound - given[i], max(1, remaining * weights[i] // pool), rest)
            given[i] = given[i] + addition
            rest = rest - addition
    return np.array(given)


def gaussian(rng, shape, spread, most, shards=(), held_as=jnp.bfloat16):
    factor_of = level_of(rng, shape, shards, -0.22, 0.18) if shards else 1.0
    values = jax.random.normal(rng, shape, jnp.float32) * spread * factor_of
    return jnp.minimum(jnp.maximum(values, -most), most).astype(held_as)


def setup_inputs(seed: int = 0) -> dict:
    seeds = jax.random.split(jax.random.key(seed), 15)
    tokens = gaussian(seeds[0], (TOKENS, D), 1.0, 6.0, ((0, 32),))
    query_weight = gaussian(seeds[1], (D, D), D ** -0.5, 0.21875, ((0, 8),))
    key_weight = gaussian(seeds[2], (D, D), D ** -0.5, 0.21875, ((0, 8),))
    value_weight = gaussian(seeds[3], (D, D), D ** -0.5, 0.21875, ((0, 8),))
    project_weight = gaussian(seeds[4], (D, D), (D // 16) ** -0.5, 0.875, ((0, 8),))
    router_weight = gaussian(seeds[5], (D, EXPERTS), D ** -0.5, 0.21875, ((0, 8),))
    prenorm_gain = jnp.clip(1.0 + 0.1 * jax.random.normal(seeds[6], (D,), jnp.float32), 0.5, 1.5).astype(jnp.bfloat16)
    midnorm_gain = jnp.clip(1.0 + 0.1 * jax.random.normal(seeds[7], (D,), jnp.float32), 0.5, 1.5).astype(jnp.bfloat16)
    bias_table = gaussian(seeds[8], (BUCKETS, HEADS), 1.0, 5.0, ((0, 8),))
    up_weight = gaussian(seeds[9], (EXPERTS, D, FF), D ** -0.5, 0.21875, ((0, 4), (2, 8)))
    down_weight = gaussian(seeds[10], (EXPERTS, FF, D), FF ** -0.5, 0.109375, ((0, 4), (1, 8)))
    routes_keys = jax.random.split(jax.random.fold_in(seeds[11], 1), TOKENS // SEQ)
    routes_turns = jax.random.permutation(jax.random.fold_in(seeds[11], 3), TOKENS // SEQ)
    routes = jax.vmap(lambda own, number: deal_out(jax.random.fold_in(seeds[11], 2), own, number, SEQ, EXPERTS, 2, CAP, 1))(routes_keys, routes_turns).reshape((TOKENS, 2))
    bucket_index = with_ends(jax.random.randint(seeds[12], (SEQ,), 0, BUCKETS), jax.random.fold_in(seeds[12], 1), 0, BUCKETS - 1).astype(jnp.int32)
    cotangent = gaussian(seeds[13], (TOKENS, D), 1.0, 6.0, ((0, 32),))
    return {"tokens": tokens, "query_weight": query_weight, "key_weight": key_weight, "value_weight": value_weight, "project_weight": project_weight, "router_weight": router_weight, "prenorm_gain": prenorm_gain, "midnorm_gain": midnorm_gain, "bias_table": bias_table, "up_weight": up_weight, "down_weight": down_weight, "routes": routes, "bucket_index": bucket_index, "cotangent": cotangent}


@jax.custom_vjp
def low(v):
    return lax.optimization_barrier(v.astype(jnp.bfloat16)).astype(jnp.float32)

@jax.custom_vjp
def low_back(v):
    return v

def low_keep(v):
    return (low(v), None)

def low_pass(kept, grad):
    return (grad,)

def back_keep(v):
    return (v, None)

def back_low(kept, grad):
    return (low(grad),)
low.defvjp(low_keep, low_pass)
low_back.defvjp(back_keep, back_low)
EPSILON = 1e-06
HIGH = lax.Precision.HIGHEST

def norm_rows(values, gain):
    return values * lax.rsqrt(lax.optimization_barrier(jnp.mean(values * values, axis=-1, keepdims=True)) + EPSILON) * gain

def product(left, right):
    return jnp.dot(left, right, precision=HIGH, preferred_element_type=jnp.float32)

def slot_places(route_seq, capacity, experts_all):
    count = route_seq.shape[0] * route_seq.shape[1]
    flat = route_seq.reshape(count).astype(jnp.int32)
    onehot = (flat[:, None] == jnp.arange(experts_all, dtype=jnp.int32)[None, :]).astype(jnp.int32)
    before = jnp.cumsum(onehot, axis=0) - onehot
    slot = lax.optimization_barrier(jnp.sum(before * onehot, axis=1))
    return flat * capacity + slot

def sequence_forward(params, inputs, route_seq, bucket):
    query_w, key_w, value_w, project_w, router_w, gain_one, gain_two, table, up_w, down_w = params
    seq_len = inputs.shape[0]

    def split_heads(values):
        return values.reshape(seq_len, HEADS, HEAD_DIM).transpose(1, 0, 2)
    normed = low(norm_rows(inputs, gain_one))
    query = split_heads(low(low_back(product(normed, query_w))))
    key = split_heads(low(low_back(product(normed, key_w))))
    value = split_heads(low(low_back(product(normed, value_w))))
    places = jnp.arange(seq_len, dtype=jnp.int32)
    offsets = jnp.clip(places[:, None] - places[None, :], 0, seq_len - 1)
    by_offset = table[bucket]
    bias = by_offset[offsets].transpose(2, 0, 1)
    scores = jnp.einsum('hqd,hkd->hqk', query, key, precision=HIGH) * HEAD_DIM ** (-0.5) + bias
    scores = low_back(scores)
    scores = jnp.where((places[:, None] >= places[None, :])[None], scores, -1e+30)
    total = jax.nn.logsumexp(scores, axis=-1, keepdims=True)
    probs = low(jnp.exp(scores - total))
    attended = jnp.einsum('hqk,hkd->hqd', probs, value, precision=HIGH)
    merged = low(low_back(attended.transpose(1, 0, 2).reshape(seq_len, D)))
    middle = inputs + low_back(product(merged, project_w))
    second = low(norm_rows(middle, gain_two))
    logits = low_back(product(second, router_w))
    choose = (route_seq[:, :, None] == jnp.arange(EXPERTS, dtype=jnp.int32)[None, None, :]).astype(jnp.float32)
    pair = jnp.einsum('ske,se->sk', choose, logits, precision=HIGH)
    gates = jax.nn.softmax(pair, axis=-1)
    dest = slot_places(route_seq, CAP, EXPERTS)
    filled = jnp.zeros((EXPERTS * CAP, D), jnp.float32).at[dest].set(jnp.repeat(second, 2, axis=0))
    filled = low_back(filled).reshape(EXPERTS, CAP, D)
    hidden = low_back(jnp.einsum('ecd,edf->ecf', filled, up_w, precision=HIGH))
    active = low(jax.nn.gelu(hidden, approximate=False))
    reply = low(low_back(jnp.einsum('ecf,efd->ecd', active, down_w, precision=HIGH)))
    picked = reply.reshape(EXPERTS * CAP, D)[dest].reshape(seq_len, 2, D)
    return middle + lax.optimization_barrier(jnp.sum(gates[:, :, None] * picked, axis=1))

def reference(tokens, query_weight, key_weight, value_weight, project_weight, router_weight, prenorm_gain, midnorm_gain, bias_table, up_weight, down_weight, routes, bucket_index, cotangent):
    params = tuple((w.astype(jnp.float32) for w in (query_weight, key_weight, value_weight, project_weight, router_weight, prenorm_gain, midnorm_gain, bias_table, up_weight, down_weight)))
    inputs = tokens.astype(jnp.float32)
    count = tokens.shape[0] // SEQ
    route_all = routes.astype(jnp.int32).reshape(count, SEQ, 2)
    bucket = bucket_index.astype(jnp.int32)

    def forward(weights, values):

        def one_seq(pieces):
            return sequence_forward(weights, pieces[0], pieces[1], bucket)
        result = lax.map(jax.checkpoint(one_seq), (values.reshape(count, SEQ, D), route_all))
        return result.reshape(count * SEQ, D)
    layer, pull = jax.vjp(forward, params, inputs)
    grads, input_grad = pull(cotangent.astype(jnp.float32))
    return (layer.astype(jnp.bfloat16), input_grad.astype(jnp.bfloat16), grads[0], grads[1], grads[2], grads[3], grads[4], grads[5], grads[6], grads[7], grads[8], grads[9])
```

```python
import functools

import jax
import jax.numpy as jnp
from jax import lax
from jax.experimental import pallas as pl
from jax.experimental.pallas import tpu as pltpu
from jax.sharding import PartitionSpec as P

HEADS = 12
HEAD_DIM = 64
EPSILON = 1e-06
NEGATIVE = -1e30
SCALE = HEAD_DIM ** (-0.5)
LANES = 128
TABLE_AT = 32
QBLOCK = 256
F32 = jnp.float32
BF16 = jnp.bfloat16
I32 = jnp.int32
VMEM_LIMIT = 60 * 1024 * 1024


def nn(left, right):
    return lax.dot_general(left, right, (((1,), (0,)), ((), ())), preferred_element_type=F32)


def nt(left, right):
    return lax.dot_general(left, right, (((1,), (1,)), ((), ())), preferred_element_type=F32)


def tn(left, right):
    return lax.dot_general(left, right, (((0,), (0,)), ((), ())), preferred_element_type=F32)


def iota(shape, axis):
    return lax.broadcasted_iota(I32, shape, axis)


def hot(mask):
    return jnp.where(mask, 1.0, 0.0).astype(BF16)


def vmem_call(body, name, out_shape, scratch=(), flops=0, moved=0, specs=None):
    def call(*args):
        in_specs = specs or [pl.BlockSpec(memory_space=pltpu.VMEM)] * len(args)
        return pl.pallas_call(
            body,
            name=name,
            out_shape=out_shape,
            in_specs=in_specs,
            out_specs=jax.tree.map(lambda _: pl.BlockSpec(memory_space=pltpu.VMEM), out_shape),
            scratch_shapes=scratch,
            compiler_params=pltpu.CompilerParams(vmem_limit_bytes=VMEM_LIMIT),
            cost_estimate=pl.CostEstimate(flops=flops, bytes_accessed=moved, transcendentals=0),
        )(*args)

    return call


def places(r, slot, here, local, cap):
    owner = lax.div(r, local)
    return (owner ^ here) * (local * cap) + lax.rem(r, local) * cap + slot.astype(I32)


def places_by_lane(routes_t, here, experts, local, cap):
    n = routes_t.shape[1]
    r0, r1 = routes_t[0:1, :], routes_t[1:2, :]
    tall = iota((-(-experts // 16) * 16, n), 0)
    oh0, oh1 = tall == r0, tall == r1
    earlier = hot(iota((n, n), 0) < iota((n, n), 1))
    count = nn(hot(oh0 | oh1), earlier)
    s0 = jnp.sum(jnp.where(oh0, count, 0.0), axis=0, keepdims=True)
    s1 = jnp.sum(jnp.where(oh1, count, 0.0), axis=0, keepdims=True)
    return places(r0, s0, here, local, cap), places(r1, s1, here, local, cap)


def places_by_row(routes, here, local, cap):
    n = routes.shape[0]
    r0, r1 = routes[:, 0:1], routes[:, 1:2]
    wide = iota((n, LANES), 1)
    oh0, oh1 = wide == r0, wide == r1
    earlier = hot(iota((n, n), 1) < iota((n, n), 0))
    count = nn(earlier, hot(oh0 | oh1))
    s0 = jnp.sum(jnp.where(oh0, count, 0.0), axis=1, keepdims=True)
    s1 = jnp.sum(jnp.where(oh1, count, 0.0), axis=1, keepdims=True)
    return places(r0, s0, here, local, cap), places(r1, s1, here, local, cap), oh0, oh1


def put_rows(values, d0, d1, start, count):
    at = iota((count, values.shape[0]), 0) + start
    return nn(hot((at == d0) | (at == d1)), values).astype(BF16)


def scatter_kernel(experts, local, cap, here_ref, routes_t_ref, values_ref, *out_refs):
    d0, d1 = places_by_lane(routes_t_ref[...], here_ref[0], experts, local, cap)
    values = values_ref[...]
    for at, out_ref in enumerate(out_refs):
        out_ref[...] = put_rows(values, d0, d1, at * cap, cap)


def table_rows(misc, buckets, shards):
    depth = misc.shape[0]
    per, rows = buckets // shards, depth // shards
    b = iota((buckets, depth), 0)
    select = hot(iota((buckets, depth), 1) == lax.div(b, per) * rows + lax.rem(b, per))
    return nn(select, misc)


def toeplitz(line, twice_ref):
    n = line.shape[1]
    rolled = pltpu.roll(jnp.broadcast_to(line, (LANES, n)), 0, 1, stride=1, stride_axis=0)
    twice_ref[:, :n] = rolled
    twice_ref[:, n:] = rolled


def bias_columns(twice_ref, n, block, rows):
    parts = []
    for jb in range(rows // LANES):
        start = (block * QBLOCK - jb * LANES) % n
        parts.append(twice_ref[:, start : start + QBLOCK])
    return jnp.concatenate(parts, axis=0)


def causal(scores, block):
    last = scores.shape[0] - QBLOCK
    keep = iota((QBLOCK, QBLOCK), 0) <= iota((QBLOCK, QBLOCK), 1)
    tail = jnp.where(keep, scores[last:], NEGATIVE)
    return tail if last == 0 else jnp.concatenate([scores[:last], tail], axis=0)


def forward_kernel(
    experts,
    local,
    cap,
    buckets,
    shards,
    here_ref,
    tok_ref,
    w_ref,
    routes_ref,
    routes_t_ref,
    bucket_ref,
    q_ref,
    k_ref,
    v_ref,
    normed_ref,
    merged_t_ref,
    middle_ref,
    second_ref,
    gates_ref,
    line_ref,
    *rest,
):
    groups = experts // local
    x_refs, slot_refs = rest[:experts], rest[experts : experts + groups]
    v_t_ref, out_t_ref, twice_ref = rest[experts + groups :]
    n, width = tok_ref.shape
    misc = w_ref[:, 4 * width :]
    misc_t = jnp.transpose(misc.astype(F32))
    gain_one, gain_two = misc_t[experts : experts + 1], misc_t[experts + 1 : experts + 2]
    x = tok_ref[...].astype(F32)
    normed = x * lax.rsqrt(jnp.mean(x * x, axis=-1, keepdims=True) + EPSILON) * gain_one
    normed_ref[...] = normed.astype(BF16)
    normed = normed_ref[...]
    q_ref[...] = (nn(normed, w_ref[:, :width]).astype(BF16).astype(F32) * SCALE).astype(BF16)
    k_ref[...] = nn(normed, w_ref[:, width : 2 * width]).astype(BF16)
    value = nn(normed, w_ref[:, 2 * width : 3 * width]).astype(BF16)
    v_ref[...] = value
    v_t_ref[...] = jnp.transpose(value)
    table = table_rows(misc, buckets, shards).astype(BF16)
    by_bucket = hot(iota((buckets, n), 0) == bucket_ref[...])
    line_ref[...] = tn(table, by_bucket)[TABLE_AT : TABLE_AT + 16]
    half = iota((1, LANES), 1) < HEAD_DIM

    def pair(hp, carry):
        lanes = pl.ds(pl.multiple_of(hp * LANES, LANES), LANES)
        kp, qp = k_ref[:, lanes], q_ref[:, lanes]
        for side in range(2):
            toeplitz(line_ref[pl.ds(hp * 2 + side, 1), :], twice_ref)
            keys = kp * hot(half if side == 0 else ~half)
            at = pl.ds(pl.multiple_of(hp * LANES + side * HEAD_DIM, HEAD_DIM), HEAD_DIM)
            for block in range(n // QBLOCK):
                rows = (block + 1) * QBLOCK
                cols = slice(block * QBLOCK, rows)
                scores = nt(keys[:rows], qp[cols]) + bias_columns(twice_ref, n, block, rows)
                scores = causal(scores, block)
                top = jnp.max(scores, axis=0, keepdims=True)
                e = jnp.exp(scores - top)
                probs = (e * (1.0 / jnp.sum(e, axis=0, keepdims=True))).astype(BF16)
                out_t_ref[at, cols] = nn(v_t_ref[at, :rows], probs).astype(BF16)
        return carry

    lax.fori_loop(0, HEADS // 2, pair, 0)
    merged_t_ref[...] = out_t_ref[...]
    middle = x + tn(merged_t_ref[...], w_ref[:, 3 * width : 4 * width])
    middle_ref[...] = middle
    second = middle * lax.rsqrt(jnp.mean(middle * middle, axis=-1, keepdims=True) + EPSILON)
    second_ref[...] = (second * gain_two).astype(BF16)
    second = second_ref[...]
    here = here_ref[0]
    c0, c1, oh0, oh1 = places_by_row(routes_ref[...], here, local, cap)
    logits = nn(second, misc)
    p0 = jnp.sum(jnp.where(oh0, logits, 0.0), axis=1, keepdims=True)
    p1 = jnp.sum(jnp.where(oh1, logits, 0.0), axis=1, keepdims=True)
    top = jnp.maximum(p0, p1)
    e0, e1 = jnp.exp(p0 - top), jnp.exp(p1 - top)
    g0, g1 = e0 / (e0 + e1), e1 / (e0 + e1)
    wide = iota((n, LANES), 1)
    gates_ref[...] = jnp.where(wide == 0, g0, jnp.where(wide == 1, g1, 0.0))
    d0, d1 = places_by_lane(routes_t_ref[...], here, experts, local, cap)
    for at, x_ref in enumerate(x_refs):
        x_ref[...] = put_rows(second, d0, d1, at * cap, cap)
    for at, slot_ref in enumerate(slot_refs):
        slot_ref[...] = jnp.zeros_like(slot_ref)
        for l in range(local):
            lane = iota((n, slot_ref.shape[1]), 1) + (at * local + l) * cap
            held = jnp.where(lane == c0, g0, jnp.where(lane == c1, g1, 0.0))
            slot_ref[l : l + 1, :] = jnp.sum(held, axis=0, keepdims=True)


def gelu_both(v):
    t = pl.reciprocal(1.0 + (0.3275911 * 0.7071067811865476) * jnp.abs(v))
    e = jnp.exp(-0.5 * (v * v))
    poly = 0.5 * 1.061405429
    for coefficient in (-1.453152027, 1.421413741, -0.284496736, 0.254829592):
        poly = poly * t + 0.5 * coefficient
    tail = poly * t * e
    phi = jnp.where(v < 0.0, tail, 1.0 - tail)
    return v * phi, phi + v * e * 0.3989422804014327


def expert_kernel(local_at, groups, cap, *refs):
    take = iter(refs)
    row_refs = [next(take) for _ in range(groups)]
    cot_refs = [next(take) for _ in range(groups)]
    slot_refs = [next(take) for _ in range(groups)]
    up_a, up_b, down_a, down_b = (next(take) for _ in range(4))
    reply_refs = [next(take) for _ in range(groups)]
    back_refs = [next(take) for _ in range(groups)]
    dot_refs = [next(take) for _ in range(groups)]
    ug_a, ug_b, dg_a, dg_b = (next(take) for _ in range(4))
    x_ref, xt_ref, cot_ref, gr_ref, reply_ref, back_ref = (next(take) for _ in range(6))
    up_buf, down_buf, ug_buf, dg_buf, act_ref, gh_ref = (next(take) for _ in range(6))
    in_sem, out_sem = next(take), next(take)
    rows, width = x_ref.shape
    slab = up_a.shape[2]
    block = up_buf.shape[2]
    per = block // slab
    half = up_a.shape[0] // per
    steps = 2 * half

    def fetches(up, down, at, slot):
        for i in range(per):
            cut = slice(i * slab, (i + 1) * slab)
            yield pltpu.make_async_copy(
                up.at[at * per + i], up_buf.at[slot, :, cut], in_sem.at[slot, i]
            )
            yield pltpu.make_async_copy(
                down.at[at + i * half], down_buf.at[slot, cut, :], in_sem.at[slot, per + i]
            )

    def stores(up, down, at, slot):
        for i in range(per):
            cut = slice(i * slab, (i + 1) * slab)
            yield pltpu.make_async_copy(
                ug_buf.at[slot, :, cut], up.at[at * per + i], out_sem.at[slot, i]
            )
            yield pltpu.make_async_copy(
                dg_buf.at[slot, cut, :], down.at[at + i * half], out_sem.at[slot, per + i]
            )

    def begin(kind, first, second, step, slot):
        @pl.when(step < half)
        def _():
            for copy in kind(*first, step, slot):
                copy.start()

        @pl.when(step >= half)
        def _():
            for copy in kind(*second, step - half, slot):
                copy.start()

    begin(fetches, (up_a, down_a), (up_b, down_b), 0, 0)
    for m in range(groups):
        cut = slice(m * cap, (m + 1) * cap)
        x_ref[cut, :] = row_refs[m][...]
        slots = jnp.broadcast_to(
            slot_refs[m][local_at : local_at + 1, :], (LANES, slot_refs[m].shape[1])
        )
        gate = jnp.transpose(slots)[:cap, 0:1]
        cot = cot_refs[m][...]
        cot_ref[cut, :] = cot
        gr_ref[cut, :] = (gate * cot.astype(F32)).astype(BF16)
    xt_ref[...] = jnp.transpose(x_ref[...])
    reply_ref[...] = jnp.zeros_like(reply_ref)
    back_ref[...] = jnp.zeros_like(back_ref)

    def step(at, carry):
        slot = lax.rem(at, 2)

        @pl.when(at + 1 < steps)
        def _():
            begin(fetches, (up_a, down_a), (up_b, down_b), at + 1, 1 - slot)

        for copy in fetches(up_a, down_a, 0, slot):
            copy.wait()

        @pl.when(at >= 2)
        def _():
            for copy in stores(ug_a, dg_a, 0, slot):
                copy.wait()

        chunk = 256
        for c in range(rows // chunk):
            cut = slice(c * chunk, (c + 1) * chunk)
            act, slope = gelu_both(nn(x_ref[cut, :], up_buf[slot]))
            act_ref[cut, :] = act.astype(BF16)
            grad = nt(gr_ref[cut, :], down_buf[slot])
            gh_ref[cut, :] = (grad * slope).astype(BF16)
            reply_ref[cut, :] += nn(act_ref[cut, :], down_buf[slot])
            back_ref[cut, :] += nt(gh_ref[cut, :], up_buf[slot])
        dg_buf[slot] = tn(act_ref[...], gr_ref[...]).astype(BF16)
        ug_buf[slot] = nn(xt_ref[...], gh_ref[...]).astype(BF16)
        begin(stores, (ug_a, dg_a), (ug_b, dg_b), at, slot)
        return carry

    lax.fori_loop(0, steps, step, 0)
    reply = reply_ref[...].astype(BF16)
    dots = jnp.sum(reply.astype(F32) * cot_ref[...].astype(F32), axis=1, keepdims=True)
    dots = jnp.transpose(jnp.broadcast_to(dots, (rows, LANES)))[0:8]
    for m in range(groups):
        cut = slice(m * cap, (m + 1) * cap)
        reply_refs[m][...] = reply[cut]
        back_refs[m][...] = back_ref[cut, :].astype(BF16)
        shifted = dots if m == 0 else pltpu.roll(dots, rows - m * cap, 1)
        dot_refs[m][...] = shifted[:, : dot_refs[m].shape[1]]
    for slot in range(2):
        for copy in stores(ug_a, dg_a, 0, slot):
            copy.wait()


def backward_kernel(
    experts,
    local,
    cap,
    buckets,
    shards,
    here_ref,
    tok_ref,
    w_ref,
    routes_ref,
    bucket_ref,
    cot_ref,
    q_ref,
    k_ref,
    v_ref,
    normed_ref,
    merged_t_ref,
    middle_ref,
    second_ref,
    gates_ref,
    line_ref,
    *rest,
):
    groups = experts // local
    take = iter(rest)
    back_refs = [next(take) for _ in range(experts)]
    dot_refs = [next(take) for _ in range(experts)]
    inputs_grad_ref, grads_ref = next(take), next(take)
    gm_ref, gmid_ref, k_t_ref, gq_t_ref, gk_ref, gv_ref, fold_ref, twice_ref = take
    n, width = tok_ref.shape
    misc = w_ref[:, 4 * width :]
    misc_t = jnp.transpose(misc.astype(F32))
    gain_one, gain_two = misc_t[experts : experts + 1], misc_t[experts + 1 : experts + 2]
    c0, c1, oh0, oh1 = places_by_row(routes_ref[...], here_ref[0], local, cap)
    grad_second = jnp.zeros((n, width), F32)
    gg0 = jnp.zeros((n, 1), F32)
    gg1 = jnp.zeros((n, 1), F32)
    for at in range(experts):
        lane = iota((n, cap), 1) + at * cap
        h0, h1 = lane == c0, lane == c1
        grad_second += nn(hot(h0 | h1), back_refs[at][...])
        dots = dot_refs[at][0:1, :cap]
        gg0 += jnp.sum(jnp.where(h0, dots, 0.0), axis=1, keepdims=True)
        gg1 += jnp.sum(jnp.where(h1, dots, 0.0), axis=1, keepdims=True)
    g0, g1 = gates_ref[:, 0:1], gates_ref[:, 1:2]
    inner = g0 * gg0 + g1 * gg1
    grad_logits = jnp.where(oh0, g0 * (gg0 - inner), jnp.where(oh1, g1 * (gg1 - inner), 0.0))
    grad_logits = grad_logits.astype(BF16)
    grad_second += nt(grad_logits, misc)
    router_grad = tn(second_ref[...], grad_logits)
    middle = middle_ref[...]
    r = lax.rsqrt(jnp.mean(middle * middle, axis=-1, keepdims=True) + EPSILON)
    mr = middle * r
    midnorm_grad = jnp.sum(grad_second * mr, axis=0, keepdims=True)
    u = gain_two * grad_second
    gmid = cot_ref[...].astype(F32) + r * (u - mr * jnp.mean(u * mr, axis=-1, keepdims=True))
    gmid_ref[...] = gmid
    branch = gmid.astype(BF16)
    grads_ref[:, 3 * width : 4 * width] = nn(merged_t_ref[...], branch).astype(BF16)
    gm_ref[...] = nt(branch, w_ref[:, 3 * width : 4 * width]).astype(BF16)
    k_t_ref[...] = jnp.transpose(k_ref[...])
    half = iota((1, LANES), 1) < HEAD_DIM

    def pair(hp, carry):
        lanes = pl.ds(pl.multiple_of(hp * LANES, LANES), LANES)
        kp, qp, vp, gp = k_ref[:, lanes], q_ref[:, lanes], v_ref[:, lanes], gm_ref[:, lanes]
        gk = [jnp.zeros((QBLOCK, LANES), F32) for _ in range(n // QBLOCK)]
        gv = [jnp.zeros((QBLOCK, LANES), F32) for _ in range(n // QBLOCK)]
        for side in range(2):
            toeplitz(line_ref[pl.ds(hp * 2 + side, 1), :], twice_ref)
            own = hot(half if side == 0 else ~half)
            keys, values, queries, outs = kp * own, vp * own, qp * own, gp * own
            at = pl.ds(pl.multiple_of(hp * LANES + side * HEAD_DIM, HEAD_DIM), HEAD_DIM)
            folded = jnp.zeros((LANES, n), F32)
            for block in range(n // QBLOCK):
                rows = (block + 1) * QBLOCK
                cols = slice(block * QBLOCK, rows)
                scores = nt(keys[:rows], qp[cols]) + bias_columns(twice_ref, n, block, rows)
                scores = causal(scores, block)
                top = jnp.max(scores, axis=0, keepdims=True)
                e = jnp.exp(scores - top)
                probs = e * (1.0 / jnp.sum(e, axis=0, keepdims=True))
                grad_probs = nt(values[:rows], gp[cols])
                total = jnp.sum(probs * grad_probs, axis=0, keepdims=True)
                gs = (probs * (grad_probs - total)).astype(BF16)
                low = probs.astype(BF16)
                gq_t_ref[at, cols] = (nn(k_t_ref[at, :rows], gs) * SCALE).astype(BF16)
                gk_part = nn(gs, queries[cols])
                gv_part = nn(low, outs[cols])
                for b in range(block + 1):
                    cut = slice(b * QBLOCK, (b + 1) * QBLOCK)
                    gk[b] += gk_part[cut]
                    gv[b] += gv_part[cut]
                wide = gs.astype(F32)
                for jb in range(rows // LANES):
                    piece = wide[jb * LANES : (jb + 1) * LANES]
                    parts = []
                    for lb in range(n // LANES):
                        src = (lb + jb) % (n // LANES) - block * (QBLOCK // LANES)
                        inside = 0 <= src < QBLOCK // LANES
                        parts.append(
                            piece[:, src * LANES : (src + 1) * LANES]
                            if inside
                            else jnp.zeros((LANES, LANES), F32)
                        )
                    folded += jnp.concatenate(parts, axis=1)
            size = LANES
            while size > 8:
                size //= 2
                folded = folded[:size] + pltpu.roll(folded[size : 2 * size], n - size, 1)
            fold_ref[hp * 2 + side] = folded
        for b in range(n // QBLOCK):
            cut = slice(b * QBLOCK, (b + 1) * QBLOCK)
            gk_ref[cut, lanes] = gk[b].astype(BF16)
            gv_ref[cut, lanes] = gv[b].astype(BF16)
        return carry

    lax.fori_loop(0, HEADS // 2, pair, 0)
    folded = fold_ref[...].reshape(HEADS * 8, n)
    row = iota((HEADS * 8, n), 0)
    for bit in (1, 2, 4):
        folded = jnp.where((row & bit) != 0, pltpu.roll(folded, n - bit, 1), folded)
    by_distance = jnp.sum(folded.reshape(HEADS, 8, n), axis=1)
    by_distance = jnp.concatenate([by_distance, jnp.zeros((16 - HEADS, n), F32)], axis=0)
    by_bucket = hot(iota((buckets, n), 0) == bucket_ref[...])
    table_grad = jnp.zeros((buckets, 16), F32)
    for _ in range(3):
        piece = by_distance.astype(BF16)
        table_grad += nt(by_bucket, piece)
        by_distance = by_distance - piece.astype(F32)
    spread = hot(iota((16, LANES), 1) == iota((16, LANES), 0) + TABLE_AT)
    table_grad = nn(table_grad.astype(BF16), spread).astype(BF16)
    rows, per = width // shards, buckets // shards
    b = iota((width, buckets), 1)
    select = hot(iota((width, buckets), 0) == lax.div(b, per) * rows + lax.rem(b, per))
    gq_t = gq_t_ref[...]
    gq = jnp.transpose(gq_t)
    gk, gv = gk_ref[...], gv_ref[...]
    normed_t = jnp.transpose(normed_ref[...])
    grads_ref[:, :width] = nt(normed_t, gq_t).astype(BF16)
    grads_ref[:, width : 2 * width] = nn(normed_t, gk).astype(BF16)
    grads_ref[:, 2 * width : 3 * width] = nn(normed_t, gv).astype(BF16)
    grad_normed = nt(gq, w_ref[:, :width])
    grad_normed += nt(gk, w_ref[:, width : 2 * width])
    grad_normed += nt(gv, w_ref[:, 2 * width : 3 * width])
    x = tok_ref[...].astype(F32)
    q = lax.rsqrt(jnp.mean(x * x, axis=-1, keepdims=True) + EPSILON)
    xq = x * q
    prenorm_grad = jnp.sum(grad_normed * xq, axis=0, keepdims=True)
    w = gain_one * grad_normed
    back = q * (w - xq * jnp.mean(w * xq, axis=-1, keepdims=True))
    inputs_grad_ref[...] = (gmid_ref[...] + back).astype(BF16)
    tall = iota((LANES, width), 0)
    gains = jnp.where(tall == experts, prenorm_grad, jnp.where(tall == experts + 1, midnorm_grad, 0.0))
    small = router_grad + jnp.transpose(gains) + nn(select, table_grad)
    grads_ref[:, 4 * width :] = small.astype(BF16)


def combine_kernel(local, cap, here_ref, routes_ref, gates_ref, middle_ref, *rest):
    *reply_refs, out_ref = rest
    n, width = middle_ref.shape
    c0, c1, _, _ = places_by_row(routes_ref[...], here_ref[0], local, cap)
    picked0 = jnp.zeros((n, width), F32)
    picked1 = jnp.zeros((n, width), F32)
    for at, reply_ref in enumerate(reply_refs):
        lane = iota((n, cap), 1) + at * cap
        picked0 += nn(hot(lane == c0), reply_ref[...])
        picked1 += nn(hot(lane == c1), reply_ref[...])
    out = middle_ref[...] + gates_ref[:, 0:1] * picked0 + gates_ref[:, 1:2] * picked1
    out_ref[...] = out.astype(BF16)


def swap(value, axis, bit):
    return lax.ppermute(value, axis, [(i, i ^ bit) for i in range(lax.axis_size(axis))])


def swap_all(values):
    return [v if m == 0 else swap(v, "expert", m) for m, v in enumerate(values)]


def gather_slabs(slab, bits):
    held = slab[None]
    for bit in bits[:-1]:
        held = jnp.concatenate([held, swap(held, "dp", bit)], axis=0)
    return held, swap(held, "dp", bits[-1])


def reduce_slabs(kept, sent, bits):
    def add(a, b):
        return a.astype(F32) + b.astype(F32)

    total = add(kept, swap(sent, "dp", bits[-1]))
    for bit in bits[-2::-1]:
        low = total.astype(BF16)
        half = low.shape[0] // 2
        total = add(low[:half], swap(low[half:], "dp", bit))
    return total[0]


def body(
    tokens,
    query_weight,
    key_weight,
    value_weight,
    project_weight,
    router_weight,
    prenorm_gain,
    midnorm_gain,
    bias_table,
    up_weight,
    down_weight,
    routes,
    bucket_index,
    cotangent,
):
    n, width = tokens.shape
    experts = router_weight.shape[1]
    shards, groups = lax.axis_size("dp"), lax.axis_size("expert")
    local, _, slab = up_weight.shape
    cap = 3 * n // experts
    buckets = bias_table.shape[0] * shards
    own_rows = query_weight.shape[0]
    hidden = slab * shards
    direct = slab % LANES == 0 and shards == 8
    here = lax.axis_index("expert").astype(I32).reshape(1)
    smem = pl.BlockSpec(memory_space=pltpu.SMEM)
    vmem = pl.BlockSpec(memory_space=pltpu.VMEM)
    hbm = pl.BlockSpec(memory_space=pl.ANY)
    routes_t = routes.T
    bucket_row = bucket_index[None, :]

    def shape(s, dtype=BF16):
        return jax.ShapeDtypeStruct(s, dtype)

    small = jnp.concatenate(
        [
            router_weight,
            prenorm_gain[:, None],
            midnorm_gain[:, None],
            jnp.zeros((own_rows, TABLE_AT - experts - 2), BF16),
            jnp.pad(bias_table, ((0, own_rows - bias_table.shape[0]), (0, 0))),
            jnp.zeros((own_rows, LANES - TABLE_AT - HEADS), BF16),
        ],
        axis=1,
    )
    packed = jnp.concatenate(
        [query_weight, key_weight, value_weight, project_weight, small], axis=1
    )
    full = lax.all_gather(packed, "dp", axis=0, tiled=True)

    cot_out = vmem_call(
        functools.partial(scatter_kernel, experts, local, cap),
        "send_cotangent",
        [shape((cap, width))] * experts,
        specs=[smem, vmem, vmem],
        flops=2 * n * experts * cap * width,
        moved=4 * experts * cap * width,
    )(here, routes_t, cotangent)
    cot_in = [swap_all(cot_out[l::local]) for l in range(local)]

    if direct:
        ups = [gather_slabs(up_weight[l], (2, 4, 1)) for l in range(local)]
        downs = [gather_slabs(down_weight[l], (4, 2, 1)) for l in range(local)]
    else:
        up_all = lax.all_gather(up_weight, "dp", axis=2, tiled=True)
        down_all = lax.all_gather(down_weight, "dp", axis=1, tiled=True)
        ups, downs = [], []
        for l in range(local):
            u = up_all[l].reshape(width, hidden // width, width).transpose(1, 0, 2)
            d = down_all[l].reshape(hidden // width, width, width)
            cut = hidden // width // 2
            ups.append((u[:cut], u[cut:]))
            downs.append((d[:cut], d[cut:]))

    forward = vmem_call(
        functools.partial(forward_kernel, experts, local, cap, buckets, shards),
        "attention_forward",
        [shape((n, width))] * 4
        + [
            shape((width, n)),
            shape((n, width), F32),
            shape((n, width)),
            shape((n, LANES), F32),
            shape((16, n), F32),
        ]
        + [shape((cap, width))] * experts
        + [shape((8, 256), F32)] * groups,
        scratch=[
            pltpu.VMEM((width, n), BF16),
            pltpu.VMEM((width, n), BF16),
            pltpu.VMEM((LANES, 2 * n), F32),
        ],
        specs=[smem] + [vmem] * 5,
        flops=20 * 10**9,
        moved=20 * 10**6,
    )(here, tokens, full, routes, routes_t, bucket_row)
    q, k, v, normed, merged_t, middle, second, gates, line = forward[:9]
    x_out, slots_out = forward[9 : 9 + experts], forward[9 + experts :]
    slots_in = swap_all(slots_out)
    x_in = [swap_all(x_out[l::local]) for l in range(local)]

    rows = groups * cap
    replies, backs, dots, up_grads, down_grads = [], [], [], [], []
    for l in range(local):
        up, down = ups[l], downs[l]
        count, slab_width = up[0].shape[0], up[0].shape[2]
        per = width // slab_width
        outs = pl.pallas_call(
            functools.partial(expert_kernel, l, groups, cap),
            name="expert",
            out_shape=[shape((cap, width))] * (2 * groups)
            + [shape((8, 256), F32)] * groups
            + [shape((count, width, slab_width))] * 2
            + [shape((count, slab_width, width))] * 2,
            in_specs=[vmem] * (3 * groups) + [hbm] * 4,
            out_specs=[vmem] * (3 * groups) + [hbm] * 4,
            scratch_shapes=[
                pltpu.VMEM((rows, width), BF16),
                pltpu.VMEM((width, rows), BF16),
                pltpu.VMEM((rows, width), BF16),
                pltpu.VMEM((rows, width), BF16),
                pltpu.VMEM((rows, width), F32),
                pltpu.VMEM((rows, width), F32),
                pltpu.VMEM((2, width, width), BF16),
                pltpu.VMEM((2, width, width), BF16),
                pltpu.VMEM((2, width, width), BF16),
                pltpu.VMEM((2, width, width), BF16),
                pltpu.VMEM((rows, width), BF16),
                pltpu.VMEM((rows, width), BF16),
                pltpu.SemaphoreType.DMA((2, 2 * per)),
                pltpu.SemaphoreType.DMA((2, 2 * per)),
            ],
            compiler_params=pltpu.CompilerParams(vmem_limit_bytes=VMEM_LIMIT),
            cost_estimate=pl.CostEstimate(
                flops=12 * rows * width * hidden, bytes_accessed=40 * 10**6, transcendentals=0
            ),
        )(*x_in[l], *cot_in[l], *slots_in, *up, *down)
        replies.append(outs[:groups])
        backs.append(swap_all(outs[groups : 2 * groups]))
        dots.append(swap_all(outs[2 * groups : 3 * groups]))
        ug, dg = outs[3 * groups : 3 * groups + 2], outs[3 * groups + 2 :]
        if direct:
            up_grads.append(reduce_slabs(*ug, (2, 4, 1)))
            down_grads.append(reduce_slabs(*dg, (4, 2, 1)))
        else:
            ug = jnp.concatenate(ug, axis=0).transpose(1, 0, 2).reshape(width, hidden)
            dg = jnp.concatenate(dg, axis=0).reshape(hidden, width)
            up_grads.append(lax.psum_scatter(ug, "dp", scatter_dimension=1, tiled=True).astype(F32))
            down_grads.append(
                lax.psum_scatter(dg, "dp", scatter_dimension=0, tiled=True).astype(F32)
            )

    flat = lambda parts: [parts[l][m] for m in range(groups) for l in range(local)]
    inputs_grad, grads = vmem_call(
        functools.partial(backward_kernel, experts, local, cap, buckets, shards),
        "attention_backward",
        [shape((n, width)), shape((width, packed.shape[1]))],
        scratch=[
            pltpu.VMEM((n, width), BF16),
            pltpu.VMEM((n, width), F32),
            pltpu.VMEM((width, n), BF16),
            pltpu.VMEM((width, n), BF16),
            pltpu.VMEM((n, width), BF16),
            pltpu.VMEM((n, width), BF16),
            pltpu.VMEM((HEADS, 8, n), F32),
            pltpu.VMEM((LANES, 2 * n), F32),
        ],
        specs=[smem] + [vmem] * (14 + 2 * experts),
        flops=40 * 10**9,
        moved=30 * 10**6,
    )(
        here,
        tokens,
        full,
        routes,
        bucket_row,
        cotangent,
        q,
        k,
        v,
        normed,
        merged_t,
        middle,
        second,
        gates,
        line,
        *flat(backs),
        *flat(dots),
    )
    shares = lax.psum_scatter(grads, "dp", scatter_dimension=0, tiled=True)
    totals = lax.psum(shares, "expert").astype(F32)

    replies = flat([swap_all(r) for r in replies])
    layer_out = vmem_call(
        functools.partial(combine_kernel, local, cap),
        "layer_out",
        shape((n, width)),
        specs=[smem] + [vmem] * (3 + experts),
        flops=4 * n * experts * cap * width,
        moved=6 * 10**6,
    )(here, routes, gates, middle, *replies)

    at = 4 * width
    return (
        layer_out,
        inputs_grad,
        totals[:, :width],
        totals[:, width : 2 * width],
        totals[:, 2 * width : 3 * width],
        totals[:, 3 * width : at],
        totals[:, at : at + experts],
        totals[:, at + experts],
        totals[:, at + experts + 1],
        totals[: bias_table.shape[0], at + TABLE_AT : at + TABLE_AT + HEADS],
        jnp.stack(up_grads),
        jnp.stack(down_grads),
    )


def solution(mesh):
    both, first = P(("dp", "expert"), None), P("dp", None)
    up, down = P("expert", None, "dp"), P("expert", "dp", None)
    return jax.shard_map(
        body,
        mesh=mesh,
        in_specs=(both,)
        + (first,) * 5
        + (P("dp"), P("dp"), first, up, down, both, P(), both),
        out_specs=(both, both) + (first,) * 5 + (P("dp"), P("dp"), first, up, down),
        check_vma=False,
    )
```

```python
import functools

import jax
import jax.numpy as jnp
from jax import lax
from jax.experimental import pallas as pl
from jax.experimental.pallas import tpu as pltpu
from jax.sharding import PartitionSpec as P

HEADS = 12
HEAD_DIM = 64
EPSILON = 1e-06
NEGATIVE = -1e30
SCALE = HEAD_DIM ** (-0.5)
LANES = 128
TABLE_AT = 32
QBLOCK = 256
F32 = jnp.float32
BF16 = jnp.bfloat16
I32 = jnp.int32
VMEM_LIMIT = 60 * 1024 * 1024
MESH = pl.DeviceIdType.MESH


def nn(left, right):
    return lax.dot_general(left, right, (((1,), (0,)), ((), ())), preferred_element_type=F32)


def nt(left, right):
    return lax.dot_general(left, right, (((1,), (1,)), ((), ())), preferred_element_type=F32)


def tn(left, right):
    return lax.dot_general(left, right, (((0,), (0,)), ((), ())), preferred_element_type=F32)


def iota(shape, axis):
    return lax.broadcasted_iota(I32, shape, axis)


def hot(mask):
    return jnp.where(mask, 1.0, 0.0).astype(BF16)


def vmem_call(body, name, out_shape, scratch=(), flops=0, moved=0, specs=None):
    def call(*args):
        in_specs = specs or [pl.BlockSpec(memory_space=pltpu.VMEM)] * len(args)
        return pl.pallas_call(
            body,
            name=name,
            out_shape=out_shape,
            in_specs=in_specs,
            out_specs=jax.tree.map(lambda _: pl.BlockSpec(memory_space=pltpu.VMEM), out_shape),
            scratch_shapes=scratch,
            compiler_params=pltpu.CompilerParams(vmem_limit_bytes=VMEM_LIMIT),
            cost_estimate=pl.CostEstimate(flops=flops, bytes_accessed=moved, transcendentals=0),
        )(*args)

    return call


def places(r, slot, here, local, cap):
    owner = lax.div(r, local)
    return (owner ^ here) * (local * cap) + lax.rem(r, local) * cap + slot.astype(I32)


def places_by_lane(routes_t, here, experts, local, cap):
    n = routes_t.shape[1]
    r0, r1 = routes_t[0:1, :], routes_t[1:2, :]
    tall = iota((-(-experts // 16) * 16, n), 0)
    oh0, oh1 = tall == r0, tall == r1
    earlier = hot(iota((n, n), 0) < iota((n, n), 1))
    count = nn(hot(oh0 | oh1), earlier)
    s0 = jnp.sum(jnp.where(oh0, count, 0.0), axis=0, keepdims=True)
    s1 = jnp.sum(jnp.where(oh1, count, 0.0), axis=0, keepdims=True)
    return places(r0, s0, here, local, cap), places(r1, s1, here, local, cap)


def places_by_row(routes, here, local, cap):
    n = routes.shape[0]
    r0, r1 = routes[:, 0:1], routes[:, 1:2]
    wide = iota((n, LANES), 1)
    oh0, oh1 = wide == r0, wide == r1
    earlier = hot(iota((n, n), 1) < iota((n, n), 0))
    count = nn(earlier, hot(oh0 | oh1))
    s0 = jnp.sum(jnp.where(oh0, count, 0.0), axis=1, keepdims=True)
    s1 = jnp.sum(jnp.where(oh1, count, 0.0), axis=1, keepdims=True)
    return places(r0, s0, here, local, cap), places(r1, s1, here, local, cap), oh0, oh1


def put_rows(values, d0, d1, start, count):
    at = iota((count, values.shape[0]), 0) + start
    return nn(hot((at == d0) | (at == d1)), values).astype(BF16)


def scatter_kernel(experts, local, cap, here_ref, routes_t_ref, values_ref, *out_refs):
    d0, d1 = places_by_lane(routes_t_ref[...], here_ref[0], experts, local, cap)
    values = values_ref[...]
    for at, out_ref in enumerate(out_refs):
        out_ref[...] = put_rows(values, d0, d1, at * cap, cap)


def table_rows(misc, buckets, shards):
    depth = misc.shape[0]
    per, rows = buckets // shards, depth // shards
    b = iota((buckets, depth), 0)
    select = hot(iota((buckets, depth), 1) == lax.div(b, per) * rows + lax.rem(b, per))
    return nn(select, misc)


def toeplitz(line, twice_ref):
    n = line.shape[1]
    rolled = pltpu.roll(jnp.broadcast_to(line, (LANES, n)), 0, 1, stride=1, stride_axis=0)
    twice_ref[:, :n] = rolled
    twice_ref[:, n:] = rolled


def bias_columns(twice_ref, n, block, rows):
    parts = []
    for jb in range(rows // LANES):
        start = (block * QBLOCK - jb * LANES) % n
        parts.append(twice_ref[:, start : start + QBLOCK])
    return jnp.concatenate(parts, axis=0)


def causal(scores, block):
    last = scores.shape[0] - QBLOCK
    keep = iota((QBLOCK, QBLOCK), 0) <= iota((QBLOCK, QBLOCK), 1)
    tail = jnp.where(keep, scores[last:], NEGATIVE)
    return tail if last == 0 else jnp.concatenate([scores[:last], tail], axis=0)


def project_inputs(experts, buckets, shards, tok_ref, w_ref, bucket_ref, q_ref, k_ref, v_ref, normed_ref, v_t_ref, line_ref):
    n, width = tok_ref.shape
    misc = w_ref[:, 3 * width : 3 * width + LANES]
    gain = jnp.transpose(misc.astype(F32))[experts : experts + 1]
    x = tok_ref[...].astype(F32)
    normed = x * lax.rsqrt(jnp.mean(x * x, axis=-1, keepdims=True) + EPSILON) * gain
    normed_ref[...] = normed.astype(BF16)
    normed = normed_ref[...]
    q_ref[...] = (nn(normed, w_ref[:, :width]).astype(BF16).astype(F32) * SCALE).astype(BF16)
    k_ref[...] = nn(normed, w_ref[:, width : 2 * width]).astype(BF16)
    value = nn(normed, w_ref[:, 2 * width : 3 * width]).astype(BF16)
    v_ref[...] = value
    v_t_ref[...] = jnp.transpose(value)
    table = table_rows(misc, buckets, shards).astype(BF16)
    by_bucket = hot(iota((buckets, n), 0) == bucket_ref[...])
    line_ref[...] = tn(table, by_bucket)[TABLE_AT : TABLE_AT + 16]


def attend(q_ref, k_ref, v_t_ref, line_ref, twice_ref, merged_t_ref):
    n = q_ref.shape[0]
    half = iota((1, LANES), 1) < HEAD_DIM

    def pair(hp, carry):
        lanes = pl.ds(pl.multiple_of(hp * LANES, LANES), LANES)
        kp, qp = k_ref[:, lanes], q_ref[:, lanes]
        for side in range(2):
            toeplitz(line_ref[pl.ds(hp * 2 + side, 1), :], twice_ref)
            keys = kp * hot(half if side == 0 else ~half)
            at = pl.ds(pl.multiple_of(hp * LANES + side * HEAD_DIM, HEAD_DIM), HEAD_DIM)
            for block in range(n // QBLOCK):
                rows = (block + 1) * QBLOCK
                cols = slice(block * QBLOCK, rows)
                scores = nt(keys[:rows], qp[cols]) + bias_columns(twice_ref, n, block, rows)
                scores = causal(scores, block)
                top = jnp.max(scores, axis=0, keepdims=True)
                e = jnp.exp(scores - top)
                probs = (e * (1.0 / jnp.sum(e, axis=0, keepdims=True))).astype(BF16)
                merged_t_ref[at, cols] = nn(v_t_ref[at, :rows], probs).astype(BF16)
        return carry

    lax.fori_loop(0, HEADS // 2, pair, 0)


def route(experts, local, cap, here, tok_ref, w_ref, routes_ref, merged_t_ref, middle_ref, second_ref, gates_ref, slot_refs):
    n, width = tok_ref.shape
    misc = w_ref[:, 3 * width : 3 * width + LANES]
    gain = jnp.transpose(misc.astype(F32))[experts + 1 : experts + 2]
    middle = tok_ref[...].astype(F32) + tn(merged_t_ref[...], w_ref[:, 3 * width + LANES :])
    middle_ref[...] = middle
    second = middle * lax.rsqrt(jnp.mean(middle * middle, axis=-1, keepdims=True) + EPSILON)
    second_ref[...] = (second * gain).astype(BF16)
    c0, c1, oh0, oh1 = places_by_row(routes_ref[...], here, local, cap)
    logits = nn(second_ref[...], misc)
    p0 = jnp.sum(jnp.where(oh0, logits, 0.0), axis=1, keepdims=True)
    p1 = jnp.sum(jnp.where(oh1, logits, 0.0), axis=1, keepdims=True)
    top = jnp.maximum(p0, p1)
    e0, e1 = jnp.exp(p0 - top), jnp.exp(p1 - top)
    g0, g1 = e0 / (e0 + e1), e1 / (e0 + e1)
    wide = iota((n, LANES), 1)
    gates_ref[...] = jnp.where(wide == 0, g0, jnp.where(wide == 1, g1, 0.0))
    for at, slot_ref in enumerate(slot_refs):
        slot_ref[...] = jnp.zeros(slot_ref.shape, F32)
        for l in range(local):
            lane = iota((n, slot_ref.shape[1]), 1) + (at * local + l) * cap
            held = jnp.where(lane == c0, g0, jnp.where(lane == c1, g1, 0.0))
            slot_ref[l : l + 1, :] = jnp.sum(held, axis=0, keepdims=True)


def forward_kernel(
    experts, local, cap, buckets, shards,
    here_ref, tok_ref, w_ref, routes_ref, routes_t_ref, bucket_ref,
    q_ref, k_ref, v_ref, normed_ref, merged_t_ref, middle_ref, second_ref, gates_ref, line_ref,
    *rest,
):
    groups = experts // local
    x_refs, slot_refs = rest[:experts], rest[experts : experts + groups]
    v_t_ref, twice_ref = rest[experts + groups :]
    here = here_ref[0]
    project_inputs(experts, buckets, shards, tok_ref, w_ref, bucket_ref, q_ref, k_ref, v_ref, normed_ref, v_t_ref, line_ref)
    attend(q_ref, k_ref, v_t_ref, line_ref, twice_ref, merged_t_ref)
    route(experts, local, cap, here, tok_ref, w_ref, routes_ref, merged_t_ref, middle_ref, second_ref, gates_ref, slot_refs)
    d0, d1 = places_by_lane(routes_t_ref[...], here, experts, local, cap)
    for at, x_ref in enumerate(x_refs):
        x_ref[...] = put_rows(second_ref[...], d0, d1, at * cap, cap)


def open_kernel(
    experts, local, cap, buckets, shards,
    tok_ref, wq_ref, wk_ref, wv_ref, wo_ref, small_ref, routes_ref, routes_t_ref, bucket_ref, cot_ref, up_ref, down_ref,
    q_ref, k_ref, v_ref, normed_ref, merged_t_ref, middle_ref, second_ref, gates_ref, line_ref,
    full_ref, up_a_ref, up_b_ref, down_a_ref, down_b_ref, x_in_ref, cot_in_ref, slots_in_ref,
    w_ref, cot_out_ref, x_out_ref, slots_out_ref, v_t_ref, twice_ref,
    w_send, w_recv, e_send, e_recv, z_send, z_recv, local_sem,
):
    groups = experts // local
    me, here = lax.axis_index("dp"), lax.axis_index("expert")
    n, width = tok_ref.shape
    rows = wq_ref.shape[0]
    across, along, core = me ^ 2, me ^ 4, me ^ 1
    diagonal = me ^ 6
    barrier = pltpu.get_barrier_semaphore()
    for peer in (across, along, core):
        pl.semaphore_signal(barrier, inc=1, device_id={"dp": peer}, device_id_type=MESH)
    for m in range(1, groups):
        pl.semaphore_signal(barrier, inc=1, device_id={"expert": here ^ m}, device_id_type=MESH)
    pl.semaphore_wait(barrier, 3 + groups - 1)

    def send(src, dst, sems, at, peer):
        copy = pltpu.make_async_remote_copy(
            src_ref=src, dst_ref=dst, send_sem=sems[0].at[at], recv_sem=sems[1].at[at],
            device_id=peer, device_id_type=MESH,
        )
        copy.start()
        return copy

    first = 3 * width + LANES
    parts = (slice(0, first), slice(first, first + width))
    mine = pl.ds(pl.multiple_of(me * rows, 16), rows)
    w_ref[mine, 0:width] = wq_ref[...]
    w_ref[mine, width : 2 * width] = wk_ref[...]
    w_ref[mine, 2 * width : 3 * width] = wv_ref[...]
    w_ref[mine, 3 * width : first] = small_ref[...]
    w_ref[mine, first:] = wo_ref[...]
    w_sems = (w_send, w_recv)

    def rows_of(owner, start=0, count=rows):
        return pl.ds(pl.multiple_of(owner * rows + start, 16), count)

    def w_copy(at, part, owner, peer, start=0, count=rows):
        view = w_ref.at[rows_of(owner, start, count), parts[part]]
        return send(view, view, w_sems, part * 8 + at, {"dp": peer})

    def w_wait(at, part, owner, start=0, count=rows):
        view = w_ref.at[rows_of(owner, start, count), parts[part]]
        pltpu.make_async_remote_copy(
            src_ref=view, dst_ref=view, send_sem=w_send.at[part * 8 + at], recv_sem=w_recv.at[part * 8 + at],
            device_id={"dp": core}, device_id_type=MESH,
        ).wait_recv()

    w_copies = []
    for part in range(2):
        for at, peer in ((0, across), (1, along), (2, core)):
            w_copies.append(w_copy(at, part, me, peer))

    d0, d1 = places_by_lane(routes_t_ref[...], here, experts, local, cap)
    z_sems = (z_send, z_recv)
    z_copies, own_copies = [], []

    def dispatch(values, out_ref, in_ref, base):
        for l in range(local):
            for m in [*range(1, groups), 0]:
                out_ref[l, m] = put_rows(values, d0, d1, (m * local + l) * cap, cap)
                if m:
                    z_copies.append(
                        send(out_ref.at[l, m], in_ref.at[l, m], z_sems, base + l * groups + m, {"expert": here ^ m})
                    )
                else:
                    copy = pltpu.make_async_copy(out_ref.at[l, 0], in_ref.at[l, 0], local_sem.at[base + l * groups])
                    copy.start()
                    own_copies.append(copy)

    dispatch(cot_ref[...], cot_out_ref, cot_in_ref, 0)
    half = rows // 2
    for part in range(2):
        w_wait(0, part, across)
        w_copies.append(w_copy(3, part, across, along, 0, half))
        w_copies.append(w_copy(4, part, across, core))
        w_wait(1, part, along)
        w_copies.append(w_copy(5, part, along, across, half, half))
        w_copies.append(w_copy(6, part, along, core))
        if part == 0:
            continue

    e_sems = (e_send, e_recv)
    e_copies = []
    tables = ((up_ref, up_a_ref, up_b_ref), (down_ref, down_a_ref, down_b_ref))

    def e_at(l, kind, step):
        return (l * 2 + kind) * 7 + step

    for l in range(local):
        for kind, (own_ref, a_ref, b_ref) in enumerate(tables):
            copy = pltpu.make_async_copy(own_ref.at[l], a_ref.at[l, 0], local_sem.at[2 * experts + l * 2 + kind])
            copy.start()
            own_copies.append(copy)
            e_copies.append(send(own_ref.at[l], a_ref.at[l, 1], e_sems, e_at(l, kind, 0), {"dp": across}))
            e_copies.append(send(own_ref.at[l], a_ref.at[l, 2], e_sems, e_at(l, kind, 1), {"dp": along}))
            e_copies.append(send(own_ref.at[l], b_ref.at[l, 0], e_sems, e_at(l, kind, 3), {"dp": core}))

    def w_finish(part):
        w_wait(3, part, diagonal, 0, half)
        w_wait(5, part, diagonal, half, half)
        w_copies.append(w_copy(7, part, diagonal, core))
        w_wait(2, part, core)
        w_wait(4, part, core ^ 2)
        w_wait(6, part, core ^ 4)
        w_wait(7, part, core ^ 6)

    w_finish(0)
    project_inputs(experts, buckets, shards, tok_ref, w_ref, bucket_ref, q_ref, k_ref, v_ref, normed_ref, v_t_ref, line_ref)
    attend(q_ref, k_ref, v_t_ref, line_ref, twice_ref, merged_t_ref)
    w_finish(1)
    copy = pltpu.make_async_copy(w_ref, full_ref, local_sem.at[2 * experts + 2 * local])
    copy.start()
    own_copies.append(copy)
    route(
        experts, local, cap, here, tok_ref, w_ref, routes_ref, merged_t_ref, middle_ref, second_ref, gates_ref,
        [slots_out_ref.at[m] for m in range(groups)],
    )
    base = 2 * experts
    for m in range(1, groups):
        z_copies.append(send(slots_out_ref.at[m], slots_in_ref.at[m], z_sems, base + m, {"expert": here ^ m}))
    copy = pltpu.make_async_copy(slots_out_ref.at[0], slots_in_ref.at[0], local_sem.at[2 * experts + 2 * local + 1])
    copy.start()
    own_copies.append(copy)
    dispatch(second_ref[...], x_out_ref, x_in_ref, experts)

    def e_wait(l, kind, step, slab_ref):
        at = e_at(l, kind, step)
        pltpu.make_async_remote_copy(
            src_ref=slab_ref, dst_ref=slab_ref, send_sem=e_send.at[at], recv_sem=e_recv.at[at],
            device_id={"dp": core}, device_id_type=MESH,
        ).wait_recv()

    for l in range(local):
        for kind, (own_ref, a_ref, b_ref) in enumerate(tables):
            step = kind
            e_wait(l, kind, step, a_ref.at[l, 1 + step])
            e_copies.append(
                send(a_ref.at[l, 1 + step], a_ref.at[l, 3], e_sems, e_at(l, kind, 2), {"dp": along if kind == 0 else across})
            )
            e_copies.append(send(a_ref.at[l, 1 + step], b_ref.at[l, 1 + step], e_sems, e_at(l, kind, 4 + step), {"dp": core}))
    for l in range(local):
        for kind, (own_ref, a_ref, b_ref) in enumerate(tables):
            step = 1 - kind
            e_wait(l, kind, step, a_ref.at[l, 1 + step])
            e_copies.append(send(a_ref.at[l, 1 + step], b_ref.at[l, 1 + step], e_sems, e_at(l, kind, 4 + step), {"dp": core}))
    for l in range(local):
        for kind, (own_ref, a_ref, b_ref) in enumerate(tables):
            e_wait(l, kind, 2, a_ref.at[l, 3])
            e_copies.append(send(a_ref.at[l, 3], b_ref.at[l, 3], e_sems, e_at(l, kind, 6), {"dp": core}))
    for l in range(local):
        for kind, (own_ref, a_ref, b_ref) in enumerate(tables):
            for i in range(4):
                e_wait(l, kind, 3 + i, b_ref.at[l, i])
    for copy in z_copies:
        copy.wait()
    for copy in e_copies + w_copies:
        copy.wait_send()
    for copy in own_copies:
        copy.wait()


def gelu_both(v):
    t = pl.reciprocal(1.0 + (0.3275911 * 0.7071067811865476) * jnp.abs(v))
    e = jnp.exp(-0.5 * (v * v))
    poly = 0.5 * 1.061405429
    for coefficient in (-1.453152027, 1.421413741, -0.284496736, 0.254829592):
        poly = poly * t + 0.5 * coefficient
    tail = poly * t * e
    phi = jnp.where(v < 0.0, tail, 1.0 - tail)
    return v * phi, phi + v * e * 0.3989422804014327


def expert_kernel(local_at, groups, cap, *refs):
    take = iter(refs)
    rows_in, cots_in, slots_in, up_a, up_b, down_a, down_b = (next(take) for _ in range(7))
    reply_refs = [next(take) for _ in range(groups)]
    back_refs = [next(take) for _ in range(groups)]
    dot_refs = [next(take) for _ in range(groups)]
    ug_a, ug_b, dg_a, dg_b = (next(take) for _ in range(4))
    x_ref, xt_ref, cot_ref, gr_ref, reply_ref, back_ref = (next(take) for _ in range(6))
    up_buf, down_buf, ug_buf, dg_buf, act_ref, gh_ref = (next(take) for _ in range(6))
    in_sem, out_sem, row_sem = take
    rows, width = x_ref.shape
    slab = up_a.shape[3]
    block = up_buf.shape[2]
    per = block // slab
    half = up_a.shape[1] // per
    steps = 2 * half

    def fetches(up, down, at, slot):
        for i in range(per):
            cut = slice(i * slab, (i + 1) * slab)
            yield pltpu.make_async_copy(
                up.at[local_at, at * per + i], up_buf.at[slot, :, cut], in_sem.at[slot, i]
            )
            yield pltpu.make_async_copy(
                down.at[local_at, at * per + i], down_buf.at[slot, cut, :], in_sem.at[slot, per + i]
            )

    def stores(up, down, at, slot):
        for i in range(per):
            cut = slice(i * slab, (i + 1) * slab)
            yield pltpu.make_async_copy(
                ug_buf.at[slot, :, cut], up.at[at * per + i], out_sem.at[slot, i]
            )
            yield pltpu.make_async_copy(
                dg_buf.at[slot, cut, :], down.at[at * per + i], out_sem.at[slot, per + i]
            )

    def begin(kind, first, second, step, slot):
        @pl.when(step < half)
        def _():
            for copy in kind(*first, step, slot):
                copy.start()

        @pl.when(step >= half)
        def _():
            for copy in kind(*second, step - half, slot):
                copy.start()

    begin(fetches, (up_a, down_a), (up_b, down_b), 0, 0)
    copies = []
    for m in range(groups):
        cut = slice(m * cap, (m + 1) * cap)
        copies.append(pltpu.make_async_copy(rows_in.at[local_at, m], x_ref.at[cut, :], row_sem.at[0, m]))
        copies.append(pltpu.make_async_copy(cots_in.at[local_at, m], cot_ref.at[cut, :], row_sem.at[1, m]))
    for copy in copies:
        copy.start()
    for copy in copies:
        copy.wait()
    for m in range(groups):
        cut = slice(m * cap, (m + 1) * cap)
        slots = slots_in[m, local_at : local_at + 1, :]
        gate = jnp.transpose(jnp.broadcast_to(slots, (LANES, slots.shape[1])))[:cap, 0:1]
        gr_ref[cut, :] = (gate * cot_ref[cut, :].astype(F32)).astype(BF16)
    xt_ref[...] = jnp.transpose(x_ref[...])
    reply_ref[...] = jnp.zeros_like(reply_ref)
    back_ref[...] = jnp.zeros_like(back_ref)

    def step(at, carry):
        slot = lax.rem(at, 2)

        @pl.when(at + 1 < steps)
        def _():
            begin(fetches, (up_a, down_a), (up_b, down_b), at + 1, 1 - slot)

        for copy in fetches(up_a, down_a, 0, slot):
            copy.wait()

        @pl.when(at >= 2)
        def _():
            for copy in stores(ug_a, dg_a, 0, slot):
                copy.wait()

        chunk = 256
        for c in range(rows // chunk):
            cut = slice(c * chunk, (c + 1) * chunk)
            act, slope = gelu_both(nn(x_ref[cut, :], up_buf[slot]))
            act_ref[cut, :] = act.astype(BF16)
            grad = nt(gr_ref[cut, :], down_buf[slot])
            gh_ref[cut, :] = (grad * slope).astype(BF16)
            reply_ref[cut, :] += nn(act_ref[cut, :], down_buf[slot])
            back_ref[cut, :] += nt(gh_ref[cut, :], up_buf[slot])
        dg_buf[slot] = tn(act_ref[...], gr_ref[...]).astype(BF16)
        ug_buf[slot] = nn(xt_ref[...], gh_ref[...]).astype(BF16)
        begin(stores, (ug_a, dg_a), (ug_b, dg_b), at, slot)
        return carry

    lax.fori_loop(0, steps, step, 0)
    reply = reply_ref[...].astype(BF16)
    dots = jnp.sum(reply.astype(F32) * cot_ref[...].astype(F32), axis=1, keepdims=True)
    dots = jnp.transpose(jnp.broadcast_to(dots, (rows, LANES)))[0:8]
    for m in range(groups):
        cut = slice(m * cap, (m + 1) * cap)
        reply_refs[m][...] = reply[cut]
        back_refs[m][...] = back_ref[cut, :].astype(BF16)
        shifted = dots if m == 0 else pltpu.roll(dots, rows - m * cap, 1)
        dot_refs[m][...] = shifted[:, : dot_refs[m].shape[1]]
    for slot in range(2):
        for copy in stores(ug_a, dg_a, 0, slot):
            copy.wait()


def backward_kernel(
    experts,
    local,
    cap,
    buckets,
    shards,
    here_ref,
    tok_ref,
    w_ref,
    routes_ref,
    bucket_ref,
    cot_ref,
    q_ref,
    k_ref,
    v_ref,
    normed_ref,
    merged_t_ref,
    middle_ref,
    second_ref,
    gates_ref,
    line_ref,
    *rest,
):
    groups = experts // local
    take = iter(rest)
    back_refs = [next(take) for _ in range(experts)]
    dot_refs = [next(take) for _ in range(experts)]
    inputs_grad_ref, grads_ref = next(take), next(take)
    gm_ref, gmid_ref, k_t_ref, gq_t_ref, gk_ref, gv_ref, fold_ref, twice_ref = take
    n, width = tok_ref.shape
    misc = w_ref[:, 3 * width : 3 * width + LANES]
    misc_t = jnp.transpose(misc.astype(F32))
    gain_one, gain_two = misc_t[experts : experts + 1], misc_t[experts + 1 : experts + 2]
    c0, c1, oh0, oh1 = places_by_row(routes_ref[...], here_ref[0], local, cap)
    grad_second = jnp.zeros((n, width), F32)
    gg0 = jnp.zeros((n, 1), F32)
    gg1 = jnp.zeros((n, 1), F32)
    for at in range(experts):
        lane = iota((n, cap), 1) + at * cap
        h0, h1 = lane == c0, lane == c1
        grad_second += nn(hot(h0 | h1), back_refs[at][...])
        dots = dot_refs[at][0:1, :cap]
        gg0 += jnp.sum(jnp.where(h0, dots, 0.0), axis=1, keepdims=True)
        gg1 += jnp.sum(jnp.where(h1, dots, 0.0), axis=1, keepdims=True)
    g0, g1 = gates_ref[:, 0:1], gates_ref[:, 1:2]
    inner = g0 * gg0 + g1 * gg1
    grad_logits = jnp.where(oh0, g0 * (gg0 - inner), jnp.where(oh1, g1 * (gg1 - inner), 0.0))
    grad_logits = grad_logits.astype(BF16)
    grad_second += nt(grad_logits, misc)
    router_grad = tn(second_ref[...], grad_logits)
    middle = middle_ref[...]
    r = lax.rsqrt(jnp.mean(middle * middle, axis=-1, keepdims=True) + EPSILON)
    mr = middle * r
    midnorm_grad = jnp.sum(grad_second * mr, axis=0, keepdims=True)
    u = gain_two * grad_second
    gmid = cot_ref[...].astype(F32) + r * (u - mr * jnp.mean(u * mr, axis=-1, keepdims=True))
    gmid_ref[...] = gmid
    branch = gmid.astype(BF16)
    grads_ref[:, 3 * width + LANES :] = nn(merged_t_ref[...], branch).astype(BF16)
    gm_ref[...] = nt(branch, w_ref[:, 3 * width + LANES :]).astype(BF16)
    k_t_ref[...] = jnp.transpose(k_ref[...])
    half = iota((1, LANES), 1) < HEAD_DIM

    def pair(hp, carry):
        lanes = pl.ds(pl.multiple_of(hp * LANES, LANES), LANES)
        kp, qp, vp, gp = k_ref[:, lanes], q_ref[:, lanes], v_ref[:, lanes], gm_ref[:, lanes]
        gk = [jnp.zeros((QBLOCK, LANES), F32) for _ in range(n // QBLOCK)]
        gv = [jnp.zeros((QBLOCK, LANES), F32) for _ in range(n // QBLOCK)]
        for side in range(2):
            toeplitz(line_ref[pl.ds(hp * 2 + side, 1), :], twice_ref)
            own = hot(half if side == 0 else ~half)
            keys, values, queries, outs = kp * own, vp * own, qp * own, gp * own
            at = pl.ds(pl.multiple_of(hp * LANES + side * HEAD_DIM, HEAD_DIM), HEAD_DIM)
            folded = jnp.zeros((LANES, n), F32)
            for block in range(n // QBLOCK):
                rows = (block + 1) * QBLOCK
                cols = slice(block * QBLOCK, rows)
                scores = nt(keys[:rows], qp[cols]) + bias_columns(twice_ref, n, block, rows)
                scores = causal(scores, block)
                top = jnp.max(scores, axis=0, keepdims=True)
                e = jnp.exp(scores - top)
                probs = e * (1.0 / jnp.sum(e, axis=0, keepdims=True))
                grad_probs = nt(values[:rows], gp[cols])
                total = jnp.sum(probs * grad_probs, axis=0, keepdims=True)
                gs = (probs * (grad_probs - total)).astype(BF16)
                low = probs.astype(BF16)
                gq_t_ref[at, cols] = (nn(k_t_ref[at, :rows], gs) * SCALE).astype(BF16)
                gk_part = nn(gs, queries[cols])
                gv_part = nn(low, outs[cols])
                for b in range(block + 1):
                    cut = slice(b * QBLOCK, (b + 1) * QBLOCK)
                    gk[b] += gk_part[cut]
                    gv[b] += gv_part[cut]
                wide = gs.astype(F32)
                for jb in range(rows // LANES):
                    piece = wide[jb * LANES : (jb + 1) * LANES]
                    parts = []
                    for lb in range(n // LANES):
                        src = (lb + jb) % (n // LANES) - block * (QBLOCK // LANES)
                        inside = 0 <= src < QBLOCK // LANES
                        parts.append(
                            piece[:, src * LANES : (src + 1) * LANES]
                            if inside
                            else jnp.zeros((LANES, LANES), F32)
                        )
                    folded += jnp.concatenate(parts, axis=1)
            size = LANES
            while size > 8:
                size //= 2
                folded = folded[:size] + pltpu.roll(folded[size : 2 * size], n - size, 1)
            fold_ref[hp * 2 + side] = folded
        for b in range(n // QBLOCK):
            cut = slice(b * QBLOCK, (b + 1) * QBLOCK)
            gk_ref[cut, lanes] = gk[b].astype(BF16)
            gv_ref[cut, lanes] = gv[b].astype(BF16)
        return carry

    lax.fori_loop(0, HEADS // 2, pair, 0)
    folded = fold_ref[...].reshape(HEADS * 8, n)
    row = iota((HEADS * 8, n), 0)
    for bit in (1, 2, 4):
        folded = jnp.where((row & bit) != 0, pltpu.roll(folded, n - bit, 1), folded)
    by_distance = jnp.sum(folded.reshape(HEADS, 8, n), axis=1)
    by_distance = jnp.concatenate([by_distance, jnp.zeros((16 - HEADS, n), F32)], axis=0)
    by_bucket = hot(iota((buckets, n), 0) == bucket_ref[...])
    table_grad = jnp.zeros((buckets, 16), F32)
    for _ in range(3):
        piece = by_distance.astype(BF16)
        table_grad += nt(by_bucket, piece)
        by_distance = by_distance - piece.astype(F32)
    spread = hot(iota((16, LANES), 1) == iota((16, LANES), 0) + TABLE_AT)
    table_grad = nn(table_grad.astype(BF16), spread).astype(BF16)
    rows, per = width // shards, buckets // shards
    b = iota((width, buckets), 1)
    select = hot(iota((width, buckets), 0) == lax.div(b, per) * rows + lax.rem(b, per))
    gq_t = gq_t_ref[...]
    gq = jnp.transpose(gq_t)
    gk, gv = gk_ref[...], gv_ref[...]
    normed_t = jnp.transpose(normed_ref[...])
    grads_ref[:, :width] = nt(normed_t, gq_t).astype(BF16)
    grads_ref[:, width : 2 * width] = nn(normed_t, gk).astype(BF16)
    grads_ref[:, 2 * width : 3 * width] = nn(normed_t, gv).astype(BF16)
    grad_normed = nt(gq, w_ref[:, :width])
    grad_normed += nt(gk, w_ref[:, width : 2 * width])
    grad_normed += nt(gv, w_ref[:, 2 * width : 3 * width])
    x = tok_ref[...].astype(F32)
    q = lax.rsqrt(jnp.mean(x * x, axis=-1, keepdims=True) + EPSILON)
    xq = x * q
    prenorm_grad = jnp.sum(grad_normed * xq, axis=0, keepdims=True)
    w = gain_one * grad_normed
    back = q * (w - xq * jnp.mean(w * xq, axis=-1, keepdims=True))
    inputs_grad_ref[...] = (gmid_ref[...] + back).astype(BF16)
    tall = iota((LANES, width), 0)
    gains = jnp.where(tall == experts, prenorm_grad, jnp.where(tall == experts + 1, midnorm_grad, 0.0))
    small = router_grad + jnp.transpose(gains) + nn(select, table_grad)
    grads_ref[:, 3 * width : 3 * width + LANES] = small.astype(BF16)


def combine_kernel(local, cap, here_ref, routes_ref, gates_ref, middle_ref, *rest):
    *reply_refs, out_ref = rest
    n, width = middle_ref.shape
    c0, c1, _, _ = places_by_row(routes_ref[...], here_ref[0], local, cap)
    picked0 = jnp.zeros((n, width), F32)
    picked1 = jnp.zeros((n, width), F32)
    for at, reply_ref in enumerate(reply_refs):
        lane = iota((n, cap), 1) + at * cap
        picked0 += nn(hot(lane == c0), reply_ref[...])
        picked1 += nn(hot(lane == c1), reply_ref[...])
    out = middle_ref[...] + gates_ref[:, 0:1] * picked0 + gates_ref[:, 1:2] * picked1
    out_ref[...] = out.astype(BF16)


def swap(value, axis, bit):
    return lax.ppermute(value, axis, [(i, i ^ bit) for i in range(lax.axis_size(axis))])


def swap_all(values):
    return [v if m == 0 else swap(v, "expert", m) for m, v in enumerate(values)]


def reduce_slabs(kept, sent, bits):
    def add(a, b):
        return a.astype(F32) + b.astype(F32)

    total = add(kept, swap(sent, "dp", bits[-1]))
    for bit in bits[-2::-1]:
        low = total.astype(BF16)
        half = low.shape[0] // 2
        total = add(low[:half], swap(low[half:], "dp", bit))
    return total[0]


def body(
    tokens,
    query_weight,
    key_weight,
    value_weight,
    project_weight,
    router_weight,
    prenorm_gain,
    midnorm_gain,
    bias_table,
    up_weight,
    down_weight,
    routes,
    bucket_index,
    cotangent,
):
    n, width = tokens.shape
    experts = router_weight.shape[1]
    shards, groups = lax.axis_size("dp"), lax.axis_size("expert")
    local, _, slab = up_weight.shape
    cap = 3 * n // experts
    buckets = bias_table.shape[0] * shards
    own_rows = query_weight.shape[0]
    hidden = slab * shards
    direct = slab % LANES == 0 and shards == 8
    here = lax.axis_index("expert").astype(I32).reshape(1)
    smem = pl.BlockSpec(memory_space=pltpu.SMEM)
    vmem = pl.BlockSpec(memory_space=pltpu.VMEM)
    hbm = pl.BlockSpec(memory_space=pl.ANY)
    routes_t = routes.T
    bucket_row = bucket_index[None, :]

    def shape(s, dtype=BF16):
        return jax.ShapeDtypeStruct(s, dtype)

    small = jnp.concatenate(
        [
            router_weight,
            prenorm_gain[:, None],
            midnorm_gain[:, None],
            jnp.zeros((own_rows, TABLE_AT - experts - 2), BF16),
            jnp.pad(bias_table, ((0, own_rows - bias_table.shape[0]), (0, 0))),
            jnp.zeros((own_rows, LANES - TABLE_AT - HEADS), BF16),
        ],
        axis=1,
    )
    packed_width = 4 * width + LANES
    slots_shape = (groups, 8, 256)
    kept = [shape((n, width))] * 4 + [
        shape((width, n)),
        shape((n, width), F32),
        shape((n, width)),
        shape((n, LANES), F32),
        shape((16, n), F32),
    ]
    if direct:
        slabs_up, slabs_down = shape((local, 4, width, slab)), shape((local, 4, slab, width))
        moved_rows = shape((local, groups, cap, width))
        outs = pl.pallas_call(
            functools.partial(open_kernel, experts, local, cap, buckets, shards),
            name="open",
            out_shape=kept
            + [shape((width, packed_width)), slabs_up, slabs_up, slabs_down, slabs_down]
            + [moved_rows, moved_rows, shape(slots_shape, F32)],
            in_specs=[vmem] * 10 + [hbm] * 2,
            out_specs=[vmem] * 9 + [hbm] * 8,
            scratch_shapes=[
                pltpu.VMEM((width, packed_width), BF16),
                pltpu.VMEM((local, groups, cap, width), BF16),
                pltpu.VMEM((local, groups, cap, width), BF16),
                pltpu.VMEM(slots_shape, F32),
                pltpu.VMEM((width, n), BF16),
                pltpu.VMEM((LANES, 2 * n), F32),
                pltpu.SemaphoreType.DMA((16,)),
                pltpu.SemaphoreType.DMA((16,)),
                pltpu.SemaphoreType.DMA((14 * local,)),
                pltpu.SemaphoreType.DMA((14 * local,)),
                pltpu.SemaphoreType.DMA((2 * experts + groups,)),
                pltpu.SemaphoreType.DMA((2 * experts + groups,)),
                pltpu.SemaphoreType.DMA((2 * experts + 2 * local + 2,)),
            ],
            compiler_params=pltpu.CompilerParams(
                vmem_limit_bytes=VMEM_LIMIT, collective_id=0, has_side_effects=True
            ),
            cost_estimate=pl.CostEstimate(flops=20 * 10**9, bytes_accessed=300 * 10**6, transcendentals=0),
        )(
            tokens, query_weight, key_weight, value_weight, project_weight, small,
            routes, routes_t, bucket_row, cotangent, up_weight, down_weight,
        )
        q, k, v, normed, merged_t, middle, second, gates, line, full = outs[:10]
        weights, (x_in, cot_in, slots_in) = outs[10:14], outs[14:]
    else:
        packed = jnp.concatenate(
            [query_weight, key_weight, value_weight, small, project_weight], axis=1
        )
        full = lax.all_gather(packed, "dp", axis=0, tiled=True)
        cot_out = vmem_call(
            functools.partial(scatter_kernel, experts, local, cap),
            "send_cotangent",
            [shape((cap, width))] * experts,
            specs=[smem, vmem, vmem],
        )(here, routes_t, cotangent)
        up_all = lax.all_gather(up_weight, "dp", axis=2, tiled=True)
        down_all = lax.all_gather(down_weight, "dp", axis=1, tiled=True)
        up_all = up_all.reshape(local, width, hidden // width, width).transpose(0, 2, 1, 3)
        down_all = down_all.reshape(local, hidden // width, width, width)
        cut = hidden // width // 2
        weights = (up_all[:, :cut], up_all[:, cut:], down_all[:, :cut], down_all[:, cut:])
        forward = vmem_call(
            functools.partial(forward_kernel, experts, local, cap, buckets, shards),
            "attention_forward",
            kept + [shape((cap, width))] * experts + [shape((8, 256), F32)] * groups,
            scratch=[pltpu.VMEM((width, n), BF16), pltpu.VMEM((LANES, 2 * n), F32)],
            specs=[smem] + [vmem] * 5,
        )(here, tokens, full, routes, routes_t, bucket_row)
        q, k, v, normed, merged_t, middle, second, gates, line = forward[:9]
        x_out, slots_out = forward[9 : 9 + experts], forward[9 + experts :]
        slots_in = jnp.stack(swap_all(slots_out))
        x_in = jnp.stack([jnp.stack(swap_all(x_out[l::local])) for l in range(local)])
        cot_in = jnp.stack([jnp.stack(swap_all(cot_out[l::local])) for l in range(local)])

    rows = groups * cap
    replies, backs, dots, up_grads, down_grads = [], [], [], [], []
    for l in range(local):
        count, slab_width = weights[0].shape[1], weights[0].shape[3]
        per = width // slab_width
        outs = pl.pallas_call(
            functools.partial(expert_kernel, l, groups, cap),
            name="expert",
            out_shape=[shape((cap, width))] * (2 * groups)
            + [shape((8, 256), F32)] * groups
            + [shape((count, width, slab_width))] * 2
            + [shape((count, slab_width, width))] * 2,
            in_specs=[hbm, hbm, vmem] + [hbm] * 4,
            out_specs=[vmem] * (3 * groups) + [hbm] * 4,
            scratch_shapes=[
                pltpu.VMEM((rows, width), BF16),
                pltpu.VMEM((width, rows), BF16),
                pltpu.VMEM((rows, width), BF16),
                pltpu.VMEM((rows, width), BF16),
                pltpu.VMEM((rows, width), F32),
                pltpu.VMEM((rows, width), F32),
                pltpu.VMEM((2, width, width), BF16),
                pltpu.VMEM((2, width, width), BF16),
                pltpu.VMEM((2, width, width), BF16),
                pltpu.VMEM((2, width, width), BF16),
                pltpu.VMEM((rows, width), BF16),
                pltpu.VMEM((rows, width), BF16),
                pltpu.SemaphoreType.DMA((2, 2 * per)),
                pltpu.SemaphoreType.DMA((2, 2 * per)),
                pltpu.SemaphoreType.DMA((2, groups)),
            ],
            compiler_params=pltpu.CompilerParams(vmem_limit_bytes=VMEM_LIMIT),
            cost_estimate=pl.CostEstimate(
                flops=12 * rows * width * hidden, bytes_accessed=40 * 10**6, transcendentals=0
            ),
        )(x_in, cot_in, slots_in, *weights)
        replies.append(outs[:groups])
        backs.append(swap_all(outs[groups : 2 * groups]))
        dots.append(swap_all(outs[2 * groups : 3 * groups]))
        ug, dg = outs[3 * groups : 3 * groups + 2], outs[3 * groups + 2 :]
        if direct:
            up_grads.append(reduce_slabs(*ug, (2, 4, 1)))
            down_grads.append(reduce_slabs(*dg, (2, 4, 1)))
        else:
            ug = jnp.concatenate(ug, axis=0).transpose(1, 0, 2).reshape(width, hidden)
            dg = jnp.concatenate(dg, axis=0).reshape(hidden, width)
            up_grads.append(lax.psum_scatter(ug, "dp", scatter_dimension=1, tiled=True).astype(F32))
            down_grads.append(
                lax.psum_scatter(dg, "dp", scatter_dimension=0, tiled=True).astype(F32)
            )

    flat = lambda parts: [parts[l][m] for m in range(groups) for l in range(local)]
    inputs_grad, grads = vmem_call(
        functools.partial(backward_kernel, experts, local, cap, buckets, shards),
        "attention_backward",
        [shape((n, width)), shape((width, packed_width))],
        scratch=[
            pltpu.VMEM((n, width), BF16),
            pltpu.VMEM((n, width), F32),
            pltpu.VMEM((width, n), BF16),
            pltpu.VMEM((width, n), BF16),
            pltpu.VMEM((n, width), BF16),
            pltpu.VMEM((n, width), BF16),
            pltpu.VMEM((HEADS, 8, n), F32),
            pltpu.VMEM((LANES, 2 * n), F32),
        ],
        specs=[smem] + [vmem] * (14 + 2 * experts),
        flops=40 * 10**9,
        moved=30 * 10**6,
    )(
        here,
        tokens,
        full,
        routes,
        bucket_row,
        cotangent,
        q,
        k,
        v,
        normed,
        merged_t,
        middle,
        second,
        gates,
        line,
        *flat(backs),
        *flat(dots),
    )
    shares = lax.psum_scatter(grads, "dp", scatter_dimension=0, tiled=True)
    totals = lax.psum(shares, "expert").astype(F32)

    replies = flat([swap_all(r) for r in replies])
    layer_out = vmem_call(
        functools.partial(combine_kernel, local, cap),
        "layer_out",
        shape((n, width)),
        specs=[smem] + [vmem] * (3 + experts),
        flops=4 * n * experts * cap * width,
        moved=6 * 10**6,
    )(here, routes, gates, middle, *replies)

    at = 3 * width
    return (
        layer_out,
        inputs_grad,
        totals[:, :width],
        totals[:, width : 2 * width],
        totals[:, 2 * width : 3 * width],
        totals[:, at + LANES :],
        totals[:, at : at + experts],
        totals[:, at + experts],
        totals[:, at + experts + 1],
        totals[: bias_table.shape[0], at + TABLE_AT : at + TABLE_AT + HEADS],
        jnp.stack(up_grads),
        jnp.stack(down_grads),
    )


def solution(mesh):
    both, first = P(("dp", "expert"), None), P("dp", None)
    up, down = P("expert", None, "dp"), P("expert", "dp", None)
    return jax.shard_map(
        body,
        mesh=mesh,
        in_specs=(both,)
        + (first,) * 5
        + (P("dp"), P("dp"), first, up, down, both, P(), both),
        out_specs=(both, both) + (first,) * 5 + (P("dp"), P("dp"), first, up, down),
        check_vma=False,
    )
```

```python
import functools
from types import SimpleNamespace

import jax
import jax.numpy as jnp
from jax import lax
from jax.experimental import pallas as pl
from jax.experimental.pallas import tpu as pltpu
from jax.sharding import PartitionSpec as P

HEADS = 12
HEAD_DIM = 64
EPSILON = 1e-06
NEGATIVE = -1e30
SCALE = HEAD_DIM ** (-0.5)
LANES = 128
TABLE_AT = 32
QBLOCK = 256
F32 = jnp.float32
BF16 = jnp.bfloat16
I32 = jnp.int32
VMEM_LIMIT = 60 * 1024 * 1024
LAYER_VMEM = 63 * 1024 * 1024
MESH = pl.DeviceIdType.MESH
DP, EXPERT = "dp", "expert"
UP, DOWN, OWN, A, B = range(5)


def nn(left, right):
    return lax.dot_general(left, right, (((1,), (0,)), ((), ())), preferred_element_type=F32)


def nt(left, right):
    return lax.dot_general(left, right, (((1,), (1,)), ((), ())), preferred_element_type=F32)


def tn(left, right):
    return lax.dot_general(left, right, (((0,), (0,)), ((), ())), preferred_element_type=F32)


def iota(shape, axis):
    return lax.broadcasted_iota(I32, shape, axis)


def hot(mask):
    return jnp.where(mask, 1.0, 0.0).astype(BF16)


def vmem_call(body, name, out_shape, scratch=(), flops=0, moved=0, specs=None):
    def call(*args):
        in_specs = specs or [pl.BlockSpec(memory_space=pltpu.VMEM)] * len(args)
        return pl.pallas_call(
            body,
            name=name,
            out_shape=out_shape,
            in_specs=in_specs,
            out_specs=jax.tree.map(lambda _: pl.BlockSpec(memory_space=pltpu.VMEM), out_shape),
            scratch_shapes=scratch,
            compiler_params=pltpu.CompilerParams(vmem_limit_bytes=VMEM_LIMIT),
            cost_estimate=pl.CostEstimate(flops=flops, bytes_accessed=moved, transcendentals=0),
        )(*args)

    return call


def places(r, slot, here, local, cap):
    owner = lax.div(r, local)
    return (owner ^ here) * (local * cap) + lax.rem(r, local) * cap + slot.astype(I32)


def places_by_lane(routes_t, here, experts, local, cap):
    n = routes_t.shape[1]
    r0, r1 = routes_t[0:1, :], routes_t[1:2, :]
    tall = iota((-(-experts // 16) * 16, n), 0)
    oh0, oh1 = tall == r0, tall == r1
    earlier = hot(iota((n, n), 0) < iota((n, n), 1))
    count = nn(hot(oh0 | oh1), earlier)
    s0 = jnp.sum(jnp.where(oh0, count, 0.0), axis=0, keepdims=True)
    s1 = jnp.sum(jnp.where(oh1, count, 0.0), axis=0, keepdims=True)
    return places(r0, s0, here, local, cap), places(r1, s1, here, local, cap)


def places_by_row(routes, here, local, cap):
    n = routes.shape[0]
    r0, r1 = routes[:, 0:1], routes[:, 1:2]
    wide = iota((n, LANES), 1)
    oh0, oh1 = wide == r0, wide == r1
    earlier = hot(iota((n, n), 1) < iota((n, n), 0))
    count = nn(earlier, hot(oh0 | oh1))
    s0 = jnp.sum(jnp.where(oh0, count, 0.0), axis=1, keepdims=True)
    s1 = jnp.sum(jnp.where(oh1, count, 0.0), axis=1, keepdims=True)
    return places(r0, s0, here, local, cap), places(r1, s1, here, local, cap), oh0, oh1


def put_rows(values, d0, d1, start, count):
    at = iota((count, values.shape[0]), 0) + start
    return nn(hot((at == d0) | (at == d1)), values).astype(BF16)


def scatter_kernel(experts, local, cap, here_ref, routes_t_ref, values_ref, *out_refs):
    d0, d1 = places_by_lane(routes_t_ref[...], here_ref[0], experts, local, cap)
    values = values_ref[...]
    for at, out_ref in enumerate(out_refs):
        out_ref[...] = put_rows(values, d0, d1, at * cap, cap)


def table_rows(misc, buckets, shards):
    depth = misc.shape[0]
    per, rows = buckets // shards, depth // shards
    b = iota((buckets, depth), 0)
    select = hot(iota((buckets, depth), 1) == lax.div(b, per) * rows + lax.rem(b, per))
    return nn(select, misc)


def toeplitz(line, twice_ref):
    n = line.shape[1]
    rolled = pltpu.roll(jnp.broadcast_to(line, (LANES, n)), 0, 1, stride=1, stride_axis=0)
    twice_ref[:, :n] = rolled
    twice_ref[:, n:] = rolled


def bias_columns(twice_ref, n, block, rows):
    parts = []
    for jb in range(rows // LANES):
        start = (block * QBLOCK - jb * LANES) % n
        parts.append(twice_ref[:, start : start + QBLOCK])
    return jnp.concatenate(parts, axis=0)


def causal(scores, block):
    last = scores.shape[0] - QBLOCK
    keep = iota((QBLOCK, QBLOCK), 0) <= iota((QBLOCK, QBLOCK), 1)
    tail = jnp.where(keep, scores[last:], NEGATIVE)
    return tail if last == 0 else jnp.concatenate([scores[:last], tail], axis=0)


def chunked(count, size=256):
    return [slice(at, at + size) for at in range(0, count, size)]


def project_inputs(experts, buckets, shards, tok_ref, w_ref, bucket_ref, q_ref, k_ref, v_ref, normed_t_ref, v_t_ref, line_ref):
    n, width = tok_ref.shape
    misc = w_ref[:, 3 * width : 3 * width + LANES]
    gain = jnp.transpose(misc.astype(F32))[experts : experts + 1]
    for cut in chunked(n):
        x = tok_ref[cut, :].astype(F32)
        normed = x * lax.rsqrt(jnp.mean(x * x, axis=-1, keepdims=True) + EPSILON) * gain
        normed = normed.astype(BF16)
        normed_t_ref[:, cut] = jnp.transpose(normed)
        query = nn(normed, w_ref[:, :width]).astype(BF16)
        q_ref[cut, :] = (query.astype(F32) * SCALE).astype(BF16)
        k_ref[cut, :] = nn(normed, w_ref[:, width : 2 * width]).astype(BF16)
        value = nn(normed, w_ref[:, 2 * width : 3 * width]).astype(BF16)
        v_ref[cut, :] = value
        v_t_ref[:, cut] = jnp.transpose(value)
    table = table_rows(misc, buckets, shards).astype(BF16)
    by_bucket = hot(iota((buckets, n), 0) == bucket_ref[...])
    line_ref[...] = tn(table, by_bucket)[TABLE_AT : TABLE_AT + 16]


def attend(q_ref, k_ref, v_t_ref, line_ref, twice_ref, merged_t_ref):
    n = q_ref.shape[0]
    half = iota((1, LANES), 1) < HEAD_DIM

    def pair(hp, carry):
        lanes = pl.ds(pl.multiple_of(hp * LANES, LANES), LANES)
        kp, qp = k_ref[:, lanes], q_ref[:, lanes]
        for side in range(2):
            toeplitz(line_ref[pl.ds(hp * 2 + side, 1), :], twice_ref)
            keys = kp * hot(half if side == 0 else ~half)
            at = pl.ds(pl.multiple_of(hp * LANES + side * HEAD_DIM, HEAD_DIM), HEAD_DIM)
            for block in range(n // QBLOCK):
                rows = (block + 1) * QBLOCK
                cols = slice(block * QBLOCK, rows)
                scores = nt(keys[:rows], qp[cols]) + bias_columns(twice_ref, n, block, rows)
                scores = causal(scores, block)
                top = jnp.max(scores, axis=0, keepdims=True)
                e = jnp.exp(scores - top)
                probs = (e * (1.0 / jnp.sum(e, axis=0, keepdims=True))).astype(BF16)
                merged_t_ref[at, cols] = nn(v_t_ref[at, :rows], probs).astype(BF16)
        return carry

    lax.fori_loop(0, HEADS // 2, pair, 0)


def route(experts, local, cap, here, tok_ref, w_ref, routes_ref, merged_t_ref, middle_ref, second_ref, gates_ref, slot_refs):
    n, width = tok_ref.shape
    misc = w_ref[:, 3 * width : 3 * width + LANES]
    gain = jnp.transpose(misc.astype(F32))[experts + 1 : experts + 2]
    for cut in chunked(n):
        middle = tok_ref[cut, :].astype(F32) + tn(merged_t_ref[:, cut], w_ref[:, 3 * width + LANES :])
        middle_ref[cut, :] = middle
        second = middle * lax.rsqrt(jnp.mean(middle * middle, axis=-1, keepdims=True) + EPSILON)
        second_ref[cut, :] = (second * gain).astype(BF16)
    c0, c1, oh0, oh1 = places_by_row(routes_ref[...], here, local, cap)
    logits = nn(second_ref[...], misc)
    p0 = jnp.sum(jnp.where(oh0, logits, 0.0), axis=1, keepdims=True)
    p1 = jnp.sum(jnp.where(oh1, logits, 0.0), axis=1, keepdims=True)
    top = jnp.maximum(p0, p1)
    e0, e1 = jnp.exp(p0 - top), jnp.exp(p1 - top)
    g0, g1 = e0 / (e0 + e1), e1 / (e0 + e1)
    wide = iota((n, LANES), 1)
    gates_ref[...] = jnp.where(wide == 0, g0, jnp.where(wide == 1, g1, 0.0))
    for at, slot_ref in enumerate(slot_refs):
        slot_ref[...] = jnp.zeros(slot_ref.shape, F32)
        for l in range(local):
            lane = iota((n, slot_ref.shape[1]), 1) + (at * local + l) * cap
            held = jnp.where(lane == c0, g0, jnp.where(lane == c1, g1, 0.0))
            slot_ref[l : l + 1, :] = jnp.sum(held, axis=0, keepdims=True)


def forward_kernel(
    experts, local, cap, buckets, shards,
    here_ref, tok_ref, w_ref, routes_ref, routes_t_ref, bucket_ref,
    q_ref, k_ref, v_ref, normed_t_ref, merged_t_ref, middle_ref, second_ref, gates_ref, line_ref,
    *rest,
):
    groups = experts // local
    x_refs, slot_refs = rest[:experts], rest[experts : experts + groups]
    v_t_ref, twice_ref = rest[experts + groups :]
    here = here_ref[0]
    project_inputs(experts, buckets, shards, tok_ref, w_ref, bucket_ref, q_ref, k_ref, v_ref, normed_t_ref, v_t_ref, line_ref)
    attend(q_ref, k_ref, v_t_ref, line_ref, twice_ref, merged_t_ref)
    route(experts, local, cap, here, tok_ref, w_ref, routes_ref, merged_t_ref, middle_ref, second_ref, gates_ref, slot_refs)
    d0, d1 = places_by_lane(routes_t_ref[...], here, experts, local, cap)
    for at, x_ref in enumerate(x_refs):
        x_ref[...] = put_rows(second_ref[...], d0, d1, at * cap, cap)


def gelu_both(v):
    t = pl.reciprocal(1.0 + (0.3275911 * 0.7071067811865476) * jnp.abs(v))
    e = jnp.exp(-0.5 * (v * v))
    poly = 0.5 * 1.061405429
    for coefficient in (-1.453152027, 1.421413741, -0.284496736, 0.254829592):
        poly = poly * t + 0.5 * coefficient
    tail = poly * t * e
    phi = jnp.where(v < 0.0, tail, 1.0 - tail)
    return v * phi, phi + v * e * 0.3989422804014327


def expert_kernel(local_at, groups, cap, *refs):
    take = iter(refs)
    rows_in, cots_in, slots_in, up_a, up_b, down_a, down_b = (next(take) for _ in range(7))
    reply_refs = [next(take) for _ in range(groups)]
    back_refs = [next(take) for _ in range(groups)]
    dot_refs = [next(take) for _ in range(groups)]
    ug_a, ug_b, dg_a, dg_b = (next(take) for _ in range(4))
    x_ref, xt_ref, cot_ref, gr_ref, reply_ref, back_ref = (next(take) for _ in range(6))
    up_buf, down_buf, ug_buf, dg_buf, act_ref, gh_ref = (next(take) for _ in range(6))
    in_sem, out_sem, row_sem = take
    rows, width = x_ref.shape
    slab = up_a.shape[3]
    block = up_buf.shape[2]
    per = block // slab
    half = up_a.shape[1] // per
    steps = 2 * half

    def fetches(up, down, at, slot):
        for i in range(per):
            cut = slice(i * slab, (i + 1) * slab)
            yield pltpu.make_async_copy(
                up.at[local_at, at * per + i], up_buf.at[slot, :, cut], in_sem.at[slot, i]
            )
            yield pltpu.make_async_copy(
                down.at[local_at, at * per + i], down_buf.at[slot, cut, :], in_sem.at[slot, per + i]
            )

    def stores(up, down, at, slot):
        for i in range(per):
            cut = slice(i * slab, (i + 1) * slab)
            yield pltpu.make_async_copy(
                ug_buf.at[slot, :, cut], up.at[at * per + i], out_sem.at[slot, i]
            )
            yield pltpu.make_async_copy(
                dg_buf.at[slot, cut, :], down.at[at * per + i], out_sem.at[slot, per + i]
            )

    def begin(kind, first, second, step, slot):
        @pl.when(step < half)
        def _():
            for copy in kind(*first, step, slot):
                copy.start()

        @pl.when(step >= half)
        def _():
            for copy in kind(*second, step - half, slot):
                copy.start()

    begin(fetches, (up_a, down_a), (up_b, down_b), 0, 0)
    copies = []
    for m in range(groups):
        cut = slice(m * cap, (m + 1) * cap)
        copies.append(pltpu.make_async_copy(rows_in.at[local_at, m], x_ref.at[cut, :], row_sem.at[0, m]))
        copies.append(pltpu.make_async_copy(cots_in.at[local_at, m], cot_ref.at[cut, :], row_sem.at[1, m]))
    for copy in copies:
        copy.start()
    for copy in copies:
        copy.wait()
    for m in range(groups):
        cut = slice(m * cap, (m + 1) * cap)
        slots = slots_in[m, local_at : local_at + 1, :]
        gate = jnp.transpose(jnp.broadcast_to(slots, (LANES, slots.shape[1])))[:cap, 0:1]
        gr_ref[cut, :] = (gate * cot_ref[cut, :].astype(F32)).astype(BF16)
    xt_ref[...] = jnp.transpose(x_ref[...])
    reply_ref[...] = jnp.zeros_like(reply_ref)
    back_ref[...] = jnp.zeros_like(back_ref)

    def step(at, carry):
        slot = lax.rem(at, 2)

        @pl.when(at + 1 < steps)
        def _():
            begin(fetches, (up_a, down_a), (up_b, down_b), at + 1, 1 - slot)

        for copy in fetches(up_a, down_a, 0, slot):
            copy.wait()

        @pl.when(at >= 2)
        def _():
            for copy in stores(ug_a, dg_a, 0, slot):
                copy.wait()

        chunk = 256
        for c in range(rows // chunk):
            cut = slice(c * chunk, (c + 1) * chunk)
            act, slope = gelu_both(nn(x_ref[cut, :], up_buf[slot]))
            act_ref[cut, :] = act.astype(BF16)
            grad = nt(gr_ref[cut, :], down_buf[slot])
            gh_ref[cut, :] = (grad * slope).astype(BF16)
            reply_ref[cut, :] += nn(act_ref[cut, :], down_buf[slot])
            back_ref[cut, :] += nt(gh_ref[cut, :], up_buf[slot])
        dg_buf[slot] = tn(act_ref[...], gr_ref[...]).astype(BF16)
        ug_buf[slot] = nn(xt_ref[...], gh_ref[...]).astype(BF16)
        begin(stores, (ug_a, dg_a), (ug_b, dg_b), at, slot)
        return carry

    lax.fori_loop(0, steps, step, 0)
    reply = reply_ref[...].astype(BF16)
    dots = jnp.sum(reply.astype(F32) * cot_ref[...].astype(F32), axis=1, keepdims=True)
    dots = jnp.transpose(jnp.broadcast_to(dots, (rows, LANES)))[0:8]
    for m in range(groups):
        cut = slice(m * cap, (m + 1) * cap)
        reply_refs[m][...] = reply[cut]
        back_refs[m][...] = back_ref[cut, :].astype(BF16)
        shifted = dots if m == 0 else pltpu.roll(dots, rows - m * cap, 1)
        dot_refs[m][...] = shifted[:, : dot_refs[m].shape[1]]
    for slot in range(2):
        for copy in stores(ug_a, dg_a, 0, slot):
            copy.wait()


def attend_back(after, q_ref, k_ref, v_ref, gm_ref, k_t_ref, line_ref, twice_ref, gq_t_ref, gk_ref, gv_ref, fold_ref):
    n = q_ref.shape[0]
    half = iota((1, LANES), 1) < HEAD_DIM

    def pair(hp, carry):
        lanes = pl.ds(pl.multiple_of(hp * LANES, LANES), LANES)
        kp, qp, vp, gp = k_ref[:, lanes], q_ref[:, lanes], v_ref[:, lanes], gm_ref[:, lanes]
        gk = [jnp.zeros((QBLOCK, LANES), F32) for _ in range(n // QBLOCK)]
        gv = [jnp.zeros((QBLOCK, LANES), F32) for _ in range(n // QBLOCK)]
        for side in range(2):
            toeplitz(line_ref[pl.ds(hp * 2 + side, 1), :], twice_ref)
            own = hot(half if side == 0 else ~half)
            keys, values, queries, outs = kp * own, vp * own, qp * own, gp * own
            at = pl.ds(pl.multiple_of(hp * LANES + side * HEAD_DIM, HEAD_DIM), HEAD_DIM)
            folded = jnp.zeros((LANES, n), F32)
            for block in range(n // QBLOCK):
                rows = (block + 1) * QBLOCK
                cols = slice(block * QBLOCK, rows)
                scores = nt(keys[:rows], qp[cols]) + bias_columns(twice_ref, n, block, rows)
                scores = causal(scores, block)
                top = jnp.max(scores, axis=0, keepdims=True)
                e = jnp.exp(scores - top)
                probs = e * (1.0 / jnp.sum(e, axis=0, keepdims=True))
                grad_probs = nt(values[:rows], gp[cols])
                total = jnp.sum(probs * grad_probs, axis=0, keepdims=True)
                gs = (probs * (grad_probs - total)).astype(BF16)
                low = probs.astype(BF16)
                gq_t_ref[at, cols] = (nn(k_t_ref[at, :rows], gs) * SCALE).astype(BF16)
                gk_part = nn(gs, queries[cols])
                gv_part = nn(low, outs[cols])
                for b in range(block + 1):
                    cut = slice(b * QBLOCK, (b + 1) * QBLOCK)
                    gk[b] += gk_part[cut]
                    gv[b] += gv_part[cut]
                wide = gs.astype(F32)
                for jb in range(rows // LANES):
                    piece = wide[jb * LANES : (jb + 1) * LANES]
                    parts = []
                    for lb in range(n // LANES):
                        src = (lb + jb) % (n // LANES) - block * (QBLOCK // LANES)
                        inside = 0 <= src < QBLOCK // LANES
                        parts.append(
                            piece[:, src * LANES : (src + 1) * LANES]
                            if inside
                            else jnp.zeros((LANES, LANES), F32)
                        )
                    folded += jnp.concatenate(parts, axis=1)
            size = LANES
            while size > 8:
                size //= 2
                folded = folded[:size] + pltpu.roll(folded[size : 2 * size], n - size, 1)
            fold_ref[hp * 2 + side] = folded
        for b in range(n // QBLOCK):
            cut = slice(b * QBLOCK, (b + 1) * QBLOCK)
            gk_ref[cut, lanes] = gk[b].astype(BF16)
            gv_ref[cut, lanes] = gv[b].astype(BF16)
        after(hp)
        return carry

    lax.fori_loop(0, HEADS // 2, pair, 0)


def middle_back(
    experts, local, cap, here, w_ref, routes_ref, cot_ref, middle_ref, second_ref, gates_ref, back_refs, dot_refs, gmid_ref, branch_ref
):
    n, width = cot_ref.shape
    misc = w_ref[:, 3 * width : 3 * width + LANES]
    gain = jnp.transpose(misc.astype(F32))[experts + 1 : experts + 2]
    c0_all, c1_all, oh0_all, oh1_all = places_by_row(routes_ref[...], here, local, cap)
    router_grad = jnp.zeros((width, LANES), F32)
    midnorm_grad = jnp.zeros((1, width), F32)
    for cut in chunked(n):
        c0, c1, oh0, oh1 = c0_all[cut], c1_all[cut], oh0_all[cut], oh1_all[cut]
        count = c0.shape[0]
        grad_second = jnp.zeros((count, width), F32)
        gg0 = jnp.zeros((count, 1), F32)
        gg1 = jnp.zeros((count, 1), F32)
        for at in range(experts):
            lane = iota((count, cap), 1) + at * cap
            h0, h1 = lane == c0, lane == c1
            grad_second += nn(hot(h0 | h1), back_refs[at][...])
            dots = dot_refs[at][0:1, :cap]
            gg0 += jnp.sum(jnp.where(h0, dots, 0.0), axis=1, keepdims=True)
            gg1 += jnp.sum(jnp.where(h1, dots, 0.0), axis=1, keepdims=True)
        g0, g1 = gates_ref[cut, 0:1], gates_ref[cut, 1:2]
        inner = g0 * gg0 + g1 * gg1
        grad_logits = jnp.where(oh0, g0 * (gg0 - inner), jnp.where(oh1, g1 * (gg1 - inner), 0.0))
        grad_logits = grad_logits.astype(BF16)
        grad_second += nt(grad_logits, misc)
        router_grad += tn(second_ref[cut, :], grad_logits)
        middle = middle_ref[cut, :]
        r = lax.rsqrt(jnp.mean(middle * middle, axis=-1, keepdims=True) + EPSILON)
        mr = middle * r
        midnorm_grad += jnp.sum(grad_second * mr, axis=0, keepdims=True)
        u = gain * grad_second
        gmid = cot_ref[cut, :].astype(F32) + r * (u - mr * jnp.mean(u * mr, axis=-1, keepdims=True))
        gmid_ref[cut, :] = gmid
        branch_ref[cut, :] = gmid.astype(BF16)
    return router_grad, midnorm_grad


def table_back(buckets, shards, width, bucket_ref, fold_ref):
    n = bucket_ref.shape[1]
    folded = fold_ref[...].reshape(HEADS * 8, n)
    row = iota((HEADS * 8, n), 0)
    for bit in (1, 2, 4):
        folded = jnp.where((row & bit) != 0, pltpu.roll(folded, n - bit, 1), folded)
    by_distance = jnp.sum(folded.reshape(HEADS, 8, n), axis=1)
    by_distance = jnp.concatenate([by_distance, jnp.zeros((16 - HEADS, n), F32)], axis=0)
    by_bucket = hot(iota((buckets, n), 0) == bucket_ref[...])
    table_grad = jnp.zeros((buckets, 16), F32)
    for _ in range(3):
        piece = by_distance.astype(BF16)
        table_grad += nt(by_bucket, piece)
        by_distance = by_distance - piece.astype(F32)
    spread = hot(iota((16, LANES), 1) == iota((16, LANES), 0) + TABLE_AT)
    table_grad = nn(table_grad.astype(BF16), spread).astype(BF16)
    rows, per = width // shards, buckets // shards
    b = iota((width, buckets), 1)
    select = hot(iota((width, buckets), 0) == lax.div(b, per) * rows + lax.rem(b, per))
    return nn(select, table_grad)


def inputs_back(experts, tok_ref, w_ref, gq_t_ref, gk_ref, gv_ref, gmid_ref, inputs_grad_ref):
    n, width = tok_ref.shape
    misc = w_ref[:, 3 * width : 3 * width + LANES]
    gain = jnp.transpose(misc.astype(F32))[experts : experts + 1]
    prenorm_grad = jnp.zeros((1, width), F32)
    for cut in chunked(n):
        grad_normed = nt(jnp.transpose(gq_t_ref[:, cut]), w_ref[:, :width])
        grad_normed += nt(gk_ref[cut, :], w_ref[:, width : 2 * width])
        grad_normed += nt(gv_ref[cut, :], w_ref[:, 2 * width : 3 * width])
        x = tok_ref[cut, :].astype(F32)
        q = lax.rsqrt(jnp.mean(x * x, axis=-1, keepdims=True) + EPSILON)
        xq = x * q
        prenorm_grad += jnp.sum(grad_normed * xq, axis=0, keepdims=True)
        w = gain * grad_normed
        back = q * (w - xq * jnp.mean(w * xq, axis=-1, keepdims=True))
        inputs_grad_ref[cut, :] = (gmid_ref[cut, :] + back).astype(BF16)
    return prenorm_grad


def small_grads(experts, router_grad, prenorm_grad, midnorm_grad, table):
    width = prenorm_grad.shape[1]
    tall = iota((LANES, width), 0)
    gains = jnp.where(tall == experts, prenorm_grad, jnp.where(tall == experts + 1, midnorm_grad, 0.0))
    return (router_grad + jnp.transpose(gains) + table).astype(BF16)


def backward_kernel(
    experts, local, cap, buckets, shards,
    here_ref, tok_ref, w_ref, routes_ref, bucket_ref, cot_ref, q_ref, k_ref, v_ref, normed_t_ref, merged_t_ref,
    middle_ref, second_ref, gates_ref, line_ref,
    *rest,
):
    take = iter(rest)
    back_refs = [next(take) for _ in range(experts)]
    dot_refs = [next(take) for _ in range(experts)]
    inputs_grad_ref, grads_ref = next(take), next(take)
    gm_ref, gmid_ref, k_t_ref, gq_t_ref, gk_ref, gv_ref, fold_ref, twice_ref, branch_ref = take
    width = tok_ref.shape[1]
    router_grad, midnorm_grad = middle_back(
        experts, local, cap, here_ref[0], w_ref, routes_ref, cot_ref, middle_ref, second_ref, gates_ref,
        back_refs, dot_refs, gmid_ref, branch_ref,
    )
    grads_ref[:, 3 * width + LANES :] = nn(merged_t_ref[...], branch_ref[...]).astype(BF16)
    gm_ref[...] = nt(branch_ref[...], w_ref[:, 3 * width + LANES :]).astype(BF16)
    k_t_ref[...] = jnp.transpose(k_ref[...])
    attend_back(
        lambda hp: None, q_ref, k_ref, v_ref, gm_ref, k_t_ref, line_ref, twice_ref, gq_t_ref, gk_ref, gv_ref, fold_ref
    )
    normed_t = normed_t_ref[...]
    grads_ref[:, :width] = nt(normed_t, gq_t_ref[...]).astype(BF16)
    grads_ref[:, width : 2 * width] = nn(normed_t, gk_ref[...]).astype(BF16)
    grads_ref[:, 2 * width : 3 * width] = nn(normed_t, gv_ref[...]).astype(BF16)
    prenorm_grad = inputs_back(experts, tok_ref, w_ref, gq_t_ref, gk_ref, gv_ref, gmid_ref, inputs_grad_ref)
    table = table_back(buckets, shards, width, bucket_ref, fold_ref)
    grads_ref[:, 3 * width : 3 * width + LANES] = small_grads(experts, router_grad, prenorm_grad, midnorm_grad, table)


def combine(local, cap, here, routes_ref, gates_ref, middle_ref, reply_refs, out_ref):
    n, width = middle_ref.shape
    c0, c1, _, _ = places_by_row(routes_ref[...], here, local, cap)
    for cut in chunked(n):
        picked0 = jnp.zeros((cut.stop - cut.start, width), F32)
        picked1 = jnp.zeros((cut.stop - cut.start, width), F32)
        for at, reply_ref in enumerate(reply_refs):
            lane = iota((cut.stop - cut.start, cap), 1) + at * cap
            picked0 += nn(hot(lane == c0[cut]), reply_ref[...])
            picked1 += nn(hot(lane == c1[cut]), reply_ref[...])
        out = middle_ref[cut, :] + gates_ref[cut, 0:1] * picked0 + gates_ref[cut, 1:2] * picked1
        out_ref[cut, :] = out.astype(BF16)


def combine_kernel(local, cap, here_ref, routes_ref, gates_ref, middle_ref, *rest):
    *reply_refs, out_ref = rest
    combine(local, cap, here_ref[0], routes_ref, gates_ref, middle_ref, reply_refs, out_ref)


class View:
    def __init__(self, ref, index=None):
        self.ref, self.index = ref, index

    def __getitem__(self, index):
        return View(self.ref, index)

    def cut(self):
        return self.ref if self.index is None else self.ref.at[self.index]


class Window:
    def __init__(self, ref, lead, shape):
        self.ref, self.lead, self.shape = ref, lead, shape

    def whole(self, index):
        index = () if index is Ellipsis else index if isinstance(index, tuple) else (index,)
        index += (slice(None),) * (len(self.shape) - len(index))
        limited = [slice(0, size) if i == slice(None) else i for i, size in zip(index, self.shape)]
        return (*self.lead, *limited)

    def __getitem__(self, index):
        return self.ref[self.whole(index)]

    def __setitem__(self, index, value):
        self.ref[self.whole(index)] = value

    def view(self, *index):
        return View(self.ref, self.whole(index))


class Remote:
    def __init__(self, *args):
        self.args = args

    def make(self):
        src, dst, sends, receives, at, axis, peer = self.args
        return pltpu.make_async_remote_copy(
            src_ref=src.cut(),
            dst_ref=dst.cut(),
            send_sem=sends.at[at],
            recv_sem=receives.at[at],
            device_id={axis: peer},
            device_id_type=MESH,
        )

    def start(self):
        self.make().start()

    def wait_send(self):
        self.make().wait_send()

    def wait_recv(self):
        self.make().wait_recv()

    def wait(self):
        self.wait_send()
        self.wait_recv()


class Local:
    def __init__(self, *args):
        self.args = args

    def make(self):
        src, dst, sems, at = self.args
        return pltpu.make_async_copy(src.cut(), dst.cut(), sems.at[at])

    def wait(self):
        self.make().wait()


class Links:
    def __init__(self, send_sem, recv_sem, local_sem):
        self.send_sem, self.recv_sem, self.local_sem = send_sem, recv_sem, local_sem
        self.sent = self.moved = 0
        self.open_sends = []

    def send(self, src, dst, axis, peer):
        copy = Remote(src, dst, self.send_sem, self.recv_sem, self.sent, axis, peer)
        self.sent += 1
        copy.start()
        self.open_sends.append(copy)
        return copy

    def move(self, src, dst):
        copy = Local(src, dst, self.local_sem, self.moved)
        self.moved += 1
        copy.make().start()
        return copy

    def forget(self, copies):
        self.open_sends = [other for other in self.open_sends if all(copy is not other for copy in copies)]

    def close(self):
        for copy in self.open_sends:
            copy.wait_send()


SENDS, MOVES = 144, 22


def layer_kernel(experts, local, cap, buckets, shards, names, *refs):
    r = SimpleNamespace(**dict(zip(names, refs, strict=True)))
    groups = experts // local
    me, here = lax.axis_index(DP), lax.axis_index(EXPERT)
    tok_ref, cot_ref, w_ref, routes_ref, bucket_ref = r.tok, r.cot, r.w, r.routes, r.bucket
    n, width = tok_ref.shape
    rows = r.wq.shape[0]
    slab = r.up.shape[2]
    across, along, core, diagonal = me ^ 2, me ^ 4, me ^ 1, me ^ 6
    barrier = pltpu.get_barrier_semaphore()
    for peer in (across, along, core):
        pl.semaphore_signal(barrier, inc=1, device_id={DP: peer}, device_id_type=MESH)
    for m in range(1, groups):
        pl.semaphore_signal(barrier, inc=1, device_id={EXPERT: here ^ m}, device_id_type=MESH)
    pl.semaphore_wait(barrier, 3 + groups - 1)
    links = Links(r.send_sem, r.recv_sem, r.local_sem)
    send, move = links.send, links.move

    def rows_of(owner, start=0, count=rows):
        return pl.ds(pl.multiple_of(owner * rows + start, 16), count)

    first = 3 * width + LANES
    parts = (slice(0, first), slice(first, first + width))
    mine = rows_of(me)
    w_ref[mine, 0:width] = r.wq[...]
    w_ref[mine, width : 2 * width] = r.wk[...]
    w_ref[mine, 2 * width : 3 * width] = r.wv[...]
    w_ref[mine, 3 * width : first] = r.small[...]
    w_ref[mine, first:] = r.wo[...]

    def w_copy(part, owner, peer, start=0, count=rows):
        view = View(w_ref)[rows_of(owner, start, count), parts[part]]
        return send(view, view, DP, peer)

    w_own = [[w_copy(part, me, peer) for peer in (across, along, core)] for part in range(2)]

    d0, d1 = places_by_lane(r.routes_t[...], here, experts, local, cap)

    def dispatch(values, out_ref, in_ref):
        copies = []
        for l in range(local):
            for m in range(groups):
                moved = put_rows(values, d0, d1, (m * local + l) * cap, cap)
                cut = slice(m * cap, (m + 1) * cap)
                if m == 0:
                    in_ref[l, cut, :] = moved
                else:
                    out_ref[l, cut, :] = moved
                    copies.append(send(View(out_ref)[l, cut, :], View(in_ref)[l, cut, :], EXPERT, here ^ m))
        return copies

    cot_copies = dispatch(cot_ref[...], r.out_a, r.cots)
    half = rows // 2
    w_passed = []
    for part in range(2):
        w_own[part][0].wait_recv()
        one = w_copy(part, across, along, 0, half)
        two = w_copy(part, across, core)
        w_own[part][1].wait_recv()
        three = w_copy(part, along, across, half, half)
        four = w_copy(part, along, core)
        w_passed.append((one, three, two, four))

    kinds = ((UP, r.up, r.up_a, r.up_b), (DOWN, r.down, r.down_a, r.down_b))
    weight_copies = {}

    def weights_out(l):
        for kind, own_ref, a_ref, b_ref in kinds:
            key = (l, kind)
            weight_copies[key, OWN] = move(View(own_ref)[l], View(a_ref)[l, 0])
            weight_copies[key, (A, 1)] = send(View(own_ref)[l], View(a_ref)[l, 1], DP, across)
            weight_copies[key, (A, 2)] = send(View(own_ref)[l], View(a_ref)[l, 2], DP, along)
            weight_copies[key, (B, 0)] = send(View(own_ref)[l], View(b_ref)[l, 0], DP, core)

    def weights_on(l):
        for kind, own_ref, a_ref, b_ref in kinds:
            key = (l, kind)
            at, peer = (1, along) if kind == UP else (2, across)
            weight_copies[key, (A, at)].wait_recv()
            weight_copies[key, (A, 3)] = send(View(a_ref)[l, at], View(a_ref)[l, 3], DP, peer)
            weight_copies[key, (B, at)] = send(View(a_ref)[l, at], View(b_ref)[l, at], DP, core)
        for kind, own_ref, a_ref, b_ref in kinds:
            key = (l, kind)
            at = 2 if kind == UP else 1
            weight_copies[key, (A, at)].wait_recv()
            weight_copies[key, (B, at)] = send(View(a_ref)[l, at], View(b_ref)[l, at], DP, core)

    def weights_last(l):
        for kind, own_ref, a_ref, b_ref in kinds:
            key = (l, kind)
            weight_copies[key, (A, 3)].wait_recv()
            weight_copies[key, (B, 3)] = send(View(a_ref)[l, 3], View(b_ref)[l, 3], DP, core)

    def weights_in(l):
        for kind, *_ in kinds:
            weight_copies[(l, kind), OWN].wait()
            for at in range(4):
                weight_copies[(l, kind), (B, at)].wait_recv()

    weights_out(0)
    v_t_ref = Window(r.gh, (), (width, n))

    def w_finish(part):
        one, three, two, four = w_passed[part]
        one.wait_recv()
        three.wait_recv()
        five = w_copy(part, diagonal, core)
        for copy in (w_own[part][2], two, four, five):
            copy.wait_recv()

    w_finish(0)

    project_inputs(
        experts, buckets, shards, tok_ref, w_ref, bucket_ref, r.q, r.k, r.v, r.normed_t, v_t_ref, r.line
    )
    attend(r.q, r.k, v_t_ref, r.line, r.twice, r.merged_t)
    w_finish(1)
    slots_out, slots_in = r.slots_out, r.slots_in
    route(
        experts, local, cap, here, tok_ref, w_ref, routes_ref, r.merged_t, r.middle, r.second, r.gates,
        [slots_out.at[m] for m in range(groups)],
    )
    slot_copies = [send(View(slots_out)[m], View(slots_in)[m], EXPERT, here ^ m) for m in range(1, groups)]
    slots_in[0] = slots_out[0]
    row_copies = dispatch(r.second[...], r.out_b, r.rows)
    weights_on(0)
    weights_out(1)
    weights_last(0)
    weights_in(0)
    for copy in cot_copies[: groups - 1] + row_copies[: groups - 1] + slot_copies:
        copy.wait_recv()

    up_buf, down_buf, ug_buf, dg_buf, core_buf = r.up_buf, r.down_buf, r.ug_buf, r.dg_buf, r.core_buf
    gr_ref, act_ref, gh_ref, reply_ref, back_ref = r.gr, r.act, r.gh, r.reply, r.back
    total_rows = groups * cap
    core_sems, hop_sems = (r.core_send, r.core_recv), (r.hop_send, r.hop_recv)
    back_sems = (r.back_send, r.back_recv)
    halves = [slice(i * slab, (i + 1) * slab) for i in range(2)]

    def remote(src, dst, sems, at, axis, peer):
        return pltpu.make_async_remote_copy(
            src_ref=src, dst_ref=dst, send_sem=sems[0].at[at], recv_sem=sems[1].at[at],
            device_id={axis: peer}, device_id_type=MESH,
        )

    def fetches(l, g, a_side, wait=False):
        for i in range(2):
            at = i if wait else 2 * (3 - g) + i if a_side else 2 * g + i
            up, down = (r.up_a, r.down_a) if a_side else (r.up_b, r.down_b)
            slot = lax.rem(g, 2)
            yield pltpu.make_async_copy(up.at[l, at], up_buf.at[slot, :, halves[i]], r.fetch_sem.at[slot, i])
            yield pltpu.make_async_copy(down.at[l, at], down_buf.at[slot, halves[i], :], r.fetch_sem.at[slot, 2 + i])

    def fetch(l, g):
        for a_side in (False, True):

            @pl.when((g >= 2) == a_side)
            def _():
                for copy in fetches(l, g, a_side):
                    copy.start()

    def core_copies(l, slab_at, i, out):
        at = (l * 4 + slab_at) * 2
        yield remote(ug_buf.at[out, :, halves[i]], r.core_up.at[l, slab_at], core_sems, at, DP, core)
        yield remote(dg_buf.at[out, halves[i], :], r.core_down.at[l, slab_at], core_sems, at + 1, DP, core)

    def t_copy(l, kind, i, out, half_at):
        at = l * 4 + (0 if kind == UP else 2) + i
        if kind == UP:
            return remote(ug_buf.at[out, :, halves[half_at]], r.t_up.at[l, i], hop_sems, at, DP, along)
        return remote(dg_buf.at[out, halves[half_at], :], r.t_down.at[l, i], hop_sems, at, DP, across)

    def own_moves(l, out):
        yield pltpu.make_async_copy(ug_buf.at[out, :, halves[0]], r.own_up.at[l], r.own_sem.at[0])
        yield pltpu.make_async_copy(dg_buf.at[out, halves[0], :], r.own_down.at[l], r.own_sem.at[1])

    def kept_move(l, kind, out):
        if kind == UP:
            return pltpu.make_async_copy(ug_buf.at[out, :, halves[1]], r.keep_up.at[l], r.own_sem.at[2])
        return pltpu.make_async_copy(dg_buf.at[out, halves[0], :], r.keep_down.at[l], r.own_sem.at[3])

    def sent_from(l, g, out):
        def when(condition):
            return (lambda f: f() if condition else None) if isinstance(g, int) else pl.when(condition)

        @when(g < 2)
        def _():
            for i in range(2):
                for copy in core_copies(l, 2 * g + i, i, out):
                    copy.wait_send()

        @when(g == 2)
        def _():
            for copy in (t_copy(l, UP, 0, out, 0), t_copy(l, UP, 1, out, 1), t_copy(l, DOWN, 1, out, 1)):
                copy.wait_send()
            kept_move(l, DOWN, out).wait()

        @when(g == 3)
        def _():
            t_copy(l, DOWN, 0, out, 1).wait_send()
            for copy in (*own_moves(l, out), kept_move(l, UP, out)):
                copy.wait()

    def back_copy(l, m):
        cut = slice(m * cap, (m + 1) * cap)
        at = l * (groups - 1) + m - 1
        return remote(r.out_a.at[l, cut, :], r.backs.at[l, cut, :], back_sems, at, EXPERT, here ^ m)

    def dot_copy(l, m):
        at = (local + l) * (groups - 1) + m - 1
        return remote(r.dots_out.at[l, m], r.dots_in.at[l, m], back_sems, at, EXPERT, here ^ m)

    def step(s, carry):
        l, g, out = lax.div(s, 4), lax.rem(s, 4), lax.rem(s, 3)
        slot = lax.rem(g, 2)
        x, cots = r.rows.at[l], r.cots.at[l]

        @pl.when(s == 1)
        def _():
            weights_on(1)

        @pl.when(s == 3)
        def _():
            weights_last(1)

        @pl.when(s == 4)
        def _():
            weights_in(1)
            for copy in cot_copies[groups - 1 :] + row_copies[groups - 1 :]:
                copy.wait_recv()

        @pl.when(g == 0)
        def _():
            fetch(l, g)
            for m in range(groups):
                cut = slice(m * cap, (m + 1) * cap)
                slots = slots_in[m, pl.ds(l, 1), :]
                gate = jnp.transpose(jnp.broadcast_to(slots, (LANES, slots.shape[1])))[:cap, 0:1]
                gr_ref[cut, :] = (gate * cots[cut, :].astype(F32)).astype(BF16)
            core_buf[...] = jnp.zeros_like(core_buf)
            reply_ref[...] = jnp.zeros_like(reply_ref)
            back_ref[...] = jnp.zeros_like(back_ref)

        for copy in fetches(l, g, False, True):
            copy.wait()

        @pl.when(g < 3)
        def _():
            fetch(l, g + 1)

        def arrivals():
            for i in range(2):
                at = 2 * (3 - g) + i
                yield pltpu.make_async_copy(r.core_up.at[l, at], core_buf.at[0, :, halves[i]], r.add_sem.at[i])
                yield pltpu.make_async_copy(r.core_down.at[l, at], core_buf.at[1, halves[i], :], r.add_sem.at[2 + i])

        @pl.when(g >= 2)
        def _():
            for i in range(2):
                for copy in core_copies(l, 2 * (3 - g) + i, i, out):
                    copy.wait_recv()
            for copy in arrivals():
                copy.start()

        for cut in chunked(total_rows):
            act, slope = gelu_both(nn(x[cut, :], up_buf[slot]))
            act_ref[cut, :] = act.astype(BF16)
            gh_ref[cut, :] = (nt(gr_ref[cut, :], down_buf[slot]) * slope).astype(BF16)
            reply_ref[cut, :] += nn(act_ref[cut, :], down_buf[slot])
            back_ref[cut, :] += nt(gh_ref[cut, :], up_buf[slot])

        @pl.when(s >= 3)
        def _():
            sent_from(lax.div(s - 3, 4), lax.rem(s - 3, 4), out)

        @pl.when(g >= 2)
        def _():
            for copy in arrivals():
                copy.wait()

        for cut in chunked(width):
            ug = tn(x[:, cut], gh_ref[...]) + core_buf[0, cut, :].astype(F32)
            ug_buf[out, cut, :] = ug.astype(BF16)
            dg = tn(act_ref[:, cut], gr_ref[...]) + core_buf[1, cut, :].astype(F32)
            dg_buf[out, cut, :] = dg.astype(BF16)

        @pl.when(g < 2)
        def _():
            for i in range(2):
                for copy in core_copies(l, 2 * g + i, i, out):
                    copy.start()

        @pl.when(g == 2)
        def _():
            t_copy(l, UP, 0, out, 0).start()
            t_copy(l, UP, 1, out, 1).start()
            t_copy(l, DOWN, 1, out, 1).start()
            kept_move(l, DOWN, out).start()

        @pl.when(g == 3)
        def _():
            t_copy(l, DOWN, 0, out, 1).start()
            for copy in own_moves(l, out):
                copy.start()
            kept_move(l, UP, out).start()
            for m in range(1, groups):
                at = m - 1
                for copies in (cot_copies, row_copies):
                    for which in range(local):

                        @pl.when(l == which)
                        def _():
                            copies[which * (groups - 1) + at].wait_send()

            for m in range(groups):
                cut = slice(m * cap, (m + 1) * cap)
                if m == 0:
                    r.backs[l, cut, :] = back_ref[cut, :].astype(BF16)
                else:
                    r.out_a[l, cut, :] = back_ref[cut, :].astype(BF16)
                    back_copy(l, m).start()
            reply = reply_ref[...].astype(BF16)
            r.out_b[l] = reply
            dots = jnp.sum(reply.astype(F32) * cots[...].astype(F32), axis=1, keepdims=True)
            dots = jnp.transpose(jnp.broadcast_to(dots, (total_rows, LANES)))[0:8]
            r.dots_in[l, 0] = dots[:, :256]
            for m in range(1, groups):
                r.dots_out[l, m] = pltpu.roll(dots, total_rows - m * cap, 1)[:, :256]
                dot_copy(l, m).start()

        return carry

    lax.fori_loop(0, 4 * local, step, 0)
    links.forget(cot_copies + row_copies)
    v_copies = {}

    def t_stage(l):
        t_copy(l, UP, 1, 0, 1).wait_recv()
        t_copy(l, DOWN, 1, 0, 1).wait_recv()
        return [
            move(View(r.t_up)[l, 1], View(up_buf)[l, :, :slab]),
            move(View(r.t_down)[l, 1], View(down_buf)[l, :slab, :]),
            move(View(r.keep_up)[l], View(up_buf)[l, :, slab:]),
            move(View(r.keep_down)[l], View(down_buf)[l, slab:, :]),
        ]

    def t_pass(l, staged):
        for copy in staged:
            copy.wait()
        up_sum = up_buf[l, :, slab:].astype(F32) + up_buf[l, :, :slab].astype(F32)
        up_buf[l, :, :slab] = up_sum.astype(BF16)
        v_copies[l, UP] = send(View(up_buf)[l, :, :slab], View(r.v_up)[l], DP, across)
        down_sum = down_buf[l, slab:, :].astype(F32) + down_buf[l, :slab, :].astype(F32)
        down_buf[l, :slab, :] = down_sum.astype(BF16)
        v_copies[l, DOWN] = send(View(down_buf)[l, :slab, :], View(r.v_down)[l], DP, along)

    t_pass(0, t_stage(0))

    for l in range(local):
        for m in range(1, groups):
            back_copy(l, m).wait()
            dot_copy(l, m).wait()
    reply_copies = []
    for l in range(local):
        for m in range(1, groups):
            cut = slice(m * cap, (m + 1) * cap)
            reply_copies.append(
                send(View(r.out_b)[l, cut, :], View(r.reply_in)[l, cut, :], EXPERT, here ^ m)
            )
    order = [(m, l) for m in range(groups) for l in range(local)]
    gm_ref, gk_ref = Window(r.rows, (0,), (n, width)), Window(r.rows, (1,), (n, width))
    gv_ref, k_t_ref = Window(r.cots, (0,), (n, width)), v_t_ref
    gq_t_ref, gmid_ref = Window(gr_ref, (), (width, n)), Window(reply_ref, (), (n, width))
    branch_ref, normed_t = Window(act_ref, (), (n, width)), r.normed_t
    router_grad, midnorm_grad = middle_back(
        experts, local, cap, here, w_ref, routes_ref, cot_ref, r.middle, r.second, r.gates,
        [Window(r.backs.at[l, m * cap : (m + 1) * cap, :], (), (cap, width)) for m, l in order],
        [r.dots_in.at[l, m] for m, l in order],
        gmid_ref, branch_ref,
    )
    r.gain_row[0:1, :] = midnorm_grad
    r.router_grad[...] = router_grad
    part = width // 2
    chunk_at = (2, 0)
    for at in range(4 * local - 3, 4 * local):
        sent_from(at // 4, at % 4, at % 3)
    for c in range(2):
        for cut in chunked(width):
            project = nn(r.merged_t[cut, :], branch_ref[:, c * part : (c + 1) * part])
            dg_buf[chunk_at[c], cut, part:] = project.astype(BF16)
    for cut in chunked(n):
        gm_ref[cut, :] = nt(branch_ref[cut, :], w_ref[:, first:]).astype(BF16)
    k_t_ref[...] = jnp.transpose(r.k[...])

    def weight_grads(c):
        at, columns = chunk_at[c], slice(c * part, (c + 1) * part)
        for cut in chunked(width):
            ug_buf[at, cut, :part] = nt(normed_t[cut, :], gq_t_ref[columns, :]).astype(BF16)
            ug_buf[at, cut, part:] = nn(normed_t[cut, :], gk_ref[:, columns]).astype(BF16)
            dg_buf[at, cut, :part] = nn(normed_t[cut, :], gv_ref[:, columns]).astype(BF16)

    peers = [me ^ mask for mask in range(8)]
    rows_at = [rows_of(peer) for peer in peers]

    class Reduce:
        def __init__(self, pieces):
            self.pieces = pieces

        def start(self):
            self.zero = []
            for g, from_core, *_ in self.pieces:
                for i in (2, 3, 1, 0):
                    copy = send(g.view(rows_at[1 ^ (2 * i)]), from_core.view(i), DP, peers[1])
                    self.zero.append((i, g, from_core, copy))

        def one(self):
            for i, g, from_core, copy in self.zero:
                copy.wait_recv()
                at = rows_at[2 * i]
                g[at, :] = (g[at, :].astype(F32) + from_core[i].astype(F32)).astype(BF16)
            self.hops = []
            for g, _, hop_one, _, mask in self.pieces:
                for i, owner in enumerate((mask, 6)):
                    self.hops.append(send(g.view(rows_at[owner]), hop_one.view(i), DP, peers[mask]))

        def two(self):
            for copy in self.hops:
                copy.wait_recv()
            self.last = []
            for g, _, hop_one, hop_two, mask in self.pieces:
                at = rows_at[6 - mask]
                g[at, :] = (g[at, :].astype(F32) + hop_one[1].astype(F32)).astype(BF16)
                self.last.append(send(g.view(at), hop_two.view(), DP, peers[6 - mask]))

        def three(self):
            for copy in self.last:
                copy.wait_recv()
            return [
                g[rows_at[0], :].astype(F32) + hop_one[0].astype(F32) + hop_two[...].astype(F32)
                for g, _, hop_one, hop_two, _ in self.pieces
            ]

    def window(ref, *lead):
        return Window(ref, lead, ref.shape[len(lead) :])

    chunks = [
        Reduce(
            [
                (window(ug_buf, chunk_at[c]), window(r.core_a, c), window(r.hop_a, c), window(r.last_a, c), 4),
                (window(dg_buf, chunk_at[c]), window(r.core_b, c), window(r.hop_b, c), window(r.last_b, c), 2),
            ]
        )
        for c in range(2)
    ]
    little = Reduce([(window(r.little), window(r.core_c), window(r.hop_c), window(r.last_c), 4)])
    z_copies, g_copies = {}, {}
    share = pl.ds(pl.multiple_of(here * part, LANES), part)

    def z_send(c):
        a, b = chunks[c].three()
        r.sum[c, :, :width] = a.astype(BF16)
        r.sum[c, :, width:] = b.astype(BF16)
        z_copies[c] = []
        for m in range(1, groups):
            cut = pl.ds(pl.multiple_of((here ^ m) * part, LANES), part)
            z_copies[c].append(send(View(r.sum)[c, :, cut], View(r.z_in)[c, m], EXPERT, here ^ m))

    def z_gather(c):
        total = r.sum[c, :, share].astype(F32)
        for m in range(1, groups):
            z_copies[c][m - 1].wait_recv()
            total += r.z_in[c, m].astype(F32)
        r.z_sum[c] = total.astype(BF16)
        g_copies[c] = [
            send(View(r.z_sum)[c], View(r.z_all)[c, m], EXPERT, here ^ m) for m in range(1, groups)
        ]
        r.main[here, :, c * part : (c + 1) * part] = r.z_sum[c]

    def z_finish(c):
        for m in range(1, groups):
            g_copies[c][m - 1].wait_recv()
            r.main[here ^ m, :, c * part : (c + 1) * part] = r.z_all[c, m]

    def after(hp):
        @pl.when(hp == 2)
        def _():
            weight_grads(0)
            chunks[0].start()

        @pl.when(hp == 3)
        def _():
            chunks[0].one()
            t_pass(1, t_stage(1))

        @pl.when(hp == 4)
        def _():
            chunks[0].two()

    attend_back(after, r.q, r.k, r.v, gm_ref, k_t_ref, r.line, r.twice, gq_t_ref, gk_ref, gv_ref, r.fold)
    weight_grads(1)
    chunks[1].start()
    z_send(0)
    prenorm_grad = inputs_back(experts, tok_ref, w_ref, gq_t_ref, gk_ref, gv_ref, gmid_ref, gm_ref)
    results = [move(gm_ref.view(), View(r.inputs_grad))]
    chunks[1].one()
    z_gather(0)
    table = table_back(buckets, shards, width, bucket_ref, r.fold)
    r.little[...] = small_grads(
        experts, r.router_grad[...], prenorm_grad, r.gain_row[0:1, :], table
    )
    little.start()
    chunks[1].two()
    little.one()
    z_finish(0)
    for copy in reply_copies:
        copy.wait_recv()
    staged = [move(View(r.reply_in)[l, cap:, :], View(core_buf)[l, cap:, :]) for l in range(local)]
    z_send(1)
    little.two()
    for l, copy in enumerate(staged):
        core_buf[l, :cap, :] = r.out_b[l, :cap, :]
        copy.wait()
    layer_out_ref = Window(r.cots, (1,), (n, width))
    combine(
        local, cap, here, routes_ref, r.gates, r.middle,
        [core_buf.at[l, m * cap : (m + 1) * cap, :] for m, l in order], layer_out_ref,
    )
    results.append(move(layer_out_ref.view(), View(r.layer_out)))
    z_gather(1)
    (small_sum,) = little.three()
    r.small_z[here] = small_sum.astype(BF16)
    small_copies = [
        send(View(r.small_z)[here], View(r.small_z)[here], EXPERT, here ^ m) for m in range(1, groups)
    ]
    z_finish(1)
    for copy in small_copies:
        copy.wait_recv()
    total = r.small_z[0].astype(F32)
    for m in range(1, groups):
        total += r.small_z[m].astype(F32)
    r.small_out[...] = total
    for l in range(local):
        for kind in (UP, DOWN):
            t_copy(l, kind, 0, 0, 0).wait_recv()
            v_copies[l, kind].wait_recv()
    for copy in results:
        copy.wait()
    links.close()


def whole_layer(
    tokens, query_weight, key_weight, value_weight, project_weight, small, routes, bucket_row, cotangent,
    up_weight, down_weight, experts, buckets, table_rows_own,
):
    n, width = tokens.shape
    shards, groups = lax.axis_size(DP), lax.axis_size(EXPERT)
    local, _, slab = up_weight.shape
    cap = 3 * n // experts
    rows = query_weight.shape[0]
    total = groups * cap
    vmem, hbm = pl.BlockSpec(memory_space=pltpu.VMEM), pl.BlockSpec(memory_space=pl.ANY)

    def array(*s, dtype=BF16):
        return jax.ShapeDtypeStruct(s, dtype)

    inputs = dict(
        tok=tokens, wq=query_weight, wk=key_weight, wv=value_weight, wo=project_weight, small=small,
        routes=routes, routes_t=routes.T, bucket=bucket_row, cot=cotangent, up=up_weight, down=down_weight,
    )
    near = dict(
        main=array(4, rows, width),
        small_out=array(rows, LANES, dtype=F32),
    )
    far = dict(
        layer_out=array(n, width),
        inputs_grad=array(n, width),
        own_up=array(local, width, slab),
        own_down=array(local, slab, width),
        keep_up=array(local, width, slab),
        keep_down=array(local, slab, width),
        t_up=array(local, 2, width, slab),
        t_down=array(local, 2, slab, width),
        v_up=array(local, width, slab),
        v_down=array(local, slab, width),
        up_a=array(local, 4, width, slab),
        up_b=array(local, 4, width, slab),
        down_a=array(local, 4, slab, width),
        down_b=array(local, 4, slab, width),
        core_up=array(local, 4, width, slab),
        core_down=array(local, 4, slab, width),
        reply_in=array(local, total, width),
    )
    v, part = pltpu.VMEM, width // 2
    scratch = dict(
        w=v((width, 4 * width + LANES), BF16),
        out_a=v((local, total, width), BF16),
        out_b=v((local, total, width), BF16),
        rows=v((local, total, width), BF16),
        cots=v((local, total, width), BF16),
        backs=v((local, total, width), BF16),
        slots_out=v((groups, 8, 256), F32),
        slots_in=v((groups, 8, 256), F32),
        dots_out=v((local, groups, 8, 256), F32),
        dots_in=v((local, groups, 8, 256), F32),
        q=v((n, width), BF16),
        k=v((n, width), BF16),
        v=v((n, width), BF16),
        normed_t=v((width, n), BF16),
        second=v((n, width), BF16),
        merged_t=v((width, n), BF16),
        middle=v((n, width), F32),
        gates=v((n, LANES), F32),
        line=v((16, n), F32),
        twice=v((LANES, 2 * n), F32),
        fold=v((HEADS, 8, n), F32),
        gr=v((total, width), BF16),
        act=v((total, width), BF16),
        gh=v((total, width), BF16),
        reply=v((total, width), F32),
        back=v((total, width), F32),
        up_buf=v((2, width, width), BF16),
        down_buf=v((2, width, width), BF16),
        ug_buf=v((3, width, width), BF16),
        dg_buf=v((3, width, width), BF16),
        core_buf=v((2, width, width), BF16),
        core_a=v((2, 4, rows, width), BF16),
        core_b=v((2, 4, rows, width), BF16),
        hop_a=v((2, 2, rows, width), BF16),
        hop_b=v((2, 2, rows, width), BF16),
        last_a=v((2, rows, width), BF16),
        last_b=v((2, rows, width), BF16),
        sum=v((2, rows, 2 * width), BF16),
        z_in=v((2, groups, rows, part), BF16),
        z_sum=v((2, rows, part), BF16),
        z_all=v((2, groups, rows, part), BF16),
        little=v((width, LANES), BF16),
        gain_row=v((8, width), F32),
        router_grad=v((width, LANES), F32),
        core_c=v((4, rows, LANES), BF16),
        hop_c=v((2, rows, LANES), BF16),
        last_c=v((rows, LANES), BF16),
        small_z=v((groups, rows, LANES), BF16),
        send_sem=pltpu.SemaphoreType.DMA((SENDS,)),
        recv_sem=pltpu.SemaphoreType.DMA((SENDS,)),
        local_sem=pltpu.SemaphoreType.DMA((MOVES,)),
        fetch_sem=pltpu.SemaphoreType.DMA((2, 4)),
        add_sem=pltpu.SemaphoreType.DMA((4,)),
        own_sem=pltpu.SemaphoreType.DMA((4,)),
        core_send=pltpu.SemaphoreType.DMA((8 * local,)),
        core_recv=pltpu.SemaphoreType.DMA((8 * local,)),
        hop_send=pltpu.SemaphoreType.DMA((4 * local,)),
        hop_recv=pltpu.SemaphoreType.DMA((4 * local,)),
        back_send=pltpu.SemaphoreType.DMA((2 * local * (groups - 1),)),
        back_recv=pltpu.SemaphoreType.DMA((2 * local * (groups - 1),)),
    )
    names = [*inputs, *near, *far, *scratch]
    outs = pl.pallas_call(
        functools.partial(layer_kernel, experts, local, cap, buckets, shards, names),
        name="layer",
        out_shape=[*near.values(), *far.values()],
        in_specs=[vmem] * 10 + [hbm] * 2,
        out_specs=[vmem] * len(near) + [hbm] * len(far),
        scratch_shapes=[*scratch.values()],
        compiler_params=pltpu.CompilerParams(
            vmem_limit_bytes=LAYER_VMEM, collective_id=0, has_side_effects=True
        ),
        cost_estimate=pl.CostEstimate(flops=60 * 10**9, bytes_accessed=400 * 10**6, transcendentals=0),
    )(*inputs.values())
    o = SimpleNamespace(**dict(zip([*near, *far], outs)))

    def total_of(own, first_hop, last_hop):
        return own.astype(F32) + first_hop[:, 0].astype(F32) + last_hop.astype(F32)

    little = o.small_out
    return (
        o.layer_out,
        o.inputs_grad,
        o.main[0].astype(F32),
        o.main[1].astype(F32),
        o.main[2].astype(F32),
        o.main[3].astype(F32),
        little[:, :experts],
        little[:, experts],
        little[:, experts + 1],
        little[:table_rows_own, TABLE_AT : TABLE_AT + HEADS],
        total_of(o.own_up, o.t_up, o.v_up),
        total_of(o.own_down, o.t_down, o.v_down),
    )


def swap(value, axis, bit):
    return lax.ppermute(value, axis, [(i, i ^ bit) for i in range(lax.axis_size(axis))])


def swap_all(values):
    return [v if m == 0 else swap(v, EXPERT, m) for m, v in enumerate(values)]


def body(
    tokens,
    query_weight,
    key_weight,
    value_weight,
    project_weight,
    router_weight,
    prenorm_gain,
    midnorm_gain,
    bias_table,
    up_weight,
    down_weight,
    routes,
    bucket_index,
    cotangent,
):
    n, width = tokens.shape
    experts = router_weight.shape[1]
    shards, groups = lax.axis_size(DP), lax.axis_size(EXPERT)
    local, _, slab = up_weight.shape
    cap = 3 * n // experts
    buckets = bias_table.shape[0] * shards
    own_rows = query_weight.shape[0]
    hidden = slab * shards
    direct = slab % LANES == 0 and shards == 8
    here = lax.axis_index(EXPERT).astype(I32).reshape(1)
    smem = pl.BlockSpec(memory_space=pltpu.SMEM)
    vmem = pl.BlockSpec(memory_space=pltpu.VMEM)
    hbm = pl.BlockSpec(memory_space=pl.ANY)
    routes_t = routes.T
    bucket_row = bucket_index[None, :]

    def shape(s, dtype=BF16):
        return jax.ShapeDtypeStruct(s, dtype)

    small = jnp.concatenate(
        [
            router_weight,
            prenorm_gain[:, None],
            midnorm_gain[:, None],
            jnp.zeros((own_rows, TABLE_AT - experts - 2), BF16),
            jnp.pad(bias_table, ((0, own_rows - bias_table.shape[0]), (0, 0))),
            jnp.zeros((own_rows, LANES - TABLE_AT - HEADS), BF16),
        ],
        axis=1,
    )
    if direct:
        return whole_layer(
            tokens, query_weight, key_weight, value_weight, project_weight, small, routes, bucket_row, cotangent,
            up_weight, down_weight, experts, buckets, bias_table.shape[0],
        )
    packed_width = 4 * width + LANES
    slots_shape = (groups, 8, 256)
    kept = [shape((n, width))] * 3 + [
        shape((width, n)),
        shape((width, n)),
        shape((n, width), F32),
        shape((n, width)),
        shape((n, LANES), F32),
        shape((16, n), F32),
    ]
    packed = jnp.concatenate(
        [query_weight, key_weight, value_weight, small, project_weight], axis=1
    )
    full = lax.all_gather(packed, DP, axis=0, tiled=True)
    cot_out = vmem_call(
        functools.partial(scatter_kernel, experts, local, cap),
        "send_cotangent",
        [shape((cap, width))] * experts,
        specs=[smem, vmem, vmem],
    )(here, routes_t, cotangent)
    up_all = lax.all_gather(up_weight, DP, axis=2, tiled=True)
    down_all = lax.all_gather(down_weight, DP, axis=1, tiled=True)
    up_all = up_all.reshape(local, width, hidden // width, width).transpose(0, 2, 1, 3)
    down_all = down_all.reshape(local, hidden // width, width, width)
    cut = hidden // width // 2
    weights = (up_all[:, :cut], up_all[:, cut:], down_all[:, :cut], down_all[:, cut:])
    forward = vmem_call(
        functools.partial(forward_kernel, experts, local, cap, buckets, shards),
        "attention_forward",
        kept + [shape((cap, width))] * experts + [shape((8, 256), F32)] * groups,
        scratch=[pltpu.VMEM((width, n), BF16), pltpu.VMEM((LANES, 2 * n), F32)],
        specs=[smem] + [vmem] * 5,
    )(here, tokens, full, routes, routes_t, bucket_row)
    q, k, v, normed, merged_t, middle, second, gates, line = forward[:9]
    x_out, slots_out = forward[9 : 9 + experts], forward[9 + experts :]
    slots_in = jnp.stack(swap_all(slots_out))
    x_in = jnp.stack([jnp.stack(swap_all(x_out[l::local])) for l in range(local)])
    cot_in = jnp.stack([jnp.stack(swap_all(cot_out[l::local])) for l in range(local)])

    rows = groups * cap
    replies, backs, dots, up_grads, down_grads = [], [], [], [], []
    for l in range(local):
        count, slab_width = weights[0].shape[1], weights[0].shape[3]
        per = width // slab_width
        outs = pl.pallas_call(
            functools.partial(expert_kernel, l, groups, cap),
            name=EXPERT,
            out_shape=[shape((cap, width))] * (2 * groups)
            + [shape((8, 256), F32)] * groups
            + [shape((count, width, slab_width))] * 2
            + [shape((count, slab_width, width))] * 2,
            in_specs=[hbm, hbm, vmem] + [hbm] * 4,
            out_specs=[vmem] * (3 * groups) + [hbm] * 4,
            scratch_shapes=[
                pltpu.VMEM((rows, width), BF16),
                pltpu.VMEM((width, rows), BF16),
                pltpu.VMEM((rows, width), BF16),
                pltpu.VMEM((rows, width), BF16),
                pltpu.VMEM((rows, width), F32),
                pltpu.VMEM((rows, width), F32),
                pltpu.VMEM((2, width, width), BF16),
                pltpu.VMEM((2, width, width), BF16),
                pltpu.VMEM((2, width, width), BF16),
                pltpu.VMEM((2, width, width), BF16),
                pltpu.VMEM((rows, width), BF16),
                pltpu.VMEM((rows, width), BF16),
                pltpu.SemaphoreType.DMA((2, 2 * per)),
                pltpu.SemaphoreType.DMA((2, 2 * per)),
                pltpu.SemaphoreType.DMA((2, groups)),
            ],
            compiler_params=pltpu.CompilerParams(vmem_limit_bytes=VMEM_LIMIT),
            cost_estimate=pl.CostEstimate(
                flops=12 * rows * width * hidden, bytes_accessed=40 * 10**6, transcendentals=0
            ),
        )(x_in, cot_in, slots_in, *weights)
        replies.append(outs[:groups])
        backs.append(swap_all(outs[groups : 2 * groups]))
        dots.append(swap_all(outs[2 * groups : 3 * groups]))
        ug, dg = outs[3 * groups : 3 * groups + 2], outs[3 * groups + 2 :]
        ug = jnp.concatenate(ug, axis=0).transpose(1, 0, 2).reshape(width, hidden)
        dg = jnp.concatenate(dg, axis=0).reshape(hidden, width)
        up_grads.append(lax.psum_scatter(ug, DP, scatter_dimension=1, tiled=True).astype(F32))
        down_grads.append(lax.psum_scatter(dg, DP, scatter_dimension=0, tiled=True).astype(F32))

    flat = lambda parts: [parts[l][m] for m in range(groups) for l in range(local)]
    inputs_grad, grads = vmem_call(
        functools.partial(backward_kernel, experts, local, cap, buckets, shards),
        "attention_backward",
        [shape((n, width)), shape((width, packed_width))],
        scratch=[
            pltpu.VMEM((n, width), BF16),
            pltpu.VMEM((n, width), F32),
            pltpu.VMEM((width, n), BF16),
            pltpu.VMEM((width, n), BF16),
            pltpu.VMEM((n, width), BF16),
            pltpu.VMEM((n, width), BF16),
            pltpu.VMEM((HEADS, 8, n), F32),
            pltpu.VMEM((LANES, 2 * n), F32),
            pltpu.VMEM((n, width), BF16),
        ],
        specs=[smem] + [vmem] * (14 + 2 * experts),
        flops=40 * 10**9,
        moved=30 * 10**6,
    )(
        here,
        tokens,
        full,
        routes,
        bucket_row,
        cotangent,
        q,
        k,
        v,
        normed,
        merged_t,
        middle,
        second,
        gates,
        line,
        *flat(backs),
        *flat(dots),
    )
    shares = lax.psum_scatter(grads, DP, scatter_dimension=0, tiled=True)
    totals = lax.psum(shares, EXPERT).astype(F32)

    replies = flat([swap_all(r) for r in replies])
    layer_out = vmem_call(
        functools.partial(combine_kernel, local, cap),
        "layer_out",
        shape((n, width)),
        specs=[smem] + [vmem] * (3 + experts),
        flops=4 * n * experts * cap * width,
        moved=6 * 10**6,
    )(here, routes, gates, middle, *replies)

    at = 3 * width
    return (
        layer_out,
        inputs_grad,
        totals[:, :width],
        totals[:, width : 2 * width],
        totals[:, 2 * width : 3 * width],
        totals[:, at + LANES :],
        totals[:, at : at + experts],
        totals[:, at + experts],
        totals[:, at + experts + 1],
        totals[: bias_table.shape[0], at + TABLE_AT : at + TABLE_AT + HEADS],
        jnp.stack(up_grads),
        jnp.stack(down_grads),
    )


def solution(mesh):
    both, first = P((DP, EXPERT), None), P(DP, None)
    up, down = P(EXPERT, None, DP), P(EXPERT, DP, None)
    return jax.shard_map(
        body,
        mesh=mesh,
        in_specs=(both,)
        + (first,) * 5
        + (P(DP), P(DP), first, up, down, both, P(), both),
        out_specs=(both, both) + (first,) * 5 + (P(DP), P(DP), first, up, down),
        check_vma=False,
    )
```

```python
import functools
from types import SimpleNamespace

import jax
import jax.numpy as jnp
from jax import lax
from jax.experimental import pallas as pl
from jax.experimental.pallas import tpu as pltpu
from jax.sharding import PartitionSpec as P

HEADS = 12
HEAD_DIM = 64
EPSILON = 1e-06
NEGATIVE = -1e30
SCALE = HEAD_DIM ** (-0.5)
LANES = 128
TABLE_AT = 32
QBLOCK = 256
F32 = jnp.float32
BF16 = jnp.bfloat16
I32 = jnp.int32
VMEM_LIMIT = 60 * 1024 * 1024
LAYER_VMEM = 63 * 1024 * 1024
MESH = pl.DeviceIdType.MESH
DP, EXPERT = "dp", "expert"
UP, DOWN, OWN, A, B = range(5)


def nn(left, right):
    return lax.dot_general(left, right, (((1,), (0,)), ((), ())), preferred_element_type=F32)


def nt(left, right):
    return lax.dot_general(left, right, (((1,), (1,)), ((), ())), preferred_element_type=F32)


def tn(left, right):
    return lax.dot_general(left, right, (((0,), (0,)), ((), ())), preferred_element_type=F32)


def iota(shape, axis):
    return lax.broadcasted_iota(I32, shape, axis)


def hot(mask):
    return jnp.where(mask, 1.0, 0.0).astype(BF16)


def vmem_call(body, name, out_shape, scratch=(), flops=0, moved=0, specs=None):
    def call(*args):
        in_specs = specs or [pl.BlockSpec(memory_space=pltpu.VMEM)] * len(args)
        return pl.pallas_call(
            body,
            name=name,
            out_shape=out_shape,
            in_specs=in_specs,
            out_specs=jax.tree.map(lambda _: pl.BlockSpec(memory_space=pltpu.VMEM), out_shape),
            scratch_shapes=scratch,
            compiler_params=pltpu.CompilerParams(vmem_limit_bytes=VMEM_LIMIT),
            cost_estimate=pl.CostEstimate(flops=flops, bytes_accessed=moved, transcendentals=0),
        )(*args)

    return call


def places(r, slot, here, local, cap):
    owner = lax.div(r, local)
    return (owner ^ here) * (local * cap) + lax.rem(r, local) * cap + slot.astype(I32)


def places_by_lane(routes_t, here, experts, local, cap):
    n = routes_t.shape[1]
    r0, r1 = routes_t[0:1, :], routes_t[1:2, :]
    tall = iota((-(-experts // 16) * 16, n), 0)
    oh0, oh1 = tall == r0, tall == r1
    earlier = hot(iota((n, n), 0) < iota((n, n), 1))
    count = nn(hot(oh0 | oh1), earlier)
    s0 = jnp.sum(jnp.where(oh0, count, 0.0), axis=0, keepdims=True)
    s1 = jnp.sum(jnp.where(oh1, count, 0.0), axis=0, keepdims=True)
    return places(r0, s0, here, local, cap), places(r1, s1, here, local, cap)


def places_by_row(routes, here, local, cap):
    n = routes.shape[0]
    r0, r1 = routes[:, 0:1], routes[:, 1:2]
    wide = iota((n, LANES), 1)
    oh0, oh1 = wide == r0, wide == r1
    earlier = hot(iota((n, n), 1) < iota((n, n), 0))
    count = nn(earlier, hot(oh0 | oh1))
    s0 = jnp.sum(jnp.where(oh0, count, 0.0), axis=1, keepdims=True)
    s1 = jnp.sum(jnp.where(oh1, count, 0.0), axis=1, keepdims=True)
    return places(r0, s0, here, local, cap), places(r1, s1, here, local, cap), oh0, oh1


def put_rows(values, d0, d1, start, count):
    at = iota((count, values.shape[0]), 0) + start
    return nn(hot((at == d0) | (at == d1)), values).astype(BF16)


def scatter_kernel(experts, local, cap, here_ref, routes_t_ref, values_ref, *out_refs):
    d0, d1 = places_by_lane(routes_t_ref[...], here_ref[0], experts, local, cap)
    values = values_ref[...]
    for at, out_ref in enumerate(out_refs):
        out_ref[...] = put_rows(values, d0, d1, at * cap, cap)


def table_rows(misc, buckets, shards):
    depth = misc.shape[0]
    per, rows = buckets // shards, depth // shards
    b = iota((buckets, depth), 0)
    select = hot(iota((buckets, depth), 1) == lax.div(b, per) * rows + lax.rem(b, per))
    return nn(select, misc)


def toeplitz(line, twice_ref):
    n = line.shape[1]
    rolled = pltpu.roll(jnp.broadcast_to(line, (LANES, n)), 0, 1, stride=1, stride_axis=0)
    twice_ref[:, :n] = rolled
    twice_ref[:, n:] = rolled


def bias_columns(twice_ref, n, block, rows):
    parts = []
    for jb in range(rows // LANES):
        start = (block * QBLOCK - jb * LANES) % n
        parts.append(twice_ref[:, start : start + QBLOCK])
    return jnp.concatenate(parts, axis=0)


def causal(scores, block):
    last = scores.shape[0] - QBLOCK
    keep = iota((QBLOCK, QBLOCK), 0) <= iota((QBLOCK, QBLOCK), 1)
    tail = jnp.where(keep, scores[last:], NEGATIVE)
    return tail if last == 0 else jnp.concatenate([scores[:last], tail], axis=0)


def chunked(count, size=256):
    return [slice(at, at + size) for at in range(0, count, size)]


def project_inputs(experts, buckets, shards, tok_ref, w_ref, bucket_ref, q_ref, k_ref, v_ref, normed_t_ref, v_t_ref, line_ref):
    n, width = tok_ref.shape
    misc = w_ref[:, 3 * width : 3 * width + LANES]
    gain = jnp.transpose(misc.astype(F32))[experts : experts + 1]
    for cut in chunked(n):
        x = tok_ref[cut, :].astype(F32)
        normed = x * lax.rsqrt(jnp.mean(x * x, axis=-1, keepdims=True) + EPSILON) * gain
        normed = normed.astype(BF16)
        normed_t_ref[:, cut] = jnp.transpose(normed)
        query = nn(normed, w_ref[:, :width]).astype(BF16)
        q_ref[cut, :] = (query.astype(F32) * SCALE).astype(BF16)
        k_ref[cut, :] = nn(normed, w_ref[:, width : 2 * width]).astype(BF16)
        value = nn(normed, w_ref[:, 2 * width : 3 * width]).astype(BF16)
        v_ref[cut, :] = value
        v_t_ref[:, cut] = jnp.transpose(value)
    table = table_rows(misc, buckets, shards).astype(BF16)
    by_bucket = hot(iota((buckets, n), 0) == bucket_ref[...])
    line_ref[...] = tn(table, by_bucket)[TABLE_AT : TABLE_AT + 16]


def attend(q_ref, k_ref, v_t_ref, line_ref, twice_ref, merged_t_ref):
    n = q_ref.shape[0]
    half = iota((1, LANES), 1) < HEAD_DIM

    def pair(hp, carry):
        lanes = pl.ds(pl.multiple_of(hp * LANES, LANES), LANES)
        kp, qp = k_ref[:, lanes], q_ref[:, lanes]
        for side in range(2):
            toeplitz(line_ref[pl.ds(hp * 2 + side, 1), :], twice_ref)
            keys = kp * hot(half if side == 0 else ~half)
            at = pl.ds(pl.multiple_of(hp * LANES + side * HEAD_DIM, HEAD_DIM), HEAD_DIM)
            for block in range(n // QBLOCK):
                rows = (block + 1) * QBLOCK
                cols = slice(block * QBLOCK, rows)
                scores = nt(keys[:rows], qp[cols]) + bias_columns(twice_ref, n, block, rows)
                scores = causal(scores, block)
                top = jnp.max(scores, axis=0, keepdims=True)
                e = jnp.exp(scores - top)
                probs = (e * (1.0 / jnp.sum(e, axis=0, keepdims=True))).astype(BF16)
                merged_t_ref[at, cols] = nn(v_t_ref[at, :rows], probs).astype(BF16)
        return carry

    lax.fori_loop(0, HEADS // 2, pair, 0)


def route(experts, local, cap, here, tok_ref, w_ref, routes_ref, merged_t_ref, middle_ref, second_ref, gates_ref, slot_refs):
    n, width = tok_ref.shape
    misc = w_ref[:, 3 * width : 3 * width + LANES]
    gain = jnp.transpose(misc.astype(F32))[experts + 1 : experts + 2]
    for cut in chunked(n):
        middle = tok_ref[cut, :].astype(F32) + tn(merged_t_ref[:, cut], w_ref[:, 3 * width + LANES :])
        middle_ref[cut, :] = middle
        second = middle * lax.rsqrt(jnp.mean(middle * middle, axis=-1, keepdims=True) + EPSILON)
        second_ref[cut, :] = (second * gain).astype(BF16)
    c0, c1, oh0, oh1 = places_by_row(routes_ref[...], here, local, cap)
    logits = nn(second_ref[...], misc)
    p0 = jnp.sum(jnp.where(oh0, logits, 0.0), axis=1, keepdims=True)
    p1 = jnp.sum(jnp.where(oh1, logits, 0.0), axis=1, keepdims=True)
    top = jnp.maximum(p0, p1)
    e0, e1 = jnp.exp(p0 - top), jnp.exp(p1 - top)
    g0, g1 = e0 / (e0 + e1), e1 / (e0 + e1)
    wide = iota((n, LANES), 1)
    gates_ref[...] = jnp.where(wide == 0, g0, jnp.where(wide == 1, g1, 0.0))
    for at, slot_ref in enumerate(slot_refs):
        slot_ref[...] = jnp.zeros(slot_ref.shape, F32)
        for l in range(local):
            lane = iota((n, slot_ref.shape[1]), 1) + (at * local + l) * cap
            held = jnp.where(lane == c0, g0, jnp.where(lane == c1, g1, 0.0))
            slot_ref[l : l + 1, :] = jnp.sum(held, axis=0, keepdims=True)


def forward_kernel(
    experts, local, cap, buckets, shards,
    here_ref, tok_ref, w_ref, routes_ref, routes_t_ref, bucket_ref,
    q_ref, k_ref, v_ref, normed_t_ref, merged_t_ref, middle_ref, second_ref, gates_ref, line_ref,
    *rest,
):
    groups = experts // local
    x_refs, slot_refs = rest[:experts], rest[experts : experts + groups]
    v_t_ref, twice_ref = rest[experts + groups :]
    here = here_ref[0]
    project_inputs(experts, buckets, shards, tok_ref, w_ref, bucket_ref, q_ref, k_ref, v_ref, normed_t_ref, v_t_ref, line_ref)
    attend(q_ref, k_ref, v_t_ref, line_ref, twice_ref, merged_t_ref)
    route(experts, local, cap, here, tok_ref, w_ref, routes_ref, merged_t_ref, middle_ref, second_ref, gates_ref, slot_refs)
    d0, d1 = places_by_lane(routes_t_ref[...], here, experts, local, cap)
    for at, x_ref in enumerate(x_refs):
        x_ref[...] = put_rows(second_ref[...], d0, d1, at * cap, cap)


def gelu_both(v):
    t = pl.reciprocal(1.0 + (0.3275911 * 0.7071067811865476) * jnp.abs(v))
    e = jnp.exp(-0.5 * (v * v))
    poly = 0.5 * 1.061405429
    for coefficient in (-1.453152027, 1.421413741, -0.284496736, 0.254829592):
        poly = poly * t + 0.5 * coefficient
    tail = poly * t * e
    phi = jnp.where(v < 0.0, tail, 1.0 - tail)
    return v * phi, phi + v * e * 0.3989422804014327


def expert_kernel(local_at, groups, cap, *refs):
    take = iter(refs)
    rows_in, cots_in, slots_in, up_a, up_b, down_a, down_b = (next(take) for _ in range(7))
    reply_refs = [next(take) for _ in range(groups)]
    back_refs = [next(take) for _ in range(groups)]
    dot_refs = [next(take) for _ in range(groups)]
    ug_a, ug_b, dg_a, dg_b = (next(take) for _ in range(4))
    x_ref, xt_ref, cot_ref, gr_ref, reply_ref, back_ref = (next(take) for _ in range(6))
    up_buf, down_buf, ug_buf, dg_buf, act_ref, gh_ref = (next(take) for _ in range(6))
    in_sem, out_sem, row_sem = take
    rows, width = x_ref.shape
    slab = up_a.shape[3]
    block = up_buf.shape[2]
    per = block // slab
    half = up_a.shape[1] // per
    steps = 2 * half

    def fetches(up, down, at, slot):
        for i in range(per):
            cut = slice(i * slab, (i + 1) * slab)
            yield pltpu.make_async_copy(
                up.at[local_at, at * per + i], up_buf.at[slot, :, cut], in_sem.at[slot, i]
            )
            yield pltpu.make_async_copy(
                down.at[local_at, at * per + i], down_buf.at[slot, cut, :], in_sem.at[slot, per + i]
            )

    def stores(up, down, at, slot):
        for i in range(per):
            cut = slice(i * slab, (i + 1) * slab)
            yield pltpu.make_async_copy(
                ug_buf.at[slot, :, cut], up.at[at * per + i], out_sem.at[slot, i]
            )
            yield pltpu.make_async_copy(
                dg_buf.at[slot, cut, :], down.at[at * per + i], out_sem.at[slot, per + i]
            )

    def begin(kind, first, second, step, slot):
        @pl.when(step < half)
        def _():
            for copy in kind(*first, step, slot):
                copy.start()

        @pl.when(step >= half)
        def _():
            for copy in kind(*second, step - half, slot):
                copy.start()

    begin(fetches, (up_a, down_a), (up_b, down_b), 0, 0)
    copies = []
    for m in range(groups):
        cut = slice(m * cap, (m + 1) * cap)
        copies.append(pltpu.make_async_copy(rows_in.at[local_at, m], x_ref.at[cut, :], row_sem.at[0, m]))
        copies.append(pltpu.make_async_copy(cots_in.at[local_at, m], cot_ref.at[cut, :], row_sem.at[1, m]))
    for copy in copies:
        copy.start()
    for copy in copies:
        copy.wait()
    for m in range(groups):
        cut = slice(m * cap, (m + 1) * cap)
        slots = slots_in[m, local_at : local_at + 1, :]
        gate = jnp.transpose(jnp.broadcast_to(slots, (LANES, slots.shape[1])))[:cap, 0:1]
        gr_ref[cut, :] = (gate * cot_ref[cut, :].astype(F32)).astype(BF16)
    xt_ref[...] = jnp.transpose(x_ref[...])
    reply_ref[...] = jnp.zeros_like(reply_ref)
    back_ref[...] = jnp.zeros_like(back_ref)

    def step(at, carry):
        slot = lax.rem(at, 2)

        @pl.when(at + 1 < steps)
        def _():
            begin(fetches, (up_a, down_a), (up_b, down_b), at + 1, 1 - slot)

        for copy in fetches(up_a, down_a, 0, slot):
            copy.wait()

        @pl.when(at >= 2)
        def _():
            for copy in stores(ug_a, dg_a, 0, slot):
                copy.wait()

        chunk = 256
        for c in range(rows // chunk):
            cut = slice(c * chunk, (c + 1) * chunk)
            act, slope = gelu_both(nn(x_ref[cut, :], up_buf[slot]))
            act_ref[cut, :] = act.astype(BF16)
            grad = nt(gr_ref[cut, :], down_buf[slot])
            gh_ref[cut, :] = (grad * slope).astype(BF16)
            reply_ref[cut, :] += nn(act_ref[cut, :], down_buf[slot])
            back_ref[cut, :] += nt(gh_ref[cut, :], up_buf[slot])
        dg_buf[slot] = tn(act_ref[...], gr_ref[...]).astype(BF16)
        ug_buf[slot] = nn(xt_ref[...], gh_ref[...]).astype(BF16)
        begin(stores, (ug_a, dg_a), (ug_b, dg_b), at, slot)
        return carry

    lax.fori_loop(0, steps, step, 0)
    reply = reply_ref[...].astype(BF16)
    dots = jnp.sum(reply.astype(F32) * cot_ref[...].astype(F32), axis=1, keepdims=True)
    dots = jnp.transpose(jnp.broadcast_to(dots, (rows, LANES)))[0:8]
    for m in range(groups):
        cut = slice(m * cap, (m + 1) * cap)
        reply_refs[m][...] = reply[cut]
        back_refs[m][...] = back_ref[cut, :].astype(BF16)
        shifted = dots if m == 0 else pltpu.roll(dots, rows - m * cap, 1)
        dot_refs[m][...] = shifted[:, : dot_refs[m].shape[1]]
    for slot in range(2):
        for copy in stores(ug_a, dg_a, 0, slot):
            copy.wait()


def attend_back(after, q_ref, k_ref, v_ref, gm_ref, k_t_ref, line_ref, twice_ref, gq_t_ref, gk_ref, gv_ref, fold_ref):
    n = q_ref.shape[0]
    half = iota((1, LANES), 1) < HEAD_DIM

    def pair(hp, carry):
        lanes = pl.ds(pl.multiple_of(hp * LANES, LANES), LANES)
        kp, qp, vp, gp = k_ref[:, lanes], q_ref[:, lanes], v_ref[:, lanes], gm_ref[:, lanes]
        gk = [jnp.zeros((QBLOCK, LANES), F32) for _ in range(n // QBLOCK)]
        gv = [jnp.zeros((QBLOCK, LANES), F32) for _ in range(n // QBLOCK)]
        for side in range(2):
            toeplitz(line_ref[pl.ds(hp * 2 + side, 1), :], twice_ref)
            own = hot(half if side == 0 else ~half)
            keys, values, queries, outs = kp * own, vp * own, qp * own, gp * own
            at = pl.ds(pl.multiple_of(hp * LANES + side * HEAD_DIM, HEAD_DIM), HEAD_DIM)
            folded = jnp.zeros((LANES, n), F32)
            for block in range(n // QBLOCK):
                rows = (block + 1) * QBLOCK
                cols = slice(block * QBLOCK, rows)
                scores = nt(keys[:rows], qp[cols]) + bias_columns(twice_ref, n, block, rows)
                scores = causal(scores, block)
                top = jnp.max(scores, axis=0, keepdims=True)
                e = jnp.exp(scores - top)
                probs = e * (1.0 / jnp.sum(e, axis=0, keepdims=True))
                grad_probs = nt(values[:rows], gp[cols])
                total = jnp.sum(probs * grad_probs, axis=0, keepdims=True)
                gs = (probs * (grad_probs - total)).astype(BF16)
                low = probs.astype(BF16)
                gq_t_ref[at, cols] = (nn(k_t_ref[at, :rows], gs) * SCALE).astype(BF16)
                gk_part = nn(gs, queries[cols])
                gv_part = nn(low, outs[cols])
                for b in range(block + 1):
                    cut = slice(b * QBLOCK, (b + 1) * QBLOCK)
                    gk[b] += gk_part[cut]
                    gv[b] += gv_part[cut]
                wide = gs.astype(F32)
                for jb in range(rows // LANES):
                    piece = wide[jb * LANES : (jb + 1) * LANES]
                    parts = []
                    for lb in range(n // LANES):
                        src = (lb + jb) % (n // LANES) - block * (QBLOCK // LANES)
                        inside = 0 <= src < QBLOCK // LANES
                        parts.append(
                            piece[:, src * LANES : (src + 1) * LANES]
                            if inside
                            else jnp.zeros((LANES, LANES), F32)
                        )
                    folded += jnp.concatenate(parts, axis=1)
            size = LANES
            while size > 8:
                size //= 2
                folded = folded[:size] + pltpu.roll(folded[size : 2 * size], n - size, 1)
            fold_ref[hp * 2 + side] = folded
        for b in range(n // QBLOCK):
            cut = slice(b * QBLOCK, (b + 1) * QBLOCK)
            gk_ref[cut, lanes] = gk[b].astype(BF16)
            gv_ref[cut, lanes] = gv[b].astype(BF16)
        after(hp)
        return carry

    lax.fori_loop(0, HEADS // 2, pair, 0)


def middle_back(
    experts, local, cap, here, w_ref, routes_ref, cot_ref, middle_ref, second_ref, gates_ref, back_refs, dot_refs, gmid_ref, branch_ref
):
    n, width = cot_ref.shape
    misc = w_ref[:, 3 * width : 3 * width + LANES]
    gain = jnp.transpose(misc.astype(F32))[experts + 1 : experts + 2]
    c0_all, c1_all, oh0_all, oh1_all = places_by_row(routes_ref[...], here, local, cap)
    router_grad = jnp.zeros((width, LANES), F32)
    midnorm_grad = jnp.zeros((1, width), F32)
    for cut in chunked(n):
        c0, c1, oh0, oh1 = c0_all[cut], c1_all[cut], oh0_all[cut], oh1_all[cut]
        count = c0.shape[0]
        grad_second = jnp.zeros((count, width), F32)
        gg0 = jnp.zeros((count, 1), F32)
        gg1 = jnp.zeros((count, 1), F32)
        for at in range(experts):
            lane = iota((count, cap), 1) + at * cap
            h0, h1 = lane == c0, lane == c1
            grad_second += nn(hot(h0 | h1), back_refs[at][...])
            dots = dot_refs[at][0:1, :cap]
            gg0 += jnp.sum(jnp.where(h0, dots, 0.0), axis=1, keepdims=True)
            gg1 += jnp.sum(jnp.where(h1, dots, 0.0), axis=1, keepdims=True)
        g0, g1 = gates_ref[cut, 0:1], gates_ref[cut, 1:2]
        inner = g0 * gg0 + g1 * gg1
        grad_logits = jnp.where(oh0, g0 * (gg0 - inner), jnp.where(oh1, g1 * (gg1 - inner), 0.0))
        grad_logits = grad_logits.astype(BF16)
        grad_second += nt(grad_logits, misc)
        router_grad += tn(second_ref[cut, :], grad_logits)
        middle = middle_ref[cut, :]
        r = lax.rsqrt(jnp.mean(middle * middle, axis=-1, keepdims=True) + EPSILON)
        mr = middle * r
        midnorm_grad += jnp.sum(grad_second * mr, axis=0, keepdims=True)
        u = gain * grad_second
        gmid = cot_ref[cut, :].astype(F32) + r * (u - mr * jnp.mean(u * mr, axis=-1, keepdims=True))
        gmid_ref[cut, :] = gmid
        branch_ref[cut, :] = gmid.astype(BF16)
    return router_grad, midnorm_grad


def table_back(buckets, shards, width, bucket_ref, fold_ref):
    n = bucket_ref.shape[1]
    folded = fold_ref[...].reshape(HEADS * 8, n)
    row = iota((HEADS * 8, n), 0)
    for bit in (1, 2, 4):
        folded = jnp.where((row & bit) != 0, pltpu.roll(folded, n - bit, 1), folded)
    by_distance = jnp.sum(folded.reshape(HEADS, 8, n), axis=1)
    by_distance = jnp.concatenate([by_distance, jnp.zeros((16 - HEADS, n), F32)], axis=0)
    by_bucket = hot(iota((buckets, n), 0) == bucket_ref[...])
    table_grad = jnp.zeros((buckets, 16), F32)
    for _ in range(3):
        piece = by_distance.astype(BF16)
        table_grad += nt(by_bucket, piece)
        by_distance = by_distance - piece.astype(F32)
    spread = hot(iota((16, LANES), 1) == iota((16, LANES), 0) + TABLE_AT)
    table_grad = nn(table_grad.astype(BF16), spread).astype(BF16)
    rows, per = width // shards, buckets // shards
    b = iota((width, buckets), 1)
    select = hot(iota((width, buckets), 0) == lax.div(b, per) * rows + lax.rem(b, per))
    return nn(select, table_grad)


def inputs_back(experts, tok_ref, w_ref, gq_t_ref, gk_ref, gv_ref, gmid_ref, inputs_grad_ref):
    n, width = tok_ref.shape
    misc = w_ref[:, 3 * width : 3 * width + LANES]
    gain = jnp.transpose(misc.astype(F32))[experts : experts + 1]
    prenorm_grad = jnp.zeros((1, width), F32)
    for cut in chunked(n):
        grad_normed = nt(jnp.transpose(gq_t_ref[:, cut]), w_ref[:, :width])
        grad_normed += nt(gk_ref[cut, :], w_ref[:, width : 2 * width])
        grad_normed += nt(gv_ref[cut, :], w_ref[:, 2 * width : 3 * width])
        x = tok_ref[cut, :].astype(F32)
        q = lax.rsqrt(jnp.mean(x * x, axis=-1, keepdims=True) + EPSILON)
        xq = x * q
        prenorm_grad += jnp.sum(grad_normed * xq, axis=0, keepdims=True)
        w = gain * grad_normed
        back = q * (w - xq * jnp.mean(w * xq, axis=-1, keepdims=True))
        inputs_grad_ref[cut, :] = (gmid_ref[cut, :] + back).astype(BF16)
    return prenorm_grad


def small_grads(experts, router_grad, prenorm_grad, midnorm_grad, table):
    width = prenorm_grad.shape[1]
    tall = iota((LANES, width), 0)
    gains = jnp.where(tall == experts, prenorm_grad, jnp.where(tall == experts + 1, midnorm_grad, 0.0))
    return (router_grad + jnp.transpose(gains) + table).astype(BF16)


def backward_kernel(
    experts, local, cap, buckets, shards,
    here_ref, tok_ref, w_ref, routes_ref, bucket_ref, cot_ref, q_ref, k_ref, v_ref, normed_t_ref, merged_t_ref,
    middle_ref, second_ref, gates_ref, line_ref,
    *rest,
):
    take = iter(rest)
    back_refs = [next(take) for _ in range(experts)]
    dot_refs = [next(take) for _ in range(experts)]
    inputs_grad_ref, grads_ref = next(take), next(take)
    gm_ref, gmid_ref, k_t_ref, gq_t_ref, gk_ref, gv_ref, fold_ref, twice_ref, branch_ref = take
    width = tok_ref.shape[1]
    router_grad, midnorm_grad = middle_back(
        experts, local, cap, here_ref[0], w_ref, routes_ref, cot_ref, middle_ref, second_ref, gates_ref,
        back_refs, dot_refs, gmid_ref, branch_ref,
    )
    grads_ref[:, 3 * width + LANES :] = nn(merged_t_ref[...], branch_ref[...]).astype(BF16)
    gm_ref[...] = nt(branch_ref[...], w_ref[:, 3 * width + LANES :]).astype(BF16)
    k_t_ref[...] = jnp.transpose(k_ref[...])
    attend_back(
        lambda hp: None, q_ref, k_ref, v_ref, gm_ref, k_t_ref, line_ref, twice_ref, gq_t_ref, gk_ref, gv_ref, fold_ref
    )
    normed_t = normed_t_ref[...]
    grads_ref[:, :width] = nt(normed_t, gq_t_ref[...]).astype(BF16)
    grads_ref[:, width : 2 * width] = nn(normed_t, gk_ref[...]).astype(BF16)
    grads_ref[:, 2 * width : 3 * width] = nn(normed_t, gv_ref[...]).astype(BF16)
    prenorm_grad = inputs_back(experts, tok_ref, w_ref, gq_t_ref, gk_ref, gv_ref, gmid_ref, inputs_grad_ref)
    table = table_back(buckets, shards, width, bucket_ref, fold_ref)
    grads_ref[:, 3 * width : 3 * width + LANES] = small_grads(experts, router_grad, prenorm_grad, midnorm_grad, table)


def combine(local, cap, here, routes_ref, gates_ref, middle_ref, reply_refs, out_ref):
    n, width = middle_ref.shape
    c0, c1, _, _ = places_by_row(routes_ref[...], here, local, cap)
    for cut in chunked(n):
        picked0 = jnp.zeros((cut.stop - cut.start, width), F32)
        picked1 = jnp.zeros((cut.stop - cut.start, width), F32)
        for at, reply_ref in enumerate(reply_refs):
            lane = iota((cut.stop - cut.start, cap), 1) + at * cap
            picked0 += nn(hot(lane == c0[cut]), reply_ref[...])
            picked1 += nn(hot(lane == c1[cut]), reply_ref[...])
        out = middle_ref[cut, :] + gates_ref[cut, 0:1] * picked0 + gates_ref[cut, 1:2] * picked1
        out_ref[cut, :] = out.astype(BF16)


def combine_kernel(local, cap, here_ref, routes_ref, gates_ref, middle_ref, *rest):
    *reply_refs, out_ref = rest
    combine(local, cap, here_ref[0], routes_ref, gates_ref, middle_ref, reply_refs, out_ref)


class View:
    def __init__(self, ref, index=None):
        self.ref, self.index = ref, index

    def __getitem__(self, index):
        return View(self.ref, index)

    def cut(self):
        return self.ref if self.index is None else self.ref.at[self.index]


class Window:
    def __init__(self, ref, lead, shape):
        self.ref, self.lead, self.shape = ref, lead, shape

    def whole(self, index):
        index = () if index is Ellipsis else index if isinstance(index, tuple) else (index,)
        index += (slice(None),) * (len(self.shape) - len(index))
        limited = [slice(0, size) if i == slice(None) else i for i, size in zip(index, self.shape)]
        return (*self.lead, *limited)

    def __getitem__(self, index):
        return self.ref[self.whole(index)]

    def __setitem__(self, index, value):
        self.ref[self.whole(index)] = value

    def view(self, *index):
        return View(self.ref, self.whole(index))


class Remote:
    def __init__(self, *args):
        self.args = args

    def make(self):
        src, dst, sends, receives, at, axis, peer = self.args
        return pltpu.make_async_remote_copy(
            src_ref=src.cut(),
            dst_ref=dst.cut(),
            send_sem=sends.at[at],
            recv_sem=receives.at[at],
            device_id={axis: peer},
            device_id_type=MESH,
        )

    def start(self):
        self.make().start()

    def wait_send(self):
        self.make().wait_send()

    def wait_recv(self):
        self.make().wait_recv()

    def wait(self):
        self.wait_send()
        self.wait_recv()


class Local:
    def __init__(self, *args):
        self.args = args

    def make(self):
        src, dst, sems, at = self.args
        return pltpu.make_async_copy(src.cut(), dst.cut(), sems.at[at])

    def wait(self):
        self.make().wait()


class Links:
    def __init__(self, send_sem, recv_sem, local_sem):
        self.send_sem, self.recv_sem, self.local_sem = send_sem, recv_sem, local_sem
        self.sent = self.moved = 0
        self.open_sends = []

    def send(self, src, dst, axis, peer):
        copy = Remote(src, dst, self.send_sem, self.recv_sem, self.sent, axis, peer)
        self.sent += 1
        copy.start()
        self.open_sends.append(copy)
        return copy

    def move(self, src, dst):
        copy = Local(src, dst, self.local_sem, self.moved)
        self.moved += 1
        copy.make().start()
        return copy

    def forget(self, copies):
        self.open_sends = [other for other in self.open_sends if all(copy is not other for copy in copies)]

    def close(self):
        for copy in self.open_sends:
            copy.wait_send()


SENDS, MOVES = 144, 22


def layer_kernel(experts, local, cap, buckets, shards, names, *refs):
    r = SimpleNamespace(**dict(zip(names, refs, strict=True)))
    groups = experts // local
    me, here = lax.axis_index(DP), lax.axis_index(EXPERT)
    tok_ref, cot_ref, w_ref, routes_ref, bucket_ref = r.tok, r.cot, r.w, r.routes_by_row, r.bucket
    n, width = tok_ref.shape
    rows = r.wq.shape[0]
    slab = r.up.shape[2]
    across, along, core, diagonal = me ^ 2, me ^ 4, me ^ 1, me ^ 6
    barrier = pltpu.get_barrier_semaphore()
    for peer in (across, along, core):
        pl.semaphore_signal(barrier, inc=1, device_id={DP: peer}, device_id_type=MESH)
    for m in range(1, groups):
        pl.semaphore_signal(barrier, inc=1, device_id={EXPERT: here ^ m}, device_id_type=MESH)
    pl.semaphore_wait(barrier, 3 + groups - 1)
    links = Links(r.send_sem, r.recv_sem, r.local_sem)
    send, move = links.send, links.move

    def rows_of(owner, start=0, count=rows):
        return pl.ds(pl.multiple_of(owner * rows + start, 16), count)

    first = 3 * width + LANES
    parts = (slice(0, first), slice(first, first + width))
    mine = rows_of(me)
    w_ref[mine, 0:width] = r.wq[...]
    w_ref[mine, width : 2 * width] = r.wk[...]
    w_ref[mine, 2 * width : 3 * width] = r.wv[...]
    r.columns[...] = jnp.zeros_like(r.columns)
    r.columns[0:experts, 0:rows] = r.router_t[...].astype(F32)
    r.columns[experts : experts + 1, 0:rows] = r.gain_one[...].astype(F32)
    r.columns[experts + 1 : experts + 2, 0:rows] = r.gain_two[...].astype(F32)
    own_rows = jnp.transpose(r.columns[...])[:rows]
    r.columns[...] = jnp.zeros_like(r.columns)
    r.columns[0 : r.table.shape[0], 0:HEADS] = r.table[...].astype(F32)
    w_ref[mine, 3 * width : first] = (own_rows + pltpu.roll(r.columns[...], TABLE_AT, 1)[:rows]).astype(BF16)
    w_ref[mine, first:] = r.wo[...]

    def w_copy(part, owner, peer, start=0, count=rows):
        view = View(w_ref)[rows_of(owner, start, count), parts[part]]
        return send(view, view, DP, peer)

    w_own = [[w_copy(part, me, peer) for peer in (across, along, core)] for part in range(2)]

    d0, d1 = places_by_lane(r.routes_t[...], here, experts, local, cap)
    tall = iota((LANES, n), 0)
    named = jnp.where(tall == 0, r.routes_t[0:1, :], jnp.where(tall == 1, r.routes_t[1:2, :], 0))
    routes_ref[...] = jnp.transpose(named.astype(F32)).astype(I32)

    z_peers = [here ^ m for m in range(groups)]
    far_first = (2, 3, 1)

    def dispatch(l, values, out_ref, in_ref):
        for m in (*far_first, 0):
            cut = slice(m * cap, (m + 1) * cap)
            target = out_ref if m else in_ref
            target[l, cut, :] = put_rows(values, d0, d1, (m * local + l) * cap, cap)

    def z_send_rows(l, m, out_ref, in_ref):
        cut = slice(m * cap, (m + 1) * cap)
        return send(View(out_ref)[l, cut, :], View(in_ref)[l, cut, :], EXPERT, z_peers[m])

    cot_copies, row_copies = {}, {}
    for l in range(local):
        dispatch(l, cot_ref[...], r.out_a, r.cots)
        for m in far_first:
            if (l, m) != (local - 1, 3):
                cot_copies[l, m] = z_send_rows(l, m, r.out_a, r.cots)
    half = rows // 2
    w_passed = []
    for part in range(2):
        w_own[part][0].wait_recv()
        one = w_copy(part, across, along, 0, half)
        two = w_copy(part, across, core)
        w_own[part][1].wait_recv()
        three = w_copy(part, along, across, half, half)
        four = w_copy(part, along, core)
        w_passed.append((one, three, two, four))

    kinds = ((UP, r.up, r.up_a, r.up_b), (DOWN, r.down, r.down_a, r.down_b))
    weight_copies = {}

    def weights_out(l):
        for kind, own_ref, a_ref, b_ref in kinds:
            key = (l, kind)
            weight_copies[key, OWN] = move(View(own_ref)[l], View(a_ref)[l, 0])
            weight_copies[key, (A, 1)] = send(View(own_ref)[l], View(a_ref)[l, 1], DP, across)
            weight_copies[key, (A, 2)] = send(View(own_ref)[l], View(a_ref)[l, 2], DP, along)
            weight_copies[key, (B, 0)] = send(View(own_ref)[l], View(b_ref)[l, 0], DP, core)

    def weights_on(l):
        for kind, own_ref, a_ref, b_ref in kinds:
            key = (l, kind)
            at, peer = (1, along) if kind == UP else (2, across)
            weight_copies[key, (A, at)].wait_recv()
            weight_copies[key, (A, 3)] = send(View(a_ref)[l, at], View(a_ref)[l, 3], DP, peer)
            weight_copies[key, (B, at)] = send(View(a_ref)[l, at], View(b_ref)[l, at], DP, core)
        for kind, own_ref, a_ref, b_ref in kinds:
            key = (l, kind)
            at = 2 if kind == UP else 1
            weight_copies[key, (A, at)].wait_recv()
            weight_copies[key, (B, at)] = send(View(a_ref)[l, at], View(b_ref)[l, at], DP, core)

    def weights_last(l):
        for kind, own_ref, a_ref, b_ref in kinds:
            key = (l, kind)
            weight_copies[key, (A, 3)].wait_recv()
            weight_copies[key, (B, 3)] = send(View(a_ref)[l, 3], View(b_ref)[l, 3], DP, core)

    def weights_in(l):
        for kind, *_ in kinds:
            weight_copies[(l, kind), OWN].wait()
            for at in range(4):
                weight_copies[(l, kind), (B, at)].wait_recv()

    weights_out(0)
    v_t_ref = Window(r.gh, (), (width, n))

    def w_finish(part):
        one, three, two, four = w_passed[part]
        one.wait_recv()
        three.wait_recv()
        five = w_copy(part, diagonal, core)
        for copy in (w_own[part][2], two, four, five):
            copy.wait_recv()

    w_finish(0)

    project_inputs(
        experts, buckets, shards, tok_ref, w_ref, bucket_ref, r.q, r.k, r.v, r.normed_t, v_t_ref, r.line
    )
    attend(r.q, r.k, v_t_ref, r.line, r.twice, r.merged_t)
    w_finish(1)
    slots_out, slots_in = r.slots_out, r.slots_in
    route(
        experts, local, cap, here, tok_ref, w_ref, routes_ref, r.merged_t, r.middle, r.second, r.gates,
        [slots_out.at[m] for m in range(groups)],
    )
    slot_copies = [send(View(slots_out)[m], View(slots_in)[m], EXPERT, here ^ m) for m in range(1, groups)]
    slots_in[0] = slots_out[0]
    for l in range(local):
        dispatch(l, r.second[...], r.out_b, r.rows)
        if l == 0:
            for m in far_first:
                row_copies[l, m] = z_send_rows(l, m, r.out_b, r.rows)
    weights_on(0)
    weights_out(1)
    weights_last(0)
    for m in far_first:
        row_copies[0, m].wait_send()
    cot_copies[1, 3] = z_send_rows(1, 3, r.out_a, r.cots)
    for m in far_first:
        row_copies[1, m] = z_send_rows(1, m, r.out_b, r.rows)
    weights_in(0)
    for m in far_first:
        cot_copies[0, m].wait_recv()
        row_copies[0, m].wait_recv()
    for copy in slot_copies:
        copy.wait_recv()

    up_buf, down_buf, ug_buf, dg_buf, core_buf = r.up_buf, r.down_buf, r.ug_buf, r.dg_buf, r.core_buf
    gr_ref, act_ref, gh_ref, reply_ref, back_ref = r.gr, r.act, r.gh, r.reply, r.back
    total_rows = groups * cap
    core_sems, hop_sems = (r.core_send, r.core_recv), (r.hop_send, r.hop_recv)
    back_sems = (r.back_send, r.back_recv)
    halves = [slice(i * slab, (i + 1) * slab) for i in range(2)]

    def remote(src, dst, sems, at, axis, peer):
        return pltpu.make_async_remote_copy(
            src_ref=src, dst_ref=dst, send_sem=sems[0].at[at], recv_sem=sems[1].at[at],
            device_id={axis: peer}, device_id_type=MESH,
        )

    def fetches(l, g, a_side, wait=False):
        for i in range(2):
            at = i if wait else 2 * (3 - g) + i if a_side else 2 * g + i
            up, down = (r.up_a, r.down_a) if a_side else (r.up_b, r.down_b)
            slot = lax.rem(g, 2)
            yield pltpu.make_async_copy(up.at[l, at], up_buf.at[slot, :, halves[i]], r.fetch_sem.at[slot, i])
            yield pltpu.make_async_copy(down.at[l, at], down_buf.at[slot, halves[i], :], r.fetch_sem.at[slot, 2 + i])

    def fetch(l, g):
        for a_side in (False, True):

            @pl.when((g >= 2) == a_side)
            def _():
                for copy in fetches(l, g, a_side):
                    copy.start()

    def core_copies(l, slab_at, i, out):
        at = (l * 4 + slab_at) * 2
        yield remote(ug_buf.at[out, :, halves[i]], r.core_up.at[l, slab_at], core_sems, at, DP, core)
        yield remote(dg_buf.at[out, halves[i], :], r.core_down.at[l, slab_at], core_sems, at + 1, DP, core)

    def t_copy(l, kind, i, out, half_at):
        at = l * 4 + (0 if kind == UP else 2) + i
        if kind == UP:
            return remote(ug_buf.at[out, :, halves[half_at]], r.t_up.at[l, i], hop_sems, at, DP, along)
        return remote(dg_buf.at[out, halves[half_at], :], r.t_down.at[l, i], hop_sems, at, DP, across)

    def own_moves(l, out):
        yield pltpu.make_async_copy(ug_buf.at[out, :, halves[0]], r.own_up.at[l], r.own_sem.at[0])
        yield pltpu.make_async_copy(dg_buf.at[out, halves[0], :], r.own_down.at[l], r.own_sem.at[1])

    def kept_move(l, kind, out):
        if kind == UP:
            return pltpu.make_async_copy(ug_buf.at[out, :, halves[1]], r.keep_up.at[l], r.own_sem.at[2])
        return pltpu.make_async_copy(dg_buf.at[out, halves[0], :], r.keep_down.at[l], r.own_sem.at[3])

    def sent_from(l, g, out):
        def when(condition):
            return (lambda f: f() if condition else None) if isinstance(g, int) else pl.when(condition)

        @when(g < 2)
        def _():
            for i in range(2):
                for copy in core_copies(l, 2 * g + i, i, out):
                    copy.wait_send()

        @when(g == 2)
        def _():
            for copy in (t_copy(l, UP, 0, out, 0), t_copy(l, UP, 1, out, 1), t_copy(l, DOWN, 1, out, 1)):
                copy.wait_send()
            kept_move(l, DOWN, out).wait()

        @when(g == 3)
        def _():
            t_copy(l, DOWN, 0, out, 1).wait_send()
            for copy in (*own_moves(l, out), kept_move(l, UP, out)):
                copy.wait()

    def back_copy(l, m):
        cut = slice(m * cap, (m + 1) * cap)
        at = l * (groups - 1) + m - 1
        return remote(r.out_a.at[l, cut, :], r.backs.at[l, cut, :], back_sems, at, EXPERT, here ^ m)

    def dot_copy(l, m):
        at = (local + l) * (groups - 1) + m - 1
        return remote(r.dots_out.at[l, m], r.dots_in.at[l, m], back_sems, at, EXPERT, here ^ m)

    reply_copies = []

    def reply_send(l, m):
        reply_copies.append(z_send_rows(l, m, r.out_b, r.reply_in))

    def step(s, carry):
        l, g, out = lax.div(s, 4), lax.rem(s, 4), lax.rem(s, 3)
        slot = lax.rem(g, 2)
        x, cots = r.rows.at[l], r.cots.at[l]

        @pl.when(s == 1)
        def _():
            weights_on(1)

        @pl.when(s == 3)
        def _():
            weights_last(1)

        @pl.when(s == 4)
        def _():
            weights_in(1)
            for m in far_first:
                cot_copies[1, m].wait_recv()
                row_copies[1, m].wait_recv()

        @pl.when(s == 6)
        def _():
            for m in far_first:
                back_copy(0, m).wait_send()
            for m in (2, 1):
                reply_send(0, m)

        @pl.when(g == 0)
        def _():
            fetch(l, g)
            for m in range(groups):
                cut = slice(m * cap, (m + 1) * cap)
                slots = slots_in[m, pl.ds(l, 1), :]
                gate = jnp.transpose(jnp.broadcast_to(slots, (LANES, slots.shape[1])))[:cap, 0:1]
                gr_ref[cut, :] = (gate * cots[cut, :].astype(F32)).astype(BF16)
            core_buf[...] = jnp.zeros_like(core_buf)
            reply_ref[...] = jnp.zeros_like(reply_ref)
            back_ref[...] = jnp.zeros_like(back_ref)

        for copy in fetches(l, g, False, True):
            copy.wait()

        @pl.when(g < 3)
        def _():
            fetch(l, g + 1)

        def arrivals():
            for i in range(2):
                at = 2 * (3 - g) + i
                yield pltpu.make_async_copy(r.core_up.at[l, at], core_buf.at[0, :, halves[i]], r.add_sem.at[i])
                yield pltpu.make_async_copy(r.core_down.at[l, at], core_buf.at[1, halves[i], :], r.add_sem.at[2 + i])

        @pl.when(g >= 2)
        def _():
            for i in range(2):
                for copy in core_copies(l, 2 * (3 - g) + i, i, out):
                    copy.wait_recv()
            for copy in arrivals():
                copy.start()

        for cut in chunked(total_rows):
            act, slope = gelu_both(nn(x[cut, :], up_buf[slot]))
            act_ref[cut, :] = act.astype(BF16)
            gh_ref[cut, :] = (nt(gr_ref[cut, :], down_buf[slot]) * slope).astype(BF16)
            reply_ref[cut, :] += nn(act_ref[cut, :], down_buf[slot])
            back_ref[cut, :] += nt(gh_ref[cut, :], up_buf[slot])

        @pl.when(s >= 3)
        def _():
            sent_from(lax.div(s - 3, 4), lax.rem(s - 3, 4), out)

        @pl.when(g >= 2)
        def _():
            for copy in arrivals():
                copy.wait()

        for cut in chunked(width):
            ug = tn(x[:, cut], gh_ref[...]) + core_buf[0, cut, :].astype(F32)
            ug_buf[out, cut, :] = ug.astype(BF16)
            dg = tn(act_ref[:, cut], gr_ref[...]) + core_buf[1, cut, :].astype(F32)
            dg_buf[out, cut, :] = dg.astype(BF16)

        @pl.when(g < 2)
        def _():
            for i in range(2):
                for copy in core_copies(l, 2 * g + i, i, out):
                    copy.start()

        @pl.when(g == 2)
        def _():
            t_copy(l, UP, 0, out, 0).start()
            t_copy(l, UP, 1, out, 1).start()
            t_copy(l, DOWN, 1, out, 1).start()
            kept_move(l, DOWN, out).start()

        @pl.when(g == 3)
        def _():
            t_copy(l, DOWN, 0, out, 1).start()
            for copy in own_moves(l, out):
                copy.start()
            kept_move(l, UP, out).start()
            for which in range(local):

                @pl.when(l == which)
                def _():
                    for m in far_first:
                        cot_copies[which, m].wait_send()
                        if which:
                            row_copies[which, m].wait_send()

            for m in range(groups):
                cut = slice(m * cap, (m + 1) * cap)
                if m == 0:
                    r.backs[l, cut, :] = back_ref[cut, :].astype(BF16)
                else:
                    r.out_a[l, cut, :] = back_ref[cut, :].astype(BF16)
                    back_copy(l, m).start()
            reply = reply_ref[...].astype(BF16)
            r.out_b[l] = reply
            dots = jnp.sum(reply.astype(F32) * cots[...].astype(F32), axis=1, keepdims=True)
            dots = jnp.transpose(jnp.broadcast_to(dots, (total_rows, LANES)))[0:8]
            r.dots_in[l, 0] = dots[:, :256]
            for m in range(1, groups):
                r.dots_out[l, m] = pltpu.roll(dots, total_rows - m * cap, 1)[:, :256]
                dot_copy(l, m).start()

        return carry

    lax.fori_loop(0, 4 * local, step, 0)
    links.forget([*cot_copies.values(), *row_copies.values()])
    v_copies = {}

    def t_stage(l):
        t_copy(l, UP, 1, 0, 1).wait_recv()
        t_copy(l, DOWN, 1, 0, 1).wait_recv()
        return [
            move(View(r.t_up)[l, 1], View(up_buf)[l, :, :slab]),
            move(View(r.t_down)[l, 1], View(down_buf)[l, :slab, :]),
            move(View(r.keep_up)[l], View(up_buf)[l, :, slab:]),
            move(View(r.keep_down)[l], View(down_buf)[l, slab:, :]),
        ]

    def t_pass(l, staged):
        for copy in staged:
            copy.wait()
        up_sum = up_buf[l, :, slab:].astype(F32) + up_buf[l, :, :slab].astype(F32)
        up_buf[l, :, :slab] = up_sum.astype(BF16)
        v_copies[l, UP] = send(View(up_buf)[l, :, :slab], View(r.v_up)[l], DP, across)
        down_sum = down_buf[l, slab:, :].astype(F32) + down_buf[l, :slab, :].astype(F32)
        down_buf[l, :slab, :] = down_sum.astype(BF16)
        v_copies[l, DOWN] = send(View(down_buf)[l, :slab, :], View(r.v_down)[l], DP, along)

    t_pass(0, t_stage(0))

    for l in range(local):
        for m in range(1, groups):
            back_copy(l, m).wait_recv()
            if l:
                back_copy(l, m).wait_send()
            dot_copy(l, m).wait()
    for l, m in ((0, 3), (1, 2), (1, 3), (1, 1)):
        reply_send(l, m)
    order = [(m, l) for m in range(groups) for l in range(local)]
    gm_ref, gk_ref = Window(r.rows, (0,), (n, width)), Window(r.rows, (1,), (n, width))
    gv_ref, k_t_ref = Window(r.cots, (0,), (n, width)), v_t_ref
    gq_t_ref, gmid_ref = Window(gr_ref, (), (width, n)), Window(reply_ref, (), (n, width))
    branch_ref, normed_t = Window(act_ref, (), (n, width)), r.normed_t
    router_grad, midnorm_grad = middle_back(
        experts, local, cap, here, w_ref, routes_ref, cot_ref, r.middle, r.second, r.gates,
        [Window(r.backs.at[l, m * cap : (m + 1) * cap, :], (), (cap, width)) for m, l in order],
        [r.dots_in.at[l, m] for m, l in order],
        gmid_ref, branch_ref,
    )
    r.gain_row[0:1, :] = midnorm_grad
    r.router_grad[...] = router_grad
    part = width // 2
    chunk_at = (2, 0)
    for at in range(4 * local - 3, 4 * local):
        sent_from(at // 4, at % 4, at % 3)
    for c in range(2):
        for cut in chunked(width):
            project = nn(r.merged_t[cut, :], branch_ref[:, c * part : (c + 1) * part])
            dg_buf[chunk_at[c], cut, part:] = project.astype(BF16)
    for cut in chunked(n):
        gm_ref[cut, :] = nt(branch_ref[cut, :], w_ref[:, first:]).astype(BF16)
    k_t_ref[...] = jnp.transpose(r.k[...])

    def weight_grads(c):
        at, columns = chunk_at[c], slice(c * part, (c + 1) * part)
        for cut in chunked(width):
            ug_buf[at, cut, :part] = nt(normed_t[cut, :], gq_t_ref[columns, :]).astype(BF16)
            ug_buf[at, cut, part:] = nn(normed_t[cut, :], gk_ref[:, columns]).astype(BF16)
            dg_buf[at, cut, :part] = nn(normed_t[cut, :], gv_ref[:, columns]).astype(BF16)

    peers = [me ^ mask for mask in range(8)]
    rows_at = [rows_of(peer) for peer in peers]

    class Reduce:
        def __init__(self, pieces):
            self.pieces = pieces

        def start(self):
            self.zero = []
            for g, from_core, *_ in self.pieces:
                for i in (2, 3, 1, 0):
                    copy = send(g.view(rows_at[1 ^ (2 * i)]), from_core.view(i), DP, peers[1])
                    self.zero.append((i, g, from_core, copy))

        def one(self):
            for i, g, from_core, copy in self.zero:
                copy.wait_recv()
                at = rows_at[2 * i]
                g[at, :] = (g[at, :].astype(F32) + from_core[i].astype(F32)).astype(BF16)
            self.hops = []
            for g, _, hop_one, _, mask in self.pieces:
                for i, owner in enumerate((mask, 6)):
                    self.hops.append(send(g.view(rows_at[owner]), hop_one.view(i), DP, peers[mask]))

        def two(self):
            for copy in self.hops:
                copy.wait_recv()
            self.last = []
            for g, _, hop_one, hop_two, mask in self.pieces:
                at = rows_at[6 - mask]
                g[at, :] = (g[at, :].astype(F32) + hop_one[1].astype(F32)).astype(BF16)
                self.last.append(send(g.view(at), hop_two.view(), DP, peers[6 - mask]))

        def three(self):
            for copy in self.last:
                copy.wait_recv()
            return [
                g[rows_at[0], :].astype(F32) + hop_one[0].astype(F32) + hop_two[...].astype(F32)
                for g, _, hop_one, hop_two, _ in self.pieces
            ]

    def window(ref, *lead):
        return Window(ref, lead, ref.shape[len(lead) :])

    chunks = [
        Reduce(
            [
                (window(ug_buf, chunk_at[c]), window(r.core_a, c), window(r.hop_a, c), window(r.last_a, c), 4),
                (window(dg_buf, chunk_at[c]), window(r.core_b, c), window(r.hop_b, c), window(r.last_b, c), 2),
            ]
        )
        for c in range(2)
    ]
    little = Reduce([(window(r.little), window(r.core_c), window(r.hop_c), window(r.last_c), 4)])
    z_copies, g_copies = {}, {}
    share = pl.ds(pl.multiple_of(here * part, LANES), part)

    def z_send(c):
        a, b = chunks[c].three()
        r.sum[c, :, :width] = a.astype(BF16)
        r.sum[c, :, width:] = b.astype(BF16)
        z_copies[c] = []
        for m in range(1, groups):
            cut = pl.ds(pl.multiple_of((here ^ m) * part, LANES), part)
            z_copies[c].append(send(View(r.sum)[c, :, cut], View(r.z_in)[c, m], EXPERT, here ^ m))

    def z_gather(c):
        total = r.sum[c, :, share].astype(F32)
        for m in range(1, groups):
            z_copies[c][m - 1].wait_recv()
            total += r.z_in[c, m].astype(F32)
        r.z_sum[c] = total.astype(BF16)
        g_copies[c] = [
            send(View(r.z_sum)[c], View(r.z_all)[c, m], EXPERT, here ^ m) for m in range(1, groups)
        ]
        r.main[here, :, c * part : (c + 1) * part] = r.z_sum[c]

    def z_finish(c):
        for m in range(1, groups):
            g_copies[c][m - 1].wait_recv()
            r.main[here ^ m, :, c * part : (c + 1) * part] = r.z_all[c, m]

    def after(hp):
        @pl.when(hp == 2)
        def _():
            weight_grads(0)
            chunks[0].start()

        @pl.when(hp == 3)
        def _():
            chunks[0].one()
            t_pass(1, t_stage(1))

        @pl.when(hp == 4)
        def _():
            chunks[0].two()

    attend_back(after, r.q, r.k, r.v, gm_ref, k_t_ref, r.line, r.twice, gq_t_ref, gk_ref, gv_ref, r.fold)
    weight_grads(1)
    chunks[1].start()
    z_send(0)
    prenorm_grad = inputs_back(experts, tok_ref, w_ref, gq_t_ref, gk_ref, gv_ref, gmid_ref, gm_ref)
    results = [move(gm_ref.view(), View(r.inputs_grad))]
    chunks[1].one()
    z_gather(0)
    table = table_back(buckets, shards, width, bucket_ref, r.fold)
    r.little[...] = small_grads(
        experts, r.router_grad[...], prenorm_grad, r.gain_row[0:1, :], table
    )
    little.start()
    chunks[1].two()
    little.one()
    z_finish(0)
    for copy in reply_copies:
        copy.wait_recv()
    staged = [move(View(r.reply_in)[l, cap:, :], View(core_buf)[l, cap:, :]) for l in range(local)]
    z_send(1)
    little.two()
    for l, copy in enumerate(staged):
        core_buf[l, :cap, :] = r.out_b[l, :cap, :]
        copy.wait()
    layer_out_ref = Window(r.cots, (1,), (n, width))
    combine(
        local, cap, here, routes_ref, r.gates, r.middle,
        [core_buf.at[l, m * cap : (m + 1) * cap, :] for m, l in order], layer_out_ref,
    )
    results.append(move(layer_out_ref.view(), View(r.layer_out)))
    z_gather(1)
    (small_sum,) = little.three()
    r.small_z[here] = small_sum.astype(BF16)
    small_copies = [
        send(View(r.small_z)[here], View(r.small_z)[here], EXPERT, here ^ m) for m in range(1, groups)
    ]
    z_finish(1)
    for copy in small_copies:
        copy.wait_recv()
    total = r.small_z[0].astype(F32)
    for m in range(1, groups):
        total += r.small_z[m].astype(F32)
    r.small_out[...] = total
    for l in range(local):
        for kind in (UP, DOWN):
            t_copy(l, kind, 0, 0, 0).wait_recv()
            v_copies[l, kind].wait_recv()
    for copy in results:
        copy.wait()
    links.close()


def whole_layer(
    tokens, query_weight, key_weight, value_weight, project_weight, router_weight, prenorm_gain, midnorm_gain, bias_table,
    up_weight, down_weight, routes, bucket_row, cotangent,
):
    experts, table_rows_own = router_weight.shape[1], bias_table.shape[0]
    n, width = tokens.shape
    shards, groups = lax.axis_size(DP), lax.axis_size(EXPERT)
    local, _, slab = up_weight.shape
    buckets = table_rows_own * shards
    cap = 3 * n // experts
    rows = query_weight.shape[0]
    total = groups * cap
    vmem, hbm = pl.BlockSpec(memory_space=pltpu.VMEM), pl.BlockSpec(memory_space=pl.ANY)

    def array(*s, dtype=BF16):
        return jax.ShapeDtypeStruct(s, dtype)

    inputs = dict(
        tok=tokens, wq=query_weight, wk=key_weight, wv=value_weight, wo=project_weight,
        router_t=router_weight.T, gain_one=prenorm_gain[None, :], gain_two=midnorm_gain[None, :], table=bias_table,
        routes_t=routes.T, bucket=bucket_row, cot=cotangent, up=up_weight, down=down_weight,
    )
    near = dict(
        main=array(4, rows, width),
        small_out=array(rows, LANES, dtype=F32),
    )
    far = dict(
        layer_out=array(n, width),
        inputs_grad=array(n, width),
        own_up=array(local, width, slab),
        own_down=array(local, slab, width),
        keep_up=array(local, width, slab),
        keep_down=array(local, slab, width),
        t_up=array(local, 2, width, slab),
        t_down=array(local, 2, slab, width),
        v_up=array(local, width, slab),
        v_down=array(local, slab, width),
        up_a=array(local, 4, width, slab),
        up_b=array(local, 4, width, slab),
        down_a=array(local, 4, slab, width),
        down_b=array(local, 4, slab, width),
        core_up=array(local, 4, width, slab),
        core_down=array(local, 4, slab, width),
        reply_in=array(local, total, width),
    )
    v, part = pltpu.VMEM, width // 2
    scratch = dict(
        w=v((width, 4 * width + LANES), BF16),
        out_a=v((local, total, width), BF16),
        out_b=v((local, total, width), BF16),
        rows=v((local, total, width), BF16),
        cots=v((local, total, width), BF16),
        backs=v((local, total, width), BF16),
        slots_out=v((groups, 8, 256), F32),
        slots_in=v((groups, 8, 256), F32),
        dots_out=v((local, groups, 8, 256), F32),
        dots_in=v((local, groups, 8, 256), F32),
        q=v((n, width), BF16),
        k=v((n, width), BF16),
        v=v((n, width), BF16),
        normed_t=v((width, n), BF16),
        second=v((n, width), BF16),
        merged_t=v((width, n), BF16),
        middle=v((n, width), F32),
        gates=v((n, LANES), F32),
        routes_by_row=v((n, LANES), I32),
        columns=v((LANES, LANES), F32),
        line=v((16, n), F32),
        twice=v((LANES, 2 * n), F32),
        fold=v((HEADS, 8, n), F32),
        gr=v((total, width), BF16),
        act=v((total, width), BF16),
        gh=v((total, width), BF16),
        reply=v((total, width), F32),
        back=v((total, width), F32),
        up_buf=v((2, width, width), BF16),
        down_buf=v((2, width, width), BF16),
        ug_buf=v((3, width, width), BF16),
        dg_buf=v((3, width, width), BF16),
        core_buf=v((2, width, width), BF16),
        core_a=v((2, 4, rows, width), BF16),
        core_b=v((2, 4, rows, width), BF16),
        hop_a=v((2, 2, rows, width), BF16),
        hop_b=v((2, 2, rows, width), BF16),
        last_a=v((2, rows, width), BF16),
        last_b=v((2, rows, width), BF16),
        sum=v((2, rows, 2 * width), BF16),
        z_in=v((2, groups, rows, part), BF16),
        z_sum=v((2, rows, part), BF16),
        z_all=v((2, groups, rows, part), BF16),
        little=v((width, LANES), BF16),
        gain_row=v((8, width), F32),
        router_grad=v((width, LANES), F32),
        core_c=v((4, rows, LANES), BF16),
        hop_c=v((2, rows, LANES), BF16),
        last_c=v((rows, LANES), BF16),
        small_z=v((groups, rows, LANES), BF16),
        send_sem=pltpu.SemaphoreType.DMA((SENDS,)),
        recv_sem=pltpu.SemaphoreType.DMA((SENDS,)),
        local_sem=pltpu.SemaphoreType.DMA((MOVES,)),
        fetch_sem=pltpu.SemaphoreType.DMA((2, 4)),
        add_sem=pltpu.SemaphoreType.DMA((4,)),
        own_sem=pltpu.SemaphoreType.DMA((4,)),
        core_send=pltpu.SemaphoreType.DMA((8 * local,)),
        core_recv=pltpu.SemaphoreType.DMA((8 * local,)),
        hop_send=pltpu.SemaphoreType.DMA((4 * local,)),
        hop_recv=pltpu.SemaphoreType.DMA((4 * local,)),
        back_send=pltpu.SemaphoreType.DMA((2 * local * (groups - 1),)),
        back_recv=pltpu.SemaphoreType.DMA((2 * local * (groups - 1),)),
    )
    names = [*inputs, *near, *far, *scratch]
    outs = pl.pallas_call(
        functools.partial(layer_kernel, experts, local, cap, buckets, shards, names),
        name="layer",
        out_shape=[*near.values(), *far.values()],
        in_specs=[vmem] * (len(inputs) - 2) + [hbm] * 2,
        out_specs=[vmem] * len(near) + [hbm] * len(far),
        scratch_shapes=[*scratch.values()],
        compiler_params=pltpu.CompilerParams(
            vmem_limit_bytes=LAYER_VMEM, collective_id=0, has_side_effects=True
        ),
        cost_estimate=pl.CostEstimate(flops=60 * 10**9, bytes_accessed=400 * 10**6, transcendentals=0),
    )(*inputs.values())
    o = SimpleNamespace(**dict(zip([*near, *far], outs)))

    def total_of(own, first_hop, last_hop):
        return own.astype(F32) + first_hop[:, 0].astype(F32) + last_hop.astype(F32)

    little = o.small_out
    return (
        o.layer_out,
        o.inputs_grad,
        o.main[0].astype(F32),
        o.main[1].astype(F32),
        o.main[2].astype(F32),
        o.main[3].astype(F32),
        little[:, :experts],
        little[:, experts],
        little[:, experts + 1],
        little[:table_rows_own, TABLE_AT : TABLE_AT + HEADS],
        total_of(o.own_up, o.t_up, o.v_up),
        total_of(o.own_down, o.t_down, o.v_down),
    )


def swap(value, axis, bit):
    return lax.ppermute(value, axis, [(i, i ^ bit) for i in range(lax.axis_size(axis))])


def swap_all(values):
    return [v if m == 0 else swap(v, EXPERT, m) for m, v in enumerate(values)]


def body(
    tokens,
    query_weight,
    key_weight,
    value_weight,
    project_weight,
    router_weight,
    prenorm_gain,
    midnorm_gain,
    bias_table,
    up_weight,
    down_weight,
    routes,
    bucket_index,
    cotangent,
):
    n, width = tokens.shape
    experts = router_weight.shape[1]
    shards, groups = lax.axis_size(DP), lax.axis_size(EXPERT)
    local, _, slab = up_weight.shape
    cap = 3 * n // experts
    buckets = bias_table.shape[0] * shards
    own_rows = query_weight.shape[0]
    hidden = slab * shards
    direct = slab % LANES == 0 and shards == 8
    here = lax.axis_index(EXPERT).astype(I32).reshape(1)
    smem = pl.BlockSpec(memory_space=pltpu.SMEM)
    vmem = pl.BlockSpec(memory_space=pltpu.VMEM)
    hbm = pl.BlockSpec(memory_space=pl.ANY)
    routes_t = routes.T
    bucket_row = bucket_index[None, :]

    def shape(s, dtype=BF16):
        return jax.ShapeDtypeStruct(s, dtype)

    if direct:
        return whole_layer(
            tokens, query_weight, key_weight, value_weight, project_weight, router_weight, prenorm_gain, midnorm_gain,
            bias_table, up_weight, down_weight, routes, bucket_row, cotangent,
        )
    small = jnp.concatenate(
        [
            router_weight,
            prenorm_gain[:, None],
            midnorm_gain[:, None],
            jnp.zeros((own_rows, TABLE_AT - experts - 2), BF16),
            jnp.pad(bias_table, ((0, own_rows - bias_table.shape[0]), (0, 0))),
            jnp.zeros((own_rows, LANES - TABLE_AT - HEADS), BF16),
        ],
        axis=1,
    )
    packed_width = 4 * width + LANES
    slots_shape = (groups, 8, 256)
    kept = [shape((n, width))] * 3 + [
        shape((width, n)),
        shape((width, n)),
        shape((n, width), F32),
        shape((n, width)),
        shape((n, LANES), F32),
        shape((16, n), F32),
    ]
    packed = jnp.concatenate(
        [query_weight, key_weight, value_weight, small, project_weight], axis=1
    )
    full = lax.all_gather(packed, DP, axis=0, tiled=True)
    cot_out = vmem_call(
        functools.partial(scatter_kernel, experts, local, cap),
        "send_cotangent",
        [shape((cap, width))] * experts,
        specs=[smem, vmem, vmem],
    )(here, routes_t, cotangent)
    up_all = lax.all_gather(up_weight, DP, axis=2, tiled=True)
    down_all = lax.all_gather(down_weight, DP, axis=1, tiled=True)
    up_all = up_all.reshape(local, width, hidden // width, width).transpose(0, 2, 1, 3)
    down_all = down_all.reshape(local, hidden // width, width, width)
    cut = hidden // width // 2
    weights = (up_all[:, :cut], up_all[:, cut:], down_all[:, :cut], down_all[:, cut:])
    forward = vmem_call(
        functools.partial(forward_kernel, experts, local, cap, buckets, shards),
        "attention_forward",
        kept + [shape((cap, width))] * experts + [shape((8, 256), F32)] * groups,
        scratch=[pltpu.VMEM((width, n), BF16), pltpu.VMEM((LANES, 2 * n), F32)],
        specs=[smem] + [vmem] * 5,
    )(here, tokens, full, routes, routes_t, bucket_row)
    q, k, v, normed, merged_t, middle, second, gates, line = forward[:9]
    x_out, slots_out = forward[9 : 9 + experts], forward[9 + experts :]
    slots_in = jnp.stack(swap_all(slots_out))
    x_in = jnp.stack([jnp.stack(swap_all(x_out[l::local])) for l in range(local)])
    cot_in = jnp.stack([jnp.stack(swap_all(cot_out[l::local])) for l in range(local)])

    rows = groups * cap
    replies, backs, dots, up_grads, down_grads = [], [], [], [], []
    for l in range(local):
        count, slab_width = weights[0].shape[1], weights[0].shape[3]
        per = width // slab_width
        outs = pl.pallas_call(
            functools.partial(expert_kernel, l, groups, cap),
            name=EXPERT,
            out_shape=[shape((cap, width))] * (2 * groups)
            + [shape((8, 256), F32)] * groups
            + [shape((count, width, slab_width))] * 2
            + [shape((count, slab_width, width))] * 2,
            in_specs=[hbm, hbm, vmem] + [hbm] * 4,
            out_specs=[vmem] * (3 * groups) + [hbm] * 4,
            scratch_shapes=[
                pltpu.VMEM((rows, width), BF16),
                pltpu.VMEM((width, rows), BF16),
                pltpu.VMEM((rows, width), BF16),
                pltpu.VMEM((rows, width), BF16),
                pltpu.VMEM((rows, width), F32),
                pltpu.VMEM((rows, width), F32),
                pltpu.VMEM((2, width, width), BF16),
                pltpu.VMEM((2, width, width), BF16),
                pltpu.VMEM((2, width, width), BF16),
                pltpu.VMEM((2, width, width), BF16),
                pltpu.VMEM((rows, width), BF16),
                pltpu.VMEM((rows, width), BF16),
                pltpu.SemaphoreType.DMA((2, 2 * per)),
                pltpu.SemaphoreType.DMA((2, 2 * per)),
                pltpu.SemaphoreType.DMA((2, groups)),
            ],
            compiler_params=pltpu.CompilerParams(vmem_limit_bytes=VMEM_LIMIT),
            cost_estimate=pl.CostEstimate(
                flops=12 * rows * width * hidden, bytes_accessed=40 * 10**6, transcendentals=0
            ),
        )(x_in, cot_in, slots_in, *weights)
        replies.append(outs[:groups])
        backs.append(swap_all(outs[groups : 2 * groups]))
        dots.append(swap_all(outs[2 * groups : 3 * groups]))
        ug, dg = outs[3 * groups : 3 * groups + 2], outs[3 * groups + 2 :]
        ug = jnp.concatenate(ug, axis=0).transpose(1, 0, 2).reshape(width, hidden)
        dg = jnp.concatenate(dg, axis=0).reshape(hidden, width)
        up_grads.append(lax.psum_scatter(ug, DP, scatter_dimension=1, tiled=True).astype(F32))
        down_grads.append(lax.psum_scatter(dg, DP, scatter_dimension=0, tiled=True).astype(F32))

    flat = lambda parts: [parts[l][m] for m in range(groups) for l in range(local)]
    inputs_grad, grads = vmem_call(
        functools.partial(backward_kernel, experts, local, cap, buckets, shards),
        "attention_backward",
        [shape((n, width)), shape((width, packed_width))],
        scratch=[
            pltpu.VMEM((n, width), BF16),
            pltpu.VMEM((n, width), F32),
            pltpu.VMEM((width, n), BF16),
            pltpu.VMEM((width, n), BF16),
            pltpu.VMEM((n, width), BF16),
            pltpu.VMEM((n, width), BF16),
            pltpu.VMEM((HEADS, 8, n), F32),
            pltpu.VMEM((LANES, 2 * n), F32),
            pltpu.VMEM((n, width), BF16),
        ],
        specs=[smem] + [vmem] * (14 + 2 * experts),
        flops=40 * 10**9,
        moved=30 * 10**6,
    )(
        here,
        tokens,
        full,
        routes,
        bucket_row,
        cotangent,
        q,
        k,
        v,
        normed,
        merged_t,
        middle,
        second,
        gates,
        line,
        *flat(backs),
        *flat(dots),
    )
    shares = lax.psum_scatter(grads, DP, scatter_dimension=0, tiled=True)
    totals = lax.psum(shares, EXPERT).astype(F32)

    replies = flat([swap_all(r) for r in replies])
    layer_out = vmem_call(
        functools.partial(combine_kernel, local, cap),
        "layer_out",
        shape((n, width)),
        specs=[smem] + [vmem] * (3 + experts),
        flops=4 * n * experts * cap * width,
        moved=6 * 10**6,
    )(here, routes, gates, middle, *replies)

    at = 3 * width
    return (
        layer_out,
        inputs_grad,
        totals[:, :width],
        totals[:, width : 2 * width],
        totals[:, 2 * width : 3 * width],
        totals[:, at + LANES :],
        totals[:, at : at + experts],
        totals[:, at + experts],
        totals[:, at + experts + 1],
        totals[: bias_table.shape[0], at + TABLE_AT : at + TABLE_AT + HEADS],
        jnp.stack(up_grads),
        jnp.stack(down_grads),
    )


def solution(mesh):
    both, first = P((DP, EXPERT), None), P(DP, None)
    up, down = P(EXPERT, None, DP), P(EXPERT, DP, None)
    return jax.shard_map(
        body,
        mesh=mesh,
        in_specs=(both,)
        + (first,) * 5
        + (P(DP), P(DP), first, up, down, both, P(), both),
        out_specs=(both, both) + (first,) * 5 + (P(DP), P(DP), first, up, down),
        check_vma=False,
    )
```

```python
import functools
from types import SimpleNamespace

import jax
import jax.numpy as jnp
from jax import lax
from jax.experimental import pallas as pl
from jax.experimental.pallas import tpu as pltpu
from jax.sharding import PartitionSpec as P

HEADS = 12
HEAD_DIM = 64
EPSILON = 1e-06
NEGATIVE = -1e30
SCALE = HEAD_DIM ** (-0.5)
LANES = 128
TABLE_AT = 32
QBLOCK = 256
F32 = jnp.float32
BF16 = jnp.bfloat16
I32 = jnp.int32
VMEM_LIMIT = 60 * 1024 * 1024
LAYER_VMEM = 63 * 1024 * 1024
MESH = pl.DeviceIdType.MESH
DP, EXPERT = "dp", "expert"
UP, DOWN, OWN, A, B = range(5)


def nn(left, right):
    return lax.dot_general(left, right, (((1,), (0,)), ((), ())), preferred_element_type=F32)


def nt(left, right):
    return lax.dot_general(left, right, (((1,), (1,)), ((), ())), preferred_element_type=F32)


def tn(left, right):
    return lax.dot_general(left, right, (((0,), (0,)), ((), ())), preferred_element_type=F32)


def iota(shape, axis):
    return lax.broadcasted_iota(I32, shape, axis)


def hot(mask):
    return jnp.where(mask, 1.0, 0.0).astype(BF16)


def vmem_call(body, name, out_shape, scratch=(), flops=0, moved=0, specs=None):
    def call(*args):
        in_specs = specs or [pl.BlockSpec(memory_space=pltpu.VMEM)] * len(args)
        return pl.pallas_call(
            body,
            name=name,
            out_shape=out_shape,
            in_specs=in_specs,
            out_specs=jax.tree.map(lambda _: pl.BlockSpec(memory_space=pltpu.VMEM), out_shape),
            scratch_shapes=scratch,
            compiler_params=pltpu.CompilerParams(vmem_limit_bytes=VMEM_LIMIT),
            cost_estimate=pl.CostEstimate(flops=flops, bytes_accessed=moved, transcendentals=0),
        )(*args)

    return call


def places(r, slot, here, local, cap):
    owner = lax.div(r, local)
    return (owner ^ here) * (local * cap) + lax.rem(r, local) * cap + slot.astype(I32)


def places_by_lane(routes_t, here, experts, local, cap):
    n = routes_t.shape[1]
    r0, r1 = routes_t[0:1, :], routes_t[1:2, :]
    tall = iota((-(-experts // 16) * 16, n), 0)
    oh0, oh1 = tall == r0, tall == r1
    earlier = hot(iota((n, n), 0) < iota((n, n), 1))
    count = nn(hot(oh0 | oh1), earlier)
    s0 = jnp.sum(jnp.where(oh0, count, 0.0), axis=0, keepdims=True)
    s1 = jnp.sum(jnp.where(oh1, count, 0.0), axis=0, keepdims=True)
    return places(r0, s0, here, local, cap), places(r1, s1, here, local, cap)


def places_by_row(routes, here, local, cap):
    n = routes.shape[0]
    r0, r1 = routes[:, 0:1], routes[:, 1:2]
    wide = iota((n, LANES), 1)
    oh0, oh1 = wide == r0, wide == r1
    earlier = hot(iota((n, n), 1) < iota((n, n), 0))
    count = nn(earlier, hot(oh0 | oh1))
    s0 = jnp.sum(jnp.where(oh0, count, 0.0), axis=1, keepdims=True)
    s1 = jnp.sum(jnp.where(oh1, count, 0.0), axis=1, keepdims=True)
    return places(r0, s0, here, local, cap), places(r1, s1, here, local, cap), oh0, oh1


def put_rows(values, d0, d1, start, count):
    at = iota((count, values.shape[0]), 0) + start
    return nn(hot((at == d0) | (at == d1)), values).astype(BF16)


def scatter_kernel(experts, local, cap, here_ref, routes_t_ref, values_ref, *out_refs):
    d0, d1 = places_by_lane(routes_t_ref[...], here_ref[0], experts, local, cap)
    values = values_ref[...]
    for at, out_ref in enumerate(out_refs):
        out_ref[...] = put_rows(values, d0, d1, at * cap, cap)


def table_rows(misc, buckets, shards):
    depth = misc.shape[0]
    per, rows = buckets // shards, depth // shards
    b = iota((buckets, depth), 0)
    select = hot(iota((buckets, depth), 1) == lax.div(b, per) * rows + lax.rem(b, per))
    return nn(select, misc)


def toeplitz(line, twice_ref):
    n = line.shape[1]
    rolled = pltpu.roll(jnp.broadcast_to(line, (LANES, n)), 0, 1, stride=1, stride_axis=0)
    twice_ref[:, :n] = rolled
    twice_ref[:, n:] = rolled


def bias_columns(twice_ref, n, block, rows):
    parts = []
    for jb in range(rows // LANES):
        start = (block * QBLOCK - jb * LANES) % n
        parts.append(twice_ref[:, start : start + QBLOCK])
    return jnp.concatenate(parts, axis=0)


def causal(scores, block):
    last = scores.shape[0] - QBLOCK
    keep = iota((QBLOCK, QBLOCK), 0) <= iota((QBLOCK, QBLOCK), 1)
    tail = jnp.where(keep, scores[last:], NEGATIVE)
    return tail if last == 0 else jnp.concatenate([scores[:last], tail], axis=0)


def chunked(count, size=256):
    return [slice(at, at + size) for at in range(0, count, size)]


def project_inputs(experts, buckets, shards, tok_ref, w_ref, bucket_ref, q_ref, k_ref, v_ref, normed_t_ref, v_t_ref, line_ref):
    n, width = tok_ref.shape
    misc = w_ref[:, 3 * width : 3 * width + LANES]
    gain = jnp.transpose(misc.astype(F32))[experts : experts + 1]
    for cut in chunked(n):
        x = tok_ref[cut, :].astype(F32)
        normed = x * lax.rsqrt(jnp.mean(x * x, axis=-1, keepdims=True) + EPSILON) * gain
        normed = normed.astype(BF16)
        normed_t_ref[:, cut] = jnp.transpose(normed)
        query = nn(normed, w_ref[:, :width]).astype(BF16)
        q_ref[cut, :] = (query.astype(F32) * SCALE).astype(BF16)
        k_ref[cut, :] = nn(normed, w_ref[:, width : 2 * width]).astype(BF16)
        value = nn(normed, w_ref[:, 2 * width : 3 * width]).astype(BF16)
        v_ref[cut, :] = value
        v_t_ref[:, cut] = jnp.transpose(value)
    table = table_rows(misc, buckets, shards).astype(BF16)
    by_bucket = hot(iota((buckets, n), 0) == bucket_ref[...])
    line_ref[...] = tn(table, by_bucket)[TABLE_AT : TABLE_AT + 16]


def attend(q_ref, k_ref, v_t_ref, line_ref, twice_ref, merged_t_ref):
    n = q_ref.shape[0]
    half = iota((1, LANES), 1) < HEAD_DIM

    def pair(hp, carry):
        lanes = pl.ds(pl.multiple_of(hp * LANES, LANES), LANES)
        kp, qp = k_ref[:, lanes], q_ref[:, lanes]
        for side in range(2):
            toeplitz(line_ref[pl.ds(hp * 2 + side, 1), :], twice_ref)
            keys = kp * hot(half if side == 0 else ~half)
            at = pl.ds(pl.multiple_of(hp * LANES + side * HEAD_DIM, HEAD_DIM), HEAD_DIM)
            for block in range(n // QBLOCK):
                rows = (block + 1) * QBLOCK
                cols = slice(block * QBLOCK, rows)
                scores = nt(keys[:rows], qp[cols]) + bias_columns(twice_ref, n, block, rows)
                scores = causal(scores, block)
                top = jnp.max(scores, axis=0, keepdims=True)
                e = jnp.exp(scores - top)
                probs = (e * (1.0 / jnp.sum(e, axis=0, keepdims=True))).astype(BF16)
                merged_t_ref[at, cols] = nn(v_t_ref[at, :rows], probs).astype(BF16)
        return carry

    lax.fori_loop(0, HEADS // 2, pair, 0)


def route(experts, local, cap, here, tok_ref, w_ref, routes_ref, merged_t_ref, middle_ref, second_ref, gates_ref, slot_refs):
    n, width = tok_ref.shape
    misc = w_ref[:, 3 * width : 3 * width + LANES]
    gain = jnp.transpose(misc.astype(F32))[experts + 1 : experts + 2]
    for cut in chunked(n):
        middle = tok_ref[cut, :].astype(F32) + tn(merged_t_ref[:, cut], w_ref[:, 3 * width + LANES :])
        middle_ref[cut, :] = middle
        second = middle * lax.rsqrt(jnp.mean(middle * middle, axis=-1, keepdims=True) + EPSILON)
        second_ref[cut, :] = (second * gain).astype(BF16)
    c0, c1, oh0, oh1 = places_by_row(routes_ref[...], here, local, cap)
    logits = nn(second_ref[...], misc)
    p0 = jnp.sum(jnp.where(oh0, logits, 0.0), axis=1, keepdims=True)
    p1 = jnp.sum(jnp.where(oh1, logits, 0.0), axis=1, keepdims=True)
    top = jnp.maximum(p0, p1)
    e0, e1 = jnp.exp(p0 - top), jnp.exp(p1 - top)
    g0, g1 = e0 / (e0 + e1), e1 / (e0 + e1)
    wide = iota((n, LANES), 1)
    gates_ref[...] = jnp.where(wide == 0, g0, jnp.where(wide == 1, g1, 0.0))
    for at, slot_ref in enumerate(slot_refs):
        slot_ref[...] = jnp.zeros(slot_ref.shape, F32)
        for l in range(local):
            lane = iota((n, slot_ref.shape[1]), 1) + (at * local + l) * cap
            held = jnp.where(lane == c0, g0, jnp.where(lane == c1, g1, 0.0))
            slot_ref[l : l + 1, :] = jnp.sum(held, axis=0, keepdims=True)


def forward_kernel(
    experts, local, cap, buckets, shards,
    here_ref, tok_ref, w_ref, routes_ref, routes_t_ref, bucket_ref,
    q_ref, k_ref, v_ref, normed_t_ref, merged_t_ref, middle_ref, second_ref, gates_ref, line_ref,
    *rest,
):
    groups = experts // local
    x_refs, slot_refs = rest[:experts], rest[experts : experts + groups]
    v_t_ref, twice_ref = rest[experts + groups :]
    here = here_ref[0]
    project_inputs(experts, buckets, shards, tok_ref, w_ref, bucket_ref, q_ref, k_ref, v_ref, normed_t_ref, v_t_ref, line_ref)
    attend(q_ref, k_ref, v_t_ref, line_ref, twice_ref, merged_t_ref)
    route(experts, local, cap, here, tok_ref, w_ref, routes_ref, merged_t_ref, middle_ref, second_ref, gates_ref, slot_refs)
    d0, d1 = places_by_lane(routes_t_ref[...], here, experts, local, cap)
    for at, x_ref in enumerate(x_refs):
        x_ref[...] = put_rows(second_ref[...], d0, d1, at * cap, cap)


def gelu_both(v):
    t = pl.reciprocal(1.0 + (0.3275911 * 0.7071067811865476) * jnp.abs(v))
    e = jnp.exp(-0.5 * (v * v))
    poly = 0.5 * 1.061405429
    for coefficient in (-1.453152027, 1.421413741, -0.284496736, 0.254829592):
        poly = poly * t + 0.5 * coefficient
    tail = poly * t * e
    phi = jnp.where(v < 0.0, tail, 1.0 - tail)
    return v * phi, phi + v * e * 0.3989422804014327


def expert_kernel(local_at, groups, cap, *refs):
    take = iter(refs)
    rows_in, cots_in, slots_in, up_a, up_b, down_a, down_b = (next(take) for _ in range(7))
    reply_refs = [next(take) for _ in range(groups)]
    back_refs = [next(take) for _ in range(groups)]
    dot_refs = [next(take) for _ in range(groups)]
    ug_a, ug_b, dg_a, dg_b = (next(take) for _ in range(4))
    x_ref, xt_ref, cot_ref, gr_ref, reply_ref, back_ref = (next(take) for _ in range(6))
    up_buf, down_buf, ug_buf, dg_buf, act_ref, gh_ref = (next(take) for _ in range(6))
    in_sem, out_sem, row_sem = take
    rows, width = x_ref.shape
    slab = up_a.shape[3]
    block = up_buf.shape[2]
    per = block // slab
    half = up_a.shape[1] // per
    steps = 2 * half

    def fetches(up, down, at, slot):
        for i in range(per):
            cut = slice(i * slab, (i + 1) * slab)
            yield pltpu.make_async_copy(
                up.at[local_at, at * per + i], up_buf.at[slot, :, cut], in_sem.at[slot, i]
            )
            yield pltpu.make_async_copy(
                down.at[local_at, at * per + i], down_buf.at[slot, cut, :], in_sem.at[slot, per + i]
            )

    def stores(up, down, at, slot):
        for i in range(per):
            cut = slice(i * slab, (i + 1) * slab)
            yield pltpu.make_async_copy(
                ug_buf.at[slot, :, cut], up.at[at * per + i], out_sem.at[slot, i]
            )
            yield pltpu.make_async_copy(
                dg_buf.at[slot, cut, :], down.at[at * per + i], out_sem.at[slot, per + i]
            )

    def begin(kind, first, second, step, slot):
        @pl.when(step < half)
        def _():
            for copy in kind(*first, step, slot):
                copy.start()

        @pl.when(step >= half)
        def _():
            for copy in kind(*second, step - half, slot):
                copy.start()

    begin(fetches, (up_a, down_a), (up_b, down_b), 0, 0)
    copies = []
    for m in range(groups):
        cut = slice(m * cap, (m + 1) * cap)
        copies.append(pltpu.make_async_copy(rows_in.at[local_at, m], x_ref.at[cut, :], row_sem.at[0, m]))
        copies.append(pltpu.make_async_copy(cots_in.at[local_at, m], cot_ref.at[cut, :], row_sem.at[1, m]))
    for copy in copies:
        copy.start()
    for copy in copies:
        copy.wait()
    for m in range(groups):
        cut = slice(m * cap, (m + 1) * cap)
        slots = slots_in[m, local_at : local_at + 1, :]
        gate = jnp.transpose(jnp.broadcast_to(slots, (LANES, slots.shape[1])))[:cap, 0:1]
        gr_ref[cut, :] = (gate * cot_ref[cut, :].astype(F32)).astype(BF16)
    xt_ref[...] = jnp.transpose(x_ref[...])
    reply_ref[...] = jnp.zeros_like(reply_ref)
    back_ref[...] = jnp.zeros_like(back_ref)

    def step(at, carry):
        slot = lax.rem(at, 2)

        @pl.when(at + 1 < steps)
        def _():
            begin(fetches, (up_a, down_a), (up_b, down_b), at + 1, 1 - slot)

        for copy in fetches(up_a, down_a, 0, slot):
            copy.wait()

        @pl.when(at >= 2)
        def _():
            for copy in stores(ug_a, dg_a, 0, slot):
                copy.wait()

        chunk = 256
        for c in range(rows // chunk):
            cut = slice(c * chunk, (c + 1) * chunk)
            act, slope = gelu_both(nn(x_ref[cut, :], up_buf[slot]))
            act_ref[cut, :] = act.astype(BF16)
            grad = nt(gr_ref[cut, :], down_buf[slot])
            gh_ref[cut, :] = (grad * slope).astype(BF16)
            reply_ref[cut, :] += nn(act_ref[cut, :], down_buf[slot])
            back_ref[cut, :] += nt(gh_ref[cut, :], up_buf[slot])
        dg_buf[slot] = tn(act_ref[...], gr_ref[...]).astype(BF16)
        ug_buf[slot] = nn(xt_ref[...], gh_ref[...]).astype(BF16)
        begin(stores, (ug_a, dg_a), (ug_b, dg_b), at, slot)
        return carry

    lax.fori_loop(0, steps, step, 0)
    reply = reply_ref[...].astype(BF16)
    dots = jnp.sum(reply.astype(F32) * cot_ref[...].astype(F32), axis=1, keepdims=True)
    dots = jnp.transpose(jnp.broadcast_to(dots, (rows, LANES)))[0:8]
    for m in range(groups):
        cut = slice(m * cap, (m + 1) * cap)
        reply_refs[m][...] = reply[cut]
        back_refs[m][...] = back_ref[cut, :].astype(BF16)
        shifted = dots if m == 0 else pltpu.roll(dots, rows - m * cap, 1)
        dot_refs[m][...] = shifted[:, : dot_refs[m].shape[1]]
    for slot in range(2):
        for copy in stores(ug_a, dg_a, 0, slot):
            copy.wait()


def attend_back(after, q_ref, k_ref, v_ref, gm_ref, k_t_ref, line_ref, twice_ref, gq_t_ref, gk_ref, gv_ref, fold_ref):
    n = q_ref.shape[0]
    half = iota((1, LANES), 1) < HEAD_DIM

    def pair(hp, carry):
        lanes = pl.ds(pl.multiple_of(hp * LANES, LANES), LANES)
        kp, qp, vp, gp = k_ref[:, lanes], q_ref[:, lanes], v_ref[:, lanes], gm_ref[:, lanes]
        gk = [jnp.zeros((QBLOCK, LANES), F32) for _ in range(n // QBLOCK)]
        gv = [jnp.zeros((QBLOCK, LANES), F32) for _ in range(n // QBLOCK)]
        for side in range(2):
            toeplitz(line_ref[pl.ds(hp * 2 + side, 1), :], twice_ref)
            own = hot(half if side == 0 else ~half)
            keys, values, queries, outs = kp * own, vp * own, qp * own, gp * own
            at = pl.ds(pl.multiple_of(hp * LANES + side * HEAD_DIM, HEAD_DIM), HEAD_DIM)
            folded = jnp.zeros((LANES, n), F32)
            for block in range(n // QBLOCK):
                rows = (block + 1) * QBLOCK
                cols = slice(block * QBLOCK, rows)
                scores = nt(keys[:rows], qp[cols]) + bias_columns(twice_ref, n, block, rows)
                scores = causal(scores, block)
                top = jnp.max(scores, axis=0, keepdims=True)
                e = jnp.exp(scores - top)
                probs = e * (1.0 / jnp.sum(e, axis=0, keepdims=True))
                grad_probs = nt(values[:rows], gp[cols])
                total = jnp.sum(probs * grad_probs, axis=0, keepdims=True)
                gs = (probs * (grad_probs - total)).astype(BF16)
                low = probs.astype(BF16)
                gq_t_ref[at, cols] = (nn(k_t_ref[at, :rows], gs) * SCALE).astype(BF16)
                gk_part = nn(gs, queries[cols])
                gv_part = nn(low, outs[cols])
                for b in range(block + 1):
                    cut = slice(b * QBLOCK, (b + 1) * QBLOCK)
                    gk[b] += gk_part[cut]
                    gv[b] += gv_part[cut]
                wide = gs.astype(F32)
                for jb in range(rows // LANES):
                    piece = wide[jb * LANES : (jb + 1) * LANES]
                    parts = []
                    for lb in range(n // LANES):
                        src = (lb + jb) % (n // LANES) - block * (QBLOCK // LANES)
                        inside = 0 <= src < QBLOCK // LANES
                        parts.append(
                            piece[:, src * LANES : (src + 1) * LANES]
                            if inside
                            else jnp.zeros((LANES, LANES), F32)
                        )
                    folded += jnp.concatenate(parts, axis=1)
            size = LANES
            while size > 8:
                size //= 2
                folded = folded[:size] + pltpu.roll(folded[size : 2 * size], n - size, 1)
            fold_ref[hp * 2 + side] = folded
        for b in range(n // QBLOCK):
            cut = slice(b * QBLOCK, (b + 1) * QBLOCK)
            gk_ref[cut, lanes] = gk[b].astype(BF16)
            gv_ref[cut, lanes] = gv[b].astype(BF16)
        after(hp)
        return carry

    lax.fori_loop(0, HEADS // 2, pair, 0)


def middle_back(
    experts, local, cap, here, w_ref, routes_ref, cot_ref, middle_ref, second_ref, gates_ref, back_refs, dot_refs, gmid_ref, branch_ref
):
    n, width = cot_ref.shape
    misc = w_ref[:, 3 * width : 3 * width + LANES]
    gain = jnp.transpose(misc.astype(F32))[experts + 1 : experts + 2]
    c0_all, c1_all, oh0_all, oh1_all = places_by_row(routes_ref[...], here, local, cap)
    router_grad = jnp.zeros((width, LANES), F32)
    midnorm_grad = jnp.zeros((1, width), F32)
    for cut in chunked(n):
        c0, c1, oh0, oh1 = c0_all[cut], c1_all[cut], oh0_all[cut], oh1_all[cut]
        count = c0.shape[0]
        grad_second = jnp.zeros((count, width), F32)
        gg0 = jnp.zeros((count, 1), F32)
        gg1 = jnp.zeros((count, 1), F32)
        for at in range(experts):
            lane = iota((count, cap), 1) + at * cap
            h0, h1 = lane == c0, lane == c1
            grad_second += nn(hot(h0 | h1), back_refs[at][...])
            dots = dot_refs[at][0:1, :cap]
            gg0 += jnp.sum(jnp.where(h0, dots, 0.0), axis=1, keepdims=True)
            gg1 += jnp.sum(jnp.where(h1, dots, 0.0), axis=1, keepdims=True)
        g0, g1 = gates_ref[cut, 0:1], gates_ref[cut, 1:2]
        inner = g0 * gg0 + g1 * gg1
        grad_logits = jnp.where(oh0, g0 * (gg0 - inner), jnp.where(oh1, g1 * (gg1 - inner), 0.0))
        grad_logits = grad_logits.astype(BF16)
        grad_second += nt(grad_logits, misc)
        router_grad += tn(second_ref[cut, :], grad_logits)
        middle = middle_ref[cut, :]
        r = lax.rsqrt(jnp.mean(middle * middle, axis=-1, keepdims=True) + EPSILON)
        mr = middle * r
        midnorm_grad += jnp.sum(grad_second * mr, axis=0, keepdims=True)
        u = gain * grad_second
        gmid = cot_ref[cut, :].astype(F32) + r * (u - mr * jnp.mean(u * mr, axis=-1, keepdims=True))
        gmid_ref[cut, :] = gmid
        branch_ref[cut, :] = gmid.astype(BF16)
    return router_grad, midnorm_grad


def table_back(buckets, shards, width, bucket_ref, fold_ref):
    n = bucket_ref.shape[1]
    folded = fold_ref[...].reshape(HEADS * 8, n)
    row = iota((HEADS * 8, n), 0)
    for bit in (1, 2, 4):
        folded = jnp.where((row & bit) != 0, pltpu.roll(folded, n - bit, 1), folded)
    by_distance = jnp.sum(folded.reshape(HEADS, 8, n), axis=1)
    by_distance = jnp.concatenate([by_distance, jnp.zeros((16 - HEADS, n), F32)], axis=0)
    by_bucket = hot(iota((buckets, n), 0) == bucket_ref[...])
    table_grad = jnp.zeros((buckets, 16), F32)
    for _ in range(3):
        piece = by_distance.astype(BF16)
        table_grad += nt(by_bucket, piece)
        by_distance = by_distance - piece.astype(F32)
    spread = hot(iota((16, LANES), 1) == iota((16, LANES), 0) + TABLE_AT)
    table_grad = nn(table_grad.astype(BF16), spread).astype(BF16)
    rows, per = width // shards, buckets // shards
    b = iota((width, buckets), 1)
    select = hot(iota((width, buckets), 0) == lax.div(b, per) * rows + lax.rem(b, per))
    return nn(select, table_grad)


def inputs_back(experts, tok_ref, w_ref, gq_t_ref, gk_ref, gv_ref, gmid_ref, inputs_grad_ref):
    n, width = tok_ref.shape
    misc = w_ref[:, 3 * width : 3 * width + LANES]
    gain = jnp.transpose(misc.astype(F32))[experts : experts + 1]
    prenorm_grad = jnp.zeros((1, width), F32)
    for cut in chunked(n):
        grad_normed = nt(jnp.transpose(gq_t_ref[:, cut]), w_ref[:, :width])
        grad_normed += nt(gk_ref[cut, :], w_ref[:, width : 2 * width])
        grad_normed += nt(gv_ref[cut, :], w_ref[:, 2 * width : 3 * width])
        x = tok_ref[cut, :].astype(F32)
        q = lax.rsqrt(jnp.mean(x * x, axis=-1, keepdims=True) + EPSILON)
        xq = x * q
        prenorm_grad += jnp.sum(grad_normed * xq, axis=0, keepdims=True)
        w = gain * grad_normed
        back = q * (w - xq * jnp.mean(w * xq, axis=-1, keepdims=True))
        inputs_grad_ref[cut, :] = (gmid_ref[cut, :] + back).astype(BF16)
    return prenorm_grad


def small_grads(experts, router_grad, prenorm_grad, midnorm_grad, table):
    width = prenorm_grad.shape[1]
    tall = iota((LANES, width), 0)
    gains = jnp.where(tall == experts, prenorm_grad, jnp.where(tall == experts + 1, midnorm_grad, 0.0))
    return (router_grad + jnp.transpose(gains) + table).astype(BF16)


def backward_kernel(
    experts, local, cap, buckets, shards,
    here_ref, tok_ref, w_ref, routes_ref, bucket_ref, cot_ref, q_ref, k_ref, v_ref, normed_t_ref, merged_t_ref,
    middle_ref, second_ref, gates_ref, line_ref,
    *rest,
):
    take = iter(rest)
    back_refs = [next(take) for _ in range(experts)]
    dot_refs = [next(take) for _ in range(experts)]
    inputs_grad_ref, grads_ref = next(take), next(take)
    gm_ref, gmid_ref, k_t_ref, gq_t_ref, gk_ref, gv_ref, fold_ref, twice_ref, branch_ref = take
    width = tok_ref.shape[1]
    router_grad, midnorm_grad = middle_back(
        experts, local, cap, here_ref[0], w_ref, routes_ref, cot_ref, middle_ref, second_ref, gates_ref,
        back_refs, dot_refs, gmid_ref, branch_ref,
    )
    grads_ref[:, 3 * width + LANES :] = nn(merged_t_ref[...], branch_ref[...]).astype(BF16)
    gm_ref[...] = nt(branch_ref[...], w_ref[:, 3 * width + LANES :]).astype(BF16)
    k_t_ref[...] = jnp.transpose(k_ref[...])
    attend_back(
        lambda hp: None, q_ref, k_ref, v_ref, gm_ref, k_t_ref, line_ref, twice_ref, gq_t_ref, gk_ref, gv_ref, fold_ref
    )
    normed_t = normed_t_ref[...]
    grads_ref[:, :width] = nt(normed_t, gq_t_ref[...]).astype(BF16)
    grads_ref[:, width : 2 * width] = nn(normed_t, gk_ref[...]).astype(BF16)
    grads_ref[:, 2 * width : 3 * width] = nn(normed_t, gv_ref[...]).astype(BF16)
    prenorm_grad = inputs_back(experts, tok_ref, w_ref, gq_t_ref, gk_ref, gv_ref, gmid_ref, inputs_grad_ref)
    table = table_back(buckets, shards, width, bucket_ref, fold_ref)
    grads_ref[:, 3 * width : 3 * width + LANES] = small_grads(experts, router_grad, prenorm_grad, midnorm_grad, table)


def combine(local, cap, here, routes_ref, gates_ref, middle_ref, reply_refs, out_ref):
    n, width = middle_ref.shape
    c0, c1, _, _ = places_by_row(routes_ref[...], here, local, cap)
    for cut in chunked(n):
        picked0 = jnp.zeros((cut.stop - cut.start, width), F32)
        picked1 = jnp.zeros((cut.stop - cut.start, width), F32)
        for at, reply_ref in enumerate(reply_refs):
            lane = iota((cut.stop - cut.start, cap), 1) + at * cap
            picked0 += nn(hot(lane == c0[cut]), reply_ref[...])
            picked1 += nn(hot(lane == c1[cut]), reply_ref[...])
        out = middle_ref[cut, :] + gates_ref[cut, 0:1] * picked0 + gates_ref[cut, 1:2] * picked1
        out_ref[cut, :] = out.astype(BF16)


def combine_kernel(local, cap, here_ref, routes_ref, gates_ref, middle_ref, *rest):
    *reply_refs, out_ref = rest
    combine(local, cap, here_ref[0], routes_ref, gates_ref, middle_ref, reply_refs, out_ref)


class View:
    def __init__(self, ref, index=None):
        self.ref, self.index = ref, index

    def __getitem__(self, index):
        return View(self.ref, index)

    def cut(self):
        return self.ref if self.index is None else self.ref.at[self.index]


class Window:
    def __init__(self, ref, lead, shape):
        self.ref, self.lead, self.shape = ref, lead, shape

    def whole(self, index):
        index = () if index is Ellipsis else index if isinstance(index, tuple) else (index,)
        index += (slice(None),) * (len(self.shape) - len(index))
        limited = [slice(0, size) if i == slice(None) else i for i, size in zip(index, self.shape)]
        return (*self.lead, *limited)

    def __getitem__(self, index):
        return self.ref[self.whole(index)]

    def __setitem__(self, index, value):
        self.ref[self.whole(index)] = value

    def view(self, *index):
        return View(self.ref, self.whole(index))


class Remote:
    def __init__(self, *args):
        self.args = args

    def make(self):
        src, dst, sends, receives, at, axis, peer = self.args
        return pltpu.make_async_remote_copy(
            src_ref=src.cut(),
            dst_ref=dst.cut(),
            send_sem=sends.at[at],
            recv_sem=receives.at[at],
            device_id={axis: peer},
            device_id_type=MESH,
        )

    def start(self):
        self.make().start()

    def wait_send(self):
        self.make().wait_send()

    def wait_recv(self):
        self.make().wait_recv()

    def wait(self):
        self.wait_send()
        self.wait_recv()


class Local:
    def __init__(self, *args):
        self.args = args

    def make(self):
        src, dst, sems, at = self.args
        return pltpu.make_async_copy(src.cut(), dst.cut(), sems.at[at])

    def wait(self):
        self.make().wait()


class Links:
    def __init__(self, send_sem, recv_sem, local_sem):
        self.send_sem, self.recv_sem, self.local_sem = send_sem, recv_sem, local_sem
        self.sent = self.moved = 0
        self.open_sends = []

    def send(self, src, dst, axis, peer):
        copy = Remote(src, dst, self.send_sem, self.recv_sem, self.sent, axis, peer)
        self.sent += 1
        copy.start()
        self.open_sends.append(copy)
        return copy

    def move(self, src, dst):
        copy = Local(src, dst, self.local_sem, self.moved)
        self.moved += 1
        copy.make().start()
        return copy

    def forget(self, copies):
        self.open_sends = [other for other in self.open_sends if all(copy is not other for copy in copies)]

    def close(self):
        for copy in self.open_sends:
            copy.wait_send()


SENDS, MOVES = 144, 26


def layer_kernel(experts, local, cap, buckets, shards, names, *refs):
    r = SimpleNamespace(**dict(zip(names, refs, strict=True)))
    groups = experts // local
    me, here = lax.axis_index(DP), lax.axis_index(EXPERT)
    tok_ref, cot_ref, w_ref, routes_ref, bucket_ref = r.tok, r.cot, r.w, r.routes_by_row, r.bucket
    n, width = tok_ref.shape
    rows = r.wq.shape[0]
    slab = r.up.shape[2]
    across, along, core, diagonal = me ^ 2, me ^ 4, me ^ 1, me ^ 6
    barrier = pltpu.get_barrier_semaphore()
    for peer in (across, along, core):
        pl.semaphore_signal(barrier, inc=1, device_id={DP: peer}, device_id_type=MESH)
    for m in range(1, groups):
        pl.semaphore_signal(barrier, inc=1, device_id={EXPERT: here ^ m}, device_id_type=MESH)
    pl.semaphore_wait(barrier, 3 + groups - 1)
    links = Links(r.send_sem, r.recv_sem, r.local_sem)
    send, move = links.send, links.move

    def rows_of(owner, start=0, count=rows):
        return pl.ds(pl.multiple_of(owner * rows + start, 16), count)

    first = 3 * width + LANES
    parts = (slice(0, first), slice(first, first + width))
    mine = rows_of(me)
    w_ref[mine, 0:width] = r.wq[...]
    w_ref[mine, width : 2 * width] = r.wk[...]
    w_ref[mine, 2 * width : 3 * width] = r.wv[...]
    r.columns[...] = jnp.zeros_like(r.columns)
    r.columns[0:experts, 0:rows] = r.router_t[...].astype(F32)
    r.columns[experts : experts + 1, 0:rows] = r.gain_one[...].astype(F32)
    r.columns[experts + 1 : experts + 2, 0:rows] = r.gain_two[...].astype(F32)
    own_rows = jnp.transpose(r.columns[...])[:rows]
    r.columns[...] = jnp.zeros_like(r.columns)
    r.columns[0 : r.table.shape[0], 0:HEADS] = r.table[...].astype(F32)
    w_ref[mine, 3 * width : first] = (own_rows + pltpu.roll(r.columns[...], TABLE_AT, 1)[:rows]).astype(BF16)
    w_ref[mine, first:] = r.wo[...]

    def w_copy(part, owner, peer, start=0, count=rows):
        view = View(w_ref)[rows_of(owner, start, count), parts[part]]
        return send(view, view, DP, peer)

    w_own = [[w_copy(part, me, peer) for peer in (across, along, core)] for part in range(2)]

    d0, d1 = places_by_lane(r.routes_t[...], here, experts, local, cap)
    tall = iota((LANES, n), 0)
    named = jnp.where(tall == 0, r.routes_t[0:1, :], jnp.where(tall == 1, r.routes_t[1:2, :], 0))
    routes_ref[...] = jnp.transpose(named.astype(F32)).astype(I32)

    z_peers = [here ^ m for m in range(groups)]
    far_first = (2, 3, 1)

    def dispatch(l, values, out_ref, in_ref):
        for m in (*far_first, 0):
            cut = slice(m * cap, (m + 1) * cap)
            target = out_ref if m else in_ref
            target[l, cut, :] = put_rows(values, d0, d1, (m * local + l) * cap, cap)

    def z_send_rows(l, m, out_ref, in_ref):
        cut = slice(m * cap, (m + 1) * cap)
        return send(View(out_ref)[l, cut, :], View(in_ref)[l, cut, :], EXPERT, z_peers[m])

    cot_copies, row_copies = {}, {}
    for l in range(local):
        dispatch(l, cot_ref[...], r.out_a, r.cots)
        for m in far_first:
            if (l, m) != (local - 1, 3):
                cot_copies[l, m] = z_send_rows(l, m, r.out_a, r.cots)
    half = rows // 2
    w_passed = []
    for part in range(2):
        w_own[part][0].wait_recv()
        one = w_copy(part, across, along, 0, half)
        two = w_copy(part, across, core)
        w_own[part][1].wait_recv()
        three = w_copy(part, along, across, half, half)
        four = w_copy(part, along, core)
        w_passed.append((one, three, two, four))

    kinds = ((UP, r.up, r.up_a, r.up_b), (DOWN, r.down, r.down_a, r.down_b))
    weight_copies = {}

    def weights_out(l):
        for kind, own_ref, a_ref, b_ref in kinds:
            key = (l, kind)
            weight_copies[key, OWN] = move(View(own_ref)[l], View(a_ref)[l, 0])
            weight_copies[key, (A, 1)] = send(View(own_ref)[l], View(a_ref)[l, 1], DP, across)
            weight_copies[key, (A, 2)] = send(View(own_ref)[l], View(a_ref)[l, 2], DP, along)
            weight_copies[key, (B, 0)] = send(View(own_ref)[l], View(b_ref)[l, 0], DP, core)

    def weights_on(l):
        for kind, own_ref, a_ref, b_ref in kinds:
            key = (l, kind)
            at, peer = (1, along) if kind == UP else (2, across)
            weight_copies[key, (A, at)].wait_recv()
            weight_copies[key, (A, 3)] = send(View(a_ref)[l, at], View(a_ref)[l, 3], DP, peer)
            weight_copies[key, (B, at)] = send(View(a_ref)[l, at], View(b_ref)[l, at], DP, core)
        for kind, own_ref, a_ref, b_ref in kinds:
            key = (l, kind)
            at = 2 if kind == UP else 1
            weight_copies[key, (A, at)].wait_recv()
            weight_copies[key, (B, at)] = send(View(a_ref)[l, at], View(b_ref)[l, at], DP, core)

    def weights_last(l):
        for kind, own_ref, a_ref, b_ref in kinds:
            key = (l, kind)
            weight_copies[key, (A, 3)].wait_recv()
            weight_copies[key, (B, 3)] = send(View(a_ref)[l, 3], View(b_ref)[l, 3], DP, core)

    def weights_in(l):
        for kind, *_ in kinds:
            weight_copies[(l, kind), OWN].wait()
            for at in range(4):
                weight_copies[(l, kind), (B, at)].wait_recv()

    weights_out(0)
    v_t_ref = Window(r.gh, (), (width, n))

    def w_finish(part):
        one, three, two, four = w_passed[part]
        one.wait_recv()
        three.wait_recv()
        five = w_copy(part, diagonal, core)
        for copy in (w_own[part][2], two, four, five):
            copy.wait_recv()

    w_finish(0)

    project_inputs(
        experts, buckets, shards, tok_ref, w_ref, bucket_ref, r.q, r.k, r.v, r.normed_t, v_t_ref, r.line
    )
    attend(r.q, r.k, v_t_ref, r.line, r.twice, r.merged_t)
    w_finish(1)
    slots_out, slots_in = r.slots_out, r.slots_in
    route(
        experts, local, cap, here, tok_ref, w_ref, routes_ref, r.merged_t, r.middle, r.second, r.gates,
        [slots_out.at[m] for m in range(groups)],
    )
    slot_copies = [send(View(slots_out)[m], View(slots_in)[m], EXPERT, here ^ m) for m in range(1, groups)]
    slots_in[0] = slots_out[0]
    for l in range(local):
        dispatch(l, r.second[...], r.out_b, r.rows)
        if l == 0:
            for m in far_first:
                row_copies[l, m] = z_send_rows(l, m, r.out_b, r.rows)
    weights_on(0)
    weights_out(1)
    weights_last(0)
    for m in far_first:
        row_copies[0, m].wait_send()
    cot_copies[1, 3] = z_send_rows(1, 3, r.out_a, r.cots)
    for m in far_first:
        row_copies[1, m] = z_send_rows(1, m, r.out_b, r.rows)
    weights_in(0)
    for m in far_first:
        cot_copies[0, m].wait_recv()
        row_copies[0, m].wait_recv()
    for copy in slot_copies:
        copy.wait_recv()

    up_buf, down_buf, ug_buf, dg_buf, core_buf = r.up_buf, r.down_buf, r.ug_buf, r.dg_buf, r.core_buf
    gr_ref, act_ref, gh_ref, reply_ref, back_ref = r.gr, r.act, r.gh, r.reply, r.back
    total_rows = groups * cap
    core_sems, hop_sems = (r.core_send, r.core_recv), (r.hop_send, r.hop_recv)
    back_sems = (r.back_send, r.back_recv)
    halves = [slice(i * slab, (i + 1) * slab) for i in range(2)]

    def remote(src, dst, sems, at, axis, peer):
        return pltpu.make_async_remote_copy(
            src_ref=src, dst_ref=dst, send_sem=sems[0].at[at], recv_sem=sems[1].at[at],
            device_id={axis: peer}, device_id_type=MESH,
        )

    def fetches(l, g, a_side, wait=False):
        for i in range(2):
            at = i if wait else 2 * (3 - g) + i if a_side else 2 * g + i
            up, down = (r.up_a, r.down_a) if a_side else (r.up_b, r.down_b)
            slot = lax.rem(g, 2)
            yield pltpu.make_async_copy(up.at[l, at], up_buf.at[slot, :, halves[i]], r.fetch_sem.at[slot, i])
            yield pltpu.make_async_copy(down.at[l, at], down_buf.at[slot, halves[i], :], r.fetch_sem.at[slot, 2 + i])

    def fetch(l, g):
        for a_side in (False, True):

            @pl.when((g >= 2) == a_side)
            def _():
                for copy in fetches(l, g, a_side):
                    copy.start()

    def core_copies(l, slab_at, i, out):
        at = (l * 4 + slab_at) * 2
        yield remote(ug_buf.at[out, :, halves[i]], r.core_up.at[l, slab_at], core_sems, at, DP, core)
        yield remote(dg_buf.at[out, halves[i], :], r.core_down.at[l, slab_at], core_sems, at + 1, DP, core)

    def t_copy(l, kind, i, out, half_at):
        at = l * 4 + (0 if kind == UP else 2) + i
        if kind == UP:
            return remote(ug_buf.at[out, :, halves[half_at]], r.t_up.at[l, i], hop_sems, at, DP, along)
        return remote(dg_buf.at[out, halves[half_at], :], r.t_down.at[l, i], hop_sems, at, DP, across)

    def own_moves(l, out):
        yield pltpu.make_async_copy(ug_buf.at[out, :, halves[0]], r.own_up.at[l], r.own_sem.at[0])
        yield pltpu.make_async_copy(dg_buf.at[out, halves[0], :], r.own_down.at[l], r.own_sem.at[1])

    def kept_move(l, kind, out):
        if kind == UP:
            return pltpu.make_async_copy(ug_buf.at[out, :, halves[1]], r.keep_up.at[l], r.own_sem.at[2])
        return pltpu.make_async_copy(dg_buf.at[out, halves[0], :], r.keep_down.at[l], r.own_sem.at[3])

    def sent_from(l, g, out):
        def when(condition):
            return (lambda f: f() if condition else None) if isinstance(g, int) else pl.when(condition)

        @when(g < 2)
        def _():
            for i in range(2):
                for copy in core_copies(l, 2 * g + i, i, out):
                    copy.wait_send()

        @when(g == 2)
        def _():
            for copy in (t_copy(l, UP, 0, out, 0), t_copy(l, UP, 1, out, 1), t_copy(l, DOWN, 1, out, 1)):
                copy.wait_send()
            kept_move(l, DOWN, out).wait()

        @when(g == 3)
        def _():
            t_copy(l, DOWN, 0, out, 1).wait_send()
            for copy in (*own_moves(l, out), kept_move(l, UP, out)):
                copy.wait()

    def back_copy(l, m):
        cut = slice(m * cap, (m + 1) * cap)
        at = l * (groups - 1) + m - 1
        return remote(r.out_a.at[l, cut, :], r.backs.at[l, cut, :], back_sems, at, EXPERT, here ^ m)

    def dot_copy(l, m):
        at = (local + l) * (groups - 1) + m - 1
        return remote(r.dots_out.at[l, m], r.dots_in.at[l, m], back_sems, at, EXPERT, here ^ m)

    reply_copies = {}

    def reply_send(l, m):
        reply_copies[l, m] = z_send_rows(l, m, r.out_b, r.reply_in)

    def step(s, carry):
        l, g, out = lax.div(s, 4), lax.rem(s, 4), lax.rem(s, 3)
        slot = lax.rem(g, 2)
        x, cots = r.rows.at[l], r.cots.at[l]

        @pl.when(s == 1)
        def _():
            weights_on(1)

        @pl.when(s == 3)
        def _():
            weights_last(1)

        @pl.when(s == 4)
        def _():
            weights_in(1)
            for m in far_first:
                cot_copies[1, m].wait_recv()
                row_copies[1, m].wait_recv()

        @pl.when(s == 6)
        def _():
            for m in far_first:
                back_copy(0, m).wait_send()
            for m in (2, 1):
                reply_send(0, m)

        @pl.when(g == 0)
        def _():
            fetch(l, g)
            for m in range(groups):
                cut = slice(m * cap, (m + 1) * cap)
                slots = slots_in[m, pl.ds(l, 1), :]
                gate = jnp.transpose(jnp.broadcast_to(slots, (LANES, slots.shape[1])))[:cap, 0:1]
                gr_ref[cut, :] = (gate * cots[cut, :].astype(F32)).astype(BF16)
            core_buf[...] = jnp.zeros_like(core_buf)
            reply_ref[...] = jnp.zeros_like(reply_ref)
            back_ref[...] = jnp.zeros_like(back_ref)

        for copy in fetches(l, g, False, True):
            copy.wait()

        @pl.when(g < 3)
        def _():
            fetch(l, g + 1)

        def arrivals():
            for i in range(2):
                at = 2 * (3 - g) + i
                yield pltpu.make_async_copy(r.core_up.at[l, at], core_buf.at[0, :, halves[i]], r.add_sem.at[i])
                yield pltpu.make_async_copy(r.core_down.at[l, at], core_buf.at[1, halves[i], :], r.add_sem.at[2 + i])

        @pl.when(g >= 2)
        def _():
            for i in range(2):
                for copy in core_copies(l, 2 * (3 - g) + i, i, out):
                    copy.wait_recv()
            for copy in arrivals():
                copy.start()

        for cut in chunked(total_rows):
            act, slope = gelu_both(nn(x[cut, :], up_buf[slot]))
            act_ref[cut, :] = act.astype(BF16)
            gh_ref[cut, :] = (nt(gr_ref[cut, :], down_buf[slot]) * slope).astype(BF16)
            reply_ref[cut, :] += nn(act_ref[cut, :], down_buf[slot])
            back_ref[cut, :] += nt(gh_ref[cut, :], up_buf[slot])

        @pl.when(s >= 3)
        def _():
            sent_from(lax.div(s - 3, 4), lax.rem(s - 3, 4), out)

        @pl.when(g >= 2)
        def _():
            for copy in arrivals():
                copy.wait()

        for cut in chunked(width):
            ug = tn(x[:, cut], gh_ref[...]) + core_buf[0, cut, :].astype(F32)
            ug_buf[out, cut, :] = ug.astype(BF16)
            dg = tn(act_ref[:, cut], gr_ref[...]) + core_buf[1, cut, :].astype(F32)
            dg_buf[out, cut, :] = dg.astype(BF16)

        @pl.when(g < 2)
        def _():
            for i in range(2):
                for copy in core_copies(l, 2 * g + i, i, out):
                    copy.start()

        @pl.when(g == 2)
        def _():
            t_copy(l, UP, 0, out, 0).start()
            t_copy(l, UP, 1, out, 1).start()
            t_copy(l, DOWN, 1, out, 1).start()
            kept_move(l, DOWN, out).start()

        @pl.when(g == 3)
        def _():
            t_copy(l, DOWN, 0, out, 1).start()
            for copy in own_moves(l, out):
                copy.start()
            kept_move(l, UP, out).start()
            for which in range(local):

                @pl.when(l == which)
                def _():
                    for m in far_first:
                        cot_copies[which, m].wait_send()
                        if which:
                            row_copies[which, m].wait_send()

            for m in range(groups):
                cut = slice(m * cap, (m + 1) * cap)
                if m == 0:
                    r.backs[l, cut, :] = back_ref[cut, :].astype(BF16)
                else:
                    r.out_a[l, cut, :] = back_ref[cut, :].astype(BF16)
                    back_copy(l, m).start()
            reply = reply_ref[...].astype(BF16)
            r.out_b[l] = reply
            dots = jnp.sum(reply.astype(F32) * cots[...].astype(F32), axis=1, keepdims=True)
            dots = jnp.transpose(jnp.broadcast_to(dots, (total_rows, LANES)))[0:8]
            r.dots_in[l, 0] = dots[:, :256]
            for m in range(1, groups):
                r.dots_out[l, m] = pltpu.roll(dots, total_rows - m * cap, 1)[:, :256]
                dot_copy(l, m).start()

        return carry

    lax.fori_loop(0, 4 * local, step, 0)
    links.forget([*cot_copies.values(), *row_copies.values()])
    v_copies = {}

    def t_stage(l):
        t_copy(l, UP, 1, 0, 1).wait_recv()
        t_copy(l, DOWN, 1, 0, 1).wait_recv()
        return [
            move(View(r.t_up)[l, 1], View(up_buf)[l, :, :slab]),
            move(View(r.t_down)[l, 1], View(down_buf)[l, :slab, :]),
            move(View(r.keep_up)[l], View(up_buf)[l, :, slab:]),
            move(View(r.keep_down)[l], View(down_buf)[l, slab:, :]),
        ]

    def t_pass(l, staged):
        for copy in staged:
            copy.wait()
        up_sum = up_buf[l, :, slab:].astype(F32) + up_buf[l, :, :slab].astype(F32)
        up_buf[l, :, :slab] = up_sum.astype(BF16)
        v_copies[l, UP] = send(View(up_buf)[l, :, :slab], View(r.v_up)[l], DP, across)
        down_sum = down_buf[l, slab:, :].astype(F32) + down_buf[l, :slab, :].astype(F32)
        down_buf[l, :slab, :] = down_sum.astype(BF16)
        v_copies[l, DOWN] = send(View(down_buf)[l, :slab, :], View(r.v_down)[l], DP, along)

    t_pass(0, t_stage(0))

    for l in range(local):
        for m in range(1, groups):
            back_copy(l, m).wait_recv()
            if l:
                back_copy(l, m).wait_send()
            dot_copy(l, m).wait()
    for l, m in ((0, 3), (1, 2), (1, 3), (1, 1)):
        reply_send(l, m)
    order = [(m, l) for m in range(groups) for l in range(local)]
    gm_ref, gk_ref = Window(r.rows, (0,), (n, width)), Window(r.rows, (1,), (n, width))
    gv_ref, k_t_ref = Window(r.cots, (0,), (n, width)), v_t_ref
    gq_t_ref, gmid_ref = Window(gr_ref, (), (width, n)), Window(reply_ref, (), (n, width))
    branch_ref, normed_t = Window(act_ref, (), (n, width)), r.normed_t
    router_grad, midnorm_grad = middle_back(
        experts, local, cap, here, w_ref, routes_ref, cot_ref, r.middle, r.second, r.gates,
        [Window(r.backs.at[l, m * cap : (m + 1) * cap, :], (), (cap, width)) for m, l in order],
        [r.dots_in.at[l, m] for m, l in order],
        gmid_ref, branch_ref,
    )
    r.gain_row[0:1, :] = midnorm_grad
    r.router_grad[...] = router_grad
    part = width // 2
    chunk_at = (2, 0)
    for at in range(4 * local - 3, 4 * local):
        sent_from(at // 4, at % 4, at % 3)
    for c in range(2):
        for cut in chunked(width):
            project = nn(r.merged_t[cut, :], branch_ref[:, c * part : (c + 1) * part])
            dg_buf[chunk_at[c], cut, part:] = project.astype(BF16)
    for cut in chunked(n):
        gm_ref[cut, :] = nt(branch_ref[cut, :], w_ref[:, first:]).astype(BF16)
    k_t_ref[...] = jnp.transpose(r.k[...])

    def weight_grads(c):
        at, columns = chunk_at[c], slice(c * part, (c + 1) * part)
        for cut in chunked(width):
            ug_buf[at, cut, :part] = nt(normed_t[cut, :], gq_t_ref[columns, :]).astype(BF16)
            ug_buf[at, cut, part:] = nn(normed_t[cut, :], gk_ref[:, columns]).astype(BF16)
            dg_buf[at, cut, :part] = nn(normed_t[cut, :], gv_ref[:, columns]).astype(BF16)

    peers = [me ^ mask for mask in range(8)]
    rows_at = [rows_of(peer) for peer in peers]

    class Reduce:
        def __init__(self, pieces):
            self.pieces = pieces

        def start(self):
            self.zero = []
            for g, from_core, *_ in self.pieces:
                for i in (2, 3, 1, 0):
                    copy = send(g.view(rows_at[1 ^ (2 * i)]), from_core.view(i), DP, peers[1])
                    self.zero.append((i, g, from_core, copy))

        def one(self):
            for i, g, from_core, copy in self.zero:
                copy.wait_recv()
                at = rows_at[2 * i]
                g[at, :] = (g[at, :].astype(F32) + from_core[i].astype(F32)).astype(BF16)
            self.hops = []
            for g, _, hop_one, _, mask in self.pieces:
                for i, owner in enumerate((mask, 6)):
                    self.hops.append(send(g.view(rows_at[owner]), hop_one.view(i), DP, peers[mask]))

        def two(self):
            for copy in self.hops:
                copy.wait_recv()
            self.last = []
            for g, _, hop_one, hop_two, mask in self.pieces:
                at = rows_at[6 - mask]
                g[at, :] = (g[at, :].astype(F32) + hop_one[1].astype(F32)).astype(BF16)
                self.last.append(send(g.view(at), hop_two.view(), DP, peers[6 - mask]))

        def three(self):
            for copy in self.last:
                copy.wait_recv()
            return [
                g[rows_at[0], :].astype(F32) + hop_one[0].astype(F32) + hop_two[...].astype(F32)
                for g, _, hop_one, hop_two, _ in self.pieces
            ]

    def window(ref, *lead):
        return Window(ref, lead, ref.shape[len(lead) :])

    chunks = [
        Reduce(
            [
                (window(ug_buf, chunk_at[c]), window(r.core_a, c), window(r.hop_a, c), window(r.last_a, c), 4),
                (window(dg_buf, chunk_at[c]), window(r.core_b, c), window(r.hop_b, c), window(r.last_b, c), 2),
            ]
        )
        for c in range(2)
    ]
    little = Reduce([(window(r.little), window(r.core_c), window(r.hop_c), window(r.last_c), 4)])
    z_copies, g_copies = {}, {}
    share = pl.ds(pl.multiple_of(here * part, LANES), part)

    def z_send(c):
        a, b = chunks[c].three()
        r.sum[c, :, :width] = a.astype(BF16)
        r.sum[c, :, width:] = b.astype(BF16)
        z_copies[c] = []
        for m in range(1, groups):
            cut = pl.ds(pl.multiple_of((here ^ m) * part, LANES), part)
            z_copies[c].append(send(View(r.sum)[c, :, cut], View(r.z_in)[c, m], EXPERT, here ^ m))

    def z_gather(c):
        total = r.sum[c, :, share].astype(F32)
        for m in range(1, groups):
            z_copies[c][m - 1].wait_recv()
            total += r.z_in[c, m].astype(F32)
        r.z_sum[c] = total.astype(BF16)
        g_copies[c] = [
            send(View(r.z_sum)[c], View(r.z_all)[c, m], EXPERT, here ^ m) for m in range(1, groups)
        ]
        r.main[here, :, c * part : (c + 1) * part] = r.z_sum[c]

    def z_finish(c):
        for m in range(1, groups):
            g_copies[c][m - 1].wait_recv()
            r.main[here ^ m, :, c * part : (c + 1) * part] = r.z_all[c, m]

    def after(hp):
        @pl.when(hp == 2)
        def _():
            weight_grads(0)
            chunks[0].start()

        @pl.when(hp == 3)
        def _():
            chunks[0].one()
            t_pass(1, t_stage(1))

        @pl.when(hp == 4)
        def _():
            chunks[0].two()

    attend_back(after, r.q, r.k, r.v, gm_ref, k_t_ref, r.line, r.twice, gq_t_ref, gk_ref, gv_ref, r.fold)
    weight_grads(1)
    chunks[1].start()
    z_send(0)
    prenorm_grad = inputs_back(experts, tok_ref, w_ref, gq_t_ref, gk_ref, gv_ref, gmid_ref, gm_ref)
    results = [move(gm_ref.view(), View(r.inputs_grad))]
    chunks[1].one()
    z_gather(0)
    table = table_back(buckets, shards, width, bucket_ref, r.fold)
    r.little[...] = small_grads(
        experts, r.router_grad[...], prenorm_grad, r.gain_row[0:1, :], table
    )
    little.start()
    chunks[1].two()
    little.one()
    z_finish(0)
    z_send(1)
    layer_out_ref = Window(r.cots, (1,), (n, width))
    c0, c1, _, _ = places_by_row(routes_ref[...], here, local, cap)

    def add_replies(which, first=False, last=False):
        moves = []
        for l, m in which:
            if m:
                cut = slice(m * cap, (m + 1) * cap)
                reply_copies[l, m].wait_recv()
                moves.append(move(View(r.reply_in)[l, cut, :], View(core_buf)[l, cut, :]))
        for copy in moves:
            copy.wait()
        for cut in chunked(n):
            count = cut.stop - cut.start
            picked0 = jnp.zeros((count, width), F32)
            picked1 = jnp.zeros((count, width), F32)
            for l, m in which:
                reply = (core_buf if m else r.out_b)[l, m * cap : (m + 1) * cap, :]
                lane = iota((count, cap), 1) + (m * local + l) * cap
                picked0 += nn(hot(lane == c0[cut]), reply)
                picked1 += nn(hot(lane == c1[cut]), reply)
            total = r.gates[cut, 0:1] * picked0 + r.gates[cut, 1:2] * picked1
            total += (r.middle if first else gmid_ref)[cut, :]
            if last:
                layer_out_ref[cut, :] = total.astype(BF16)
            else:
                gmid_ref[cut, :] = total

    add_replies([(0, 0), (1, 0), (0, 2), (0, 1)], first=True)
    little.two()
    z_gather(1)
    (small_sum,) = little.three()
    r.small_z[here] = small_sum.astype(BF16)
    small_copies = [
        send(View(r.small_z)[here], View(r.small_z)[here], EXPERT, z_peers[m]) for m in range(1, groups)
    ]
    add_replies([(0, 3)])
    add_replies([(1, 2), (1, 3), (1, 1)], last=True)
    results.append(move(layer_out_ref.view(), View(r.layer_out)))
    z_finish(1)
    for copy in small_copies:
        copy.wait_recv()
    total = r.small_z[0].astype(F32)
    for m in range(1, groups):
        total += r.small_z[m].astype(F32)
    turned = jnp.transpose(jnp.concatenate([total, jnp.zeros((LANES - rows, LANES), F32)], axis=0))
    r.router_out[...] = turned[0:experts, :rows]
    r.gains_out[...] = turned[experts : experts + 2, :rows]
    r.table_out[...] = pltpu.roll(total, LANES - TABLE_AT, 1)[0 : r.table.shape[0], 0:HEADS]
    for l in range(local):
        for kind in (UP, DOWN):
            t_copy(l, kind, 0, 0, 0).wait_recv()
            v_copies[l, kind].wait_recv()
    for copy in results:
        copy.wait()
    links.close()


def whole_layer(
    tokens, query_weight, key_weight, value_weight, project_weight, router_weight, prenorm_gain, midnorm_gain, bias_table,
    up_weight, down_weight, routes, bucket_row, cotangent,
):
    experts, table_rows_own = router_weight.shape[1], bias_table.shape[0]
    n, width = tokens.shape
    shards, groups = lax.axis_size(DP), lax.axis_size(EXPERT)
    local, _, slab = up_weight.shape
    buckets = table_rows_own * shards
    cap = 3 * n // experts
    rows = query_weight.shape[0]
    total = groups * cap
    vmem, hbm = pl.BlockSpec(memory_space=pltpu.VMEM), pl.BlockSpec(memory_space=pl.ANY)

    def array(*s, dtype=BF16):
        return jax.ShapeDtypeStruct(s, dtype)

    inputs = dict(
        tok=tokens, wq=query_weight, wk=key_weight, wv=value_weight, wo=project_weight,
        router_t=router_weight.T, gain_one=prenorm_gain[None, :], gain_two=midnorm_gain[None, :], table=bias_table,
        routes_t=routes.T, bucket=bucket_row, cot=cotangent, up=up_weight, down=down_weight,
    )
    near = dict(
        main=array(4, rows, width),
        router_out=array(experts, rows, dtype=F32),
        gains_out=array(2, rows, dtype=F32),
        table_out=array(table_rows_own, HEADS, dtype=F32),
    )
    far = dict(
        layer_out=array(n, width),
        inputs_grad=array(n, width),
        own_up=array(local, width, slab),
        own_down=array(local, slab, width),
        keep_up=array(local, width, slab),
        keep_down=array(local, slab, width),
        t_up=array(local, 2, width, slab),
        t_down=array(local, 2, slab, width),
        v_up=array(local, width, slab),
        v_down=array(local, slab, width),
        up_a=array(local, 4, width, slab),
        up_b=array(local, 4, width, slab),
        down_a=array(local, 4, slab, width),
        down_b=array(local, 4, slab, width),
        core_up=array(local, 4, width, slab),
        core_down=array(local, 4, slab, width),
        reply_in=array(local, total, width),
    )
    v, part = pltpu.VMEM, width // 2
    scratch = dict(
        w=v((width, 4 * width + LANES), BF16),
        out_a=v((local, total, width), BF16),
        out_b=v((local, total, width), BF16),
        rows=v((local, total, width), BF16),
        cots=v((local, total, width), BF16),
        backs=v((local, total, width), BF16),
        slots_out=v((groups, 8, 256), F32),
        slots_in=v((groups, 8, 256), F32),
        dots_out=v((local, groups, 8, 256), F32),
        dots_in=v((local, groups, 8, 256), F32),
        q=v((n, width), BF16),
        k=v((n, width), BF16),
        v=v((n, width), BF16),
        normed_t=v((width, n), BF16),
        second=v((n, width), BF16),
        merged_t=v((width, n), BF16),
        middle=v((n, width), F32),
        gates=v((n, LANES), F32),
        routes_by_row=v((n, LANES), I32),
        columns=v((LANES, LANES), F32),
        line=v((16, n), F32),
        twice=v((LANES, 2 * n), F32),
        fold=v((HEADS, 8, n), F32),
        gr=v((total, width), BF16),
        act=v((total, width), BF16),
        gh=v((total, width), BF16),
        reply=v((total, width), F32),
        back=v((total, width), F32),
        up_buf=v((2, width, width), BF16),
        down_buf=v((2, width, width), BF16),
        ug_buf=v((3, width, width), BF16),
        dg_buf=v((3, width, width), BF16),
        core_buf=v((2, width, width), BF16),
        core_a=v((2, 4, rows, width), BF16),
        core_b=v((2, 4, rows, width), BF16),
        hop_a=v((2, 2, rows, width), BF16),
        hop_b=v((2, 2, rows, width), BF16),
        last_a=v((2, rows, width), BF16),
        last_b=v((2, rows, width), BF16),
        sum=v((2, rows, 2 * width), BF16),
        z_in=v((2, groups, rows, part), BF16),
        z_sum=v((2, rows, part), BF16),
        z_all=v((2, groups, rows, part), BF16),
        little=v((width, LANES), BF16),
        gain_row=v((8, width), F32),
        router_grad=v((width, LANES), F32),
        core_c=v((4, rows, LANES), BF16),
        hop_c=v((2, rows, LANES), BF16),
        last_c=v((rows, LANES), BF16),
        small_z=v((groups, rows, LANES), BF16),
        send_sem=pltpu.SemaphoreType.DMA((SENDS,)),
        recv_sem=pltpu.SemaphoreType.DMA((SENDS,)),
        local_sem=pltpu.SemaphoreType.DMA((MOVES,)),
        fetch_sem=pltpu.SemaphoreType.DMA((2, 4)),
        add_sem=pltpu.SemaphoreType.DMA((4,)),
        own_sem=pltpu.SemaphoreType.DMA((4,)),
        core_send=pltpu.SemaphoreType.DMA((8 * local,)),
        core_recv=pltpu.SemaphoreType.DMA((8 * local,)),
        hop_send=pltpu.SemaphoreType.DMA((4 * local,)),
        hop_recv=pltpu.SemaphoreType.DMA((4 * local,)),
        back_send=pltpu.SemaphoreType.DMA((2 * local * (groups - 1),)),
        back_recv=pltpu.SemaphoreType.DMA((2 * local * (groups - 1),)),
    )
    names = [*inputs, *near, *far, *scratch]
    outs = pl.pallas_call(
        functools.partial(layer_kernel, experts, local, cap, buckets, shards, names),
        name="layer",
        out_shape=[*near.values(), *far.values()],
        in_specs=[vmem] * (len(inputs) - 2) + [hbm] * 2,
        out_specs=[vmem] * len(near) + [hbm] * len(far),
        scratch_shapes=[*scratch.values()],
        compiler_params=pltpu.CompilerParams(
            vmem_limit_bytes=LAYER_VMEM, collective_id=0, has_side_effects=True
        ),
        cost_estimate=pl.CostEstimate(flops=60 * 10**9, bytes_accessed=400 * 10**6, transcendentals=0),
    )(*inputs.values())
    o = SimpleNamespace(**dict(zip([*near, *far], outs)))

    def total_of(own, first_hop, last_hop):
        return own.astype(F32) + first_hop[:, 0].astype(F32) + last_hop.astype(F32)

    return (
        o.layer_out,
        o.inputs_grad,
        o.main[0].astype(F32),
        o.main[1].astype(F32),
        o.main[2].astype(F32),
        o.main[3].astype(F32),
        o.router_out.T,
        o.gains_out[0],
        o.gains_out[1],
        o.table_out,
        total_of(o.own_up, o.t_up, o.v_up),
        total_of(o.own_down, o.t_down, o.v_down),
    )


def swap(value, axis, bit):
    return lax.ppermute(value, axis, [(i, i ^ bit) for i in range(lax.axis_size(axis))])


def swap_all(values):
    return [v if m == 0 else swap(v, EXPERT, m) for m, v in enumerate(values)]


def body(
    tokens,
    query_weight,
    key_weight,
    value_weight,
    project_weight,
    router_weight,
    prenorm_gain,
    midnorm_gain,
    bias_table,
    up_weight,
    down_weight,
    routes,
    bucket_index,
    cotangent,
):
    n, width = tokens.shape
    experts = router_weight.shape[1]
    shards, groups = lax.axis_size(DP), lax.axis_size(EXPERT)
    local, _, slab = up_weight.shape
    cap = 3 * n // experts
    buckets = bias_table.shape[0] * shards
    own_rows = query_weight.shape[0]
    hidden = slab * shards
    direct = slab % LANES == 0 and shards == 8
    here = lax.axis_index(EXPERT).astype(I32).reshape(1)
    smem = pl.BlockSpec(memory_space=pltpu.SMEM)
    vmem = pl.BlockSpec(memory_space=pltpu.VMEM)
    hbm = pl.BlockSpec(memory_space=pl.ANY)
    routes_t = routes.T
    bucket_row = bucket_index[None, :]

    def shape(s, dtype=BF16):
        return jax.ShapeDtypeStruct(s, dtype)

    if direct:
        return whole_layer(
            tokens, query_weight, key_weight, value_weight, project_weight, router_weight, prenorm_gain, midnorm_gain,
            bias_table, up_weight, down_weight, routes, bucket_row, cotangent,
        )
    small = jnp.concatenate(
        [
            router_weight,
            prenorm_gain[:, None],
            midnorm_gain[:, None],
            jnp.zeros((own_rows, TABLE_AT - experts - 2), BF16),
            jnp.pad(bias_table, ((0, own_rows - bias_table.shape[0]), (0, 0))),
            jnp.zeros((own_rows, LANES - TABLE_AT - HEADS), BF16),
        ],
        axis=1,
    )
    packed_width = 4 * width + LANES
    slots_shape = (groups, 8, 256)
    kept = [shape((n, width))] * 3 + [
        shape((width, n)),
        shape((width, n)),
        shape((n, width), F32),
        shape((n, width)),
        shape((n, LANES), F32),
        shape((16, n), F32),
    ]
    packed = jnp.concatenate(
        [query_weight, key_weight, value_weight, small, project_weight], axis=1
    )
    full = lax.all_gather(packed, DP, axis=0, tiled=True)
    cot_out = vmem_call(
        functools.partial(scatter_kernel, experts, local, cap),
        "send_cotangent",
        [shape((cap, width))] * experts,
        specs=[smem, vmem, vmem],
    )(here, routes_t, cotangent)
    up_all = lax.all_gather(up_weight, DP, axis=2, tiled=True)
    down_all = lax.all_gather(down_weight, DP, axis=1, tiled=True)
    up_all = up_all.reshape(local, width, hidden // width, width).transpose(0, 2, 1, 3)
    down_all = down_all.reshape(local, hidden // width, width, width)
    cut = hidden // width // 2
    weights = (up_all[:, :cut], up_all[:, cut:], down_all[:, :cut], down_all[:, cut:])
    forward = vmem_call(
        functools.partial(forward_kernel, experts, local, cap, buckets, shards),
        "attention_forward",
        kept + [shape((cap, width))] * experts + [shape((8, 256), F32)] * groups,
        scratch=[pltpu.VMEM((width, n), BF16), pltpu.VMEM((LANES, 2 * n), F32)],
        specs=[smem] + [vmem] * 5,
    )(here, tokens, full, routes, routes_t, bucket_row)
    q, k, v, normed, merged_t, middle, second, gates, line = forward[:9]
    x_out, slots_out = forward[9 : 9 + experts], forward[9 + experts :]
    slots_in = jnp.stack(swap_all(slots_out))
    x_in = jnp.stack([jnp.stack(swap_all(x_out[l::local])) for l in range(local)])
    cot_in = jnp.stack([jnp.stack(swap_all(cot_out[l::local])) for l in range(local)])

    rows = groups * cap
    replies, backs, dots, up_grads, down_grads = [], [], [], [], []
    for l in range(local):
        count, slab_width = weights[0].shape[1], weights[0].shape[3]
        per = width // slab_width
        outs = pl.pallas_call(
            functools.partial(expert_kernel, l, groups, cap),
            name=EXPERT,
            out_shape=[shape((cap, width))] * (2 * groups)
            + [shape((8, 256), F32)] * groups
            + [shape((count, width, slab_width))] * 2
            + [shape((count, slab_width, width))] * 2,
            in_specs=[hbm, hbm, vmem] + [hbm] * 4,
            out_specs=[vmem] * (3 * groups) + [hbm] * 4,
            scratch_shapes=[
                pltpu.VMEM((rows, width), BF16),
                pltpu.VMEM((width, rows), BF16),
                pltpu.VMEM((rows, width), BF16),
                pltpu.VMEM((rows, width), BF16),
                pltpu.VMEM((rows, width), F32),
                pltpu.VMEM((rows, width), F32),
                pltpu.VMEM((2, width, width), BF16),
                pltpu.VMEM((2, width, width), BF16),
                pltpu.VMEM((2, width, width), BF16),
                pltpu.VMEM((2, width, width), BF16),
                pltpu.VMEM((rows, width), BF16),
                pltpu.VMEM((rows, width), BF16),
                pltpu.SemaphoreType.DMA((2, 2 * per)),
                pltpu.SemaphoreType.DMA((2, 2 * per)),
                pltpu.SemaphoreType.DMA((2, groups)),
            ],
            compiler_params=pltpu.CompilerParams(vmem_limit_bytes=VMEM_LIMIT),
            cost_estimate=pl.CostEstimate(
                flops=12 * rows * width * hidden, bytes_accessed=40 * 10**6, transcendentals=0
            ),
        )(x_in, cot_in, slots_in, *weights)
        replies.append(outs[:groups])
        backs.append(swap_all(outs[groups : 2 * groups]))
        dots.append(swap_all(outs[2 * groups : 3 * groups]))
        ug, dg = outs[3 * groups : 3 * groups + 2], outs[3 * groups + 2 :]
        ug = jnp.concatenate(ug, axis=0).transpose(1, 0, 2).reshape(width, hidden)
        dg = jnp.concatenate(dg, axis=0).reshape(hidden, width)
        up_grads.append(lax.psum_scatter(ug, DP, scatter_dimension=1, tiled=True).astype(F32))
        down_grads.append(lax.psum_scatter(dg, DP, scatter_dimension=0, tiled=True).astype(F32))

    flat = lambda parts: [parts[l][m] for m in range(groups) for l in range(local)]
    inputs_grad, grads = vmem_call(
        functools.partial(backward_kernel, experts, local, cap, buckets, shards),
        "attention_backward",
        [shape((n, width)), shape((width, packed_width))],
        scratch=[
            pltpu.VMEM((n, width), BF16),
            pltpu.VMEM((n, width), F32),
            pltpu.VMEM((width, n), BF16),
            pltpu.VMEM((width, n), BF16),
            pltpu.VMEM((n, width), BF16),
            pltpu.VMEM((n, width), BF16),
            pltpu.VMEM((HEADS, 8, n), F32),
            pltpu.VMEM((LANES, 2 * n), F32),
            pltpu.VMEM((n, width), BF16),
        ],
        specs=[smem] + [vmem] * (14 + 2 * experts),
        flops=40 * 10**9,
        moved=30 * 10**6,
    )(
        here,
        tokens,
        full,
        routes,
        bucket_row,
        cotangent,
        q,
        k,
        v,
        normed,
        merged_t,
        middle,
        second,
        gates,
        line,
        *flat(backs),
        *flat(dots),
    )
    shares = lax.psum_scatter(grads, DP, scatter_dimension=0, tiled=True)
    totals = lax.psum(shares, EXPERT).astype(F32)

    replies = flat([swap_all(r) for r in replies])
    layer_out = vmem_call(
        functools.partial(combine_kernel, local, cap),
        "layer_out",
        shape((n, width)),
        specs=[smem] + [vmem] * (3 + experts),
        flops=4 * n * experts * cap * width,
        moved=6 * 10**6,
    )(here, routes, gates, middle, *replies)

    at = 3 * width
    return (
        layer_out,
        inputs_grad,
        totals[:, :width],
        totals[:, width : 2 * width],
        totals[:, 2 * width : 3 * width],
        totals[:, at + LANES :],
        totals[:, at : at + experts],
        totals[:, at + experts],
        totals[:, at + experts + 1],
        totals[: bias_table.shape[0], at + TABLE_AT : at + TABLE_AT + HEADS],
        jnp.stack(up_grads),
        jnp.stack(down_grads),
    )


def solution(mesh):
    both, first = P((DP, EXPERT), None), P(DP, None)
    up, down = P(EXPERT, None, DP), P(EXPERT, DP, None)
    return jax.shard_map(
        body,
        mesh=mesh,
        in_specs=(both,)
        + (first,) * 5
        + (P(DP), P(DP), first, up, down, both, P(), both),
        out_specs=(both, both) + (first,) * 5 + (P(DP), P(DP), first, up, down),
        check_vma=False,
    )
```

```python
import functools
from types import SimpleNamespace

import jax
import jax.numpy as jnp
from jax import lax
from jax.experimental import pallas as pl
from jax.experimental.pallas import tpu as pltpu
from jax.sharding import PartitionSpec as P

HEADS = 12
HEAD_DIM = 64
EPSILON = 1e-06
NEGATIVE = -1e30
SCALE = HEAD_DIM ** (-0.5)
LANES = 128
TABLE_AT = 32
QBLOCK = 256
F32 = jnp.float32
BF16 = jnp.bfloat16
I32 = jnp.int32
VMEM_LIMIT = 60 * 1024 * 1024
LAYER_VMEM = 63 * 1024 * 1024
MESH = pl.DeviceIdType.MESH
DP, EXPERT = "dp", "expert"
UP, DOWN, OWN, A, B = range(5)


def nn(left, right):
    return lax.dot_general(left, right, (((1,), (0,)), ((), ())), preferred_element_type=F32)


def nt(left, right):
    return lax.dot_general(left, right, (((1,), (1,)), ((), ())), preferred_element_type=F32)


def tn(left, right):
    return lax.dot_general(left, right, (((0,), (0,)), ((), ())), preferred_element_type=F32)


def iota(shape, axis):
    return lax.broadcasted_iota(I32, shape, axis)


def hot(mask):
    return jnp.where(mask, 1.0, 0.0).astype(BF16)


def vmem_call(body, name, out_shape, scratch=(), flops=0, moved=0, specs=None):
    def call(*args):
        in_specs = specs or [pl.BlockSpec(memory_space=pltpu.VMEM)] * len(args)
        return pl.pallas_call(
            body,
            name=name,
            out_shape=out_shape,
            in_specs=in_specs,
            out_specs=jax.tree.map(lambda _: pl.BlockSpec(memory_space=pltpu.VMEM), out_shape),
            scratch_shapes=scratch,
            compiler_params=pltpu.CompilerParams(vmem_limit_bytes=VMEM_LIMIT),
            cost_estimate=pl.CostEstimate(flops=flops, bytes_accessed=moved, transcendentals=0),
        )(*args)

    return call


def places(r, slot, here, local, cap):
    owner = lax.div(r, local)
    return (owner ^ here) * (local * cap) + lax.rem(r, local) * cap + slot.astype(I32)


def places_by_lane(routes_t, here, experts, local, cap):
    n = routes_t.shape[1]
    r0, r1 = routes_t[0:1, :], routes_t[1:2, :]
    tall = iota((-(-experts // 16) * 16, n), 0)
    oh0, oh1 = tall == r0, tall == r1
    earlier = hot(iota((n, n), 0) < iota((n, n), 1))
    count = nn(hot(oh0 | oh1), earlier)
    s0 = jnp.sum(jnp.where(oh0, count, 0.0), axis=0, keepdims=True)
    s1 = jnp.sum(jnp.where(oh1, count, 0.0), axis=0, keepdims=True)
    return places(r0, s0, here, local, cap), places(r1, s1, here, local, cap)


def places_by_row(routes, here, local, cap):
    n = routes.shape[0]
    r0, r1 = routes[:, 0:1], routes[:, 1:2]
    wide = iota((n, LANES), 1)
    oh0, oh1 = wide == r0, wide == r1
    earlier = hot(iota((n, n), 1) < iota((n, n), 0))
    count = nn(earlier, hot(oh0 | oh1))
    s0 = jnp.sum(jnp.where(oh0, count, 0.0), axis=1, keepdims=True)
    s1 = jnp.sum(jnp.where(oh1, count, 0.0), axis=1, keepdims=True)
    return places(r0, s0, here, local, cap), places(r1, s1, here, local, cap), oh0, oh1


def put_rows(values, d0, d1, start, count):
    at = iota((count, values.shape[0]), 0) + start
    return nn(hot((at == d0) | (at == d1)), values).astype(BF16)


def scatter_kernel(experts, local, cap, here_ref, routes_t_ref, values_ref, *out_refs):
    d0, d1 = places_by_lane(routes_t_ref[...], here_ref[0], experts, local, cap)
    values = values_ref[...]
    for at, out_ref in enumerate(out_refs):
        out_ref[...] = put_rows(values, d0, d1, at * cap, cap)


def table_rows(misc, buckets, shards):
    depth = misc.shape[0]
    per, rows = buckets // shards, depth // shards
    b = iota((buckets, depth), 0)
    select = hot(iota((buckets, depth), 1) == lax.div(b, per) * rows + lax.rem(b, per))
    return nn(select, misc)


def toeplitz(line, twice_ref):
    n = line.shape[1]
    rolled = pltpu.roll(jnp.broadcast_to(line, (LANES, n)), 0, 1, stride=1, stride_axis=0)
    twice_ref[:, :n] = rolled
    twice_ref[:, n:] = rolled


def bias_columns(twice_ref, n, block, rows):
    parts = []
    for jb in range(rows // LANES):
        start = (block * QBLOCK - jb * LANES) % n
        parts.append(twice_ref[:, start : start + QBLOCK])
    return jnp.concatenate(parts, axis=0)


def causal(scores, block):
    last = scores.shape[0] - QBLOCK
    keep = iota((QBLOCK, QBLOCK), 0) <= iota((QBLOCK, QBLOCK), 1)
    tail = jnp.where(keep, scores[last:], NEGATIVE)
    return tail if last == 0 else jnp.concatenate([scores[:last], tail], axis=0)


def chunked(count, size=256):
    return [slice(at, at + size) for at in range(0, count, size)]


def project_inputs(experts, buckets, shards, tok_ref, w_ref, bucket_ref, q_ref, k_ref, v_ref, normed_t_ref, v_t_ref, line_ref):
    n, width = tok_ref.shape
    misc = w_ref[:, 3 * width : 3 * width + LANES]
    gain = jnp.transpose(misc.astype(F32))[experts : experts + 1]
    for cut in chunked(n):
        x = tok_ref[cut, :].astype(F32)
        normed = x * lax.rsqrt(jnp.mean(x * x, axis=-1, keepdims=True) + EPSILON) * gain
        normed = normed.astype(BF16)
        normed_t_ref[:, cut] = jnp.transpose(normed)
        query = nn(normed, w_ref[:, :width]).astype(BF16)
        q_ref[cut, :] = (query.astype(F32) * SCALE).astype(BF16)
        k_ref[cut, :] = nn(normed, w_ref[:, width : 2 * width]).astype(BF16)
        value = nn(normed, w_ref[:, 2 * width : 3 * width]).astype(BF16)
        v_ref[cut, :] = value
        v_t_ref[:, cut] = jnp.transpose(value)
    table = table_rows(misc, buckets, shards).astype(BF16)
    by_bucket = hot(iota((buckets, n), 0) == bucket_ref[...])
    line_ref[...] = tn(table, by_bucket)[TABLE_AT : TABLE_AT + 16]


def attend(q_ref, k_ref, v_t_ref, line_ref, twice_ref, merged_t_ref):
    n = q_ref.shape[0]
    half = iota((1, LANES), 1) < HEAD_DIM

    def pair(hp, carry):
        lanes = pl.ds(pl.multiple_of(hp * LANES, LANES), LANES)
        kp, qp = k_ref[:, lanes], q_ref[:, lanes]
        for side in range(2):
            toeplitz(line_ref[pl.ds(hp * 2 + side, 1), :], twice_ref)
            keys = kp * hot(half if side == 0 else ~half)
            at = pl.ds(pl.multiple_of(hp * LANES + side * HEAD_DIM, HEAD_DIM), HEAD_DIM)
            for block in range(n // QBLOCK):
                rows = (block + 1) * QBLOCK
                cols = slice(block * QBLOCK, rows)
                scores = nt(keys[:rows], qp[cols]) + bias_columns(twice_ref, n, block, rows)
                scores = causal(scores, block)
                top = jnp.max(scores, axis=0, keepdims=True)
                e = jnp.exp(scores - top)
                probs = (e * (1.0 / jnp.sum(e, axis=0, keepdims=True))).astype(BF16)
                merged_t_ref[at, cols] = nn(v_t_ref[at, :rows], probs).astype(BF16)
        return carry

    lax.fori_loop(0, HEADS // 2, pair, 0)


def route(experts, local, cap, here, tok_ref, w_ref, routes_ref, merged_t_ref, middle_ref, second_ref, gates_ref, slot_refs):
    n, width = tok_ref.shape
    misc = w_ref[:, 3 * width : 3 * width + LANES]
    gain = jnp.transpose(misc.astype(F32))[experts + 1 : experts + 2]
    for cut in chunked(n):
        middle = tok_ref[cut, :].astype(F32) + tn(merged_t_ref[:, cut], w_ref[:, 3 * width + LANES :])
        middle_ref[cut, :] = middle
        second = middle * lax.rsqrt(jnp.mean(middle * middle, axis=-1, keepdims=True) + EPSILON)
        second_ref[cut, :] = (second * gain).astype(BF16)
    c0, c1, oh0, oh1 = places_by_row(routes_ref[...], here, local, cap)
    logits = nn(second_ref[...], misc)
    p0 = jnp.sum(jnp.where(oh0, logits, 0.0), axis=1, keepdims=True)
    p1 = jnp.sum(jnp.where(oh1, logits, 0.0), axis=1, keepdims=True)
    top = jnp.maximum(p0, p1)
    e0, e1 = jnp.exp(p0 - top), jnp.exp(p1 - top)
    g0, g1 = e0 / (e0 + e1), e1 / (e0 + e1)
    wide = iota((n, LANES), 1)
    gates_ref[...] = jnp.where(wide == 0, g0, jnp.where(wide == 1, g1, 0.0))
    for at, slot_ref in enumerate(slot_refs):
        slot_ref[...] = jnp.zeros(slot_ref.shape, F32)
        for l in range(local):
            lane = iota((n, slot_ref.shape[1]), 1) + (at * local + l) * cap
            held = jnp.where(lane == c0, g0, jnp.where(lane == c1, g1, 0.0))
            slot_ref[l : l + 1, :] = jnp.sum(held, axis=0, keepdims=True)


def forward_kernel(
    experts, local, cap, buckets, shards,
    here_ref, tok_ref, w_ref, routes_ref, routes_t_ref, bucket_ref,
    q_ref, k_ref, v_ref, normed_t_ref, merged_t_ref, middle_ref, second_ref, gates_ref, line_ref,
    *rest,
):
    groups = experts // local
    x_refs, slot_refs = rest[:experts], rest[experts : experts + groups]
    v_t_ref, twice_ref = rest[experts + groups :]
    here = here_ref[0]
    project_inputs(experts, buckets, shards, tok_ref, w_ref, bucket_ref, q_ref, k_ref, v_ref, normed_t_ref, v_t_ref, line_ref)
    attend(q_ref, k_ref, v_t_ref, line_ref, twice_ref, merged_t_ref)
    route(experts, local, cap, here, tok_ref, w_ref, routes_ref, merged_t_ref, middle_ref, second_ref, gates_ref, slot_refs)
    d0, d1 = places_by_lane(routes_t_ref[...], here, experts, local, cap)
    for at, x_ref in enumerate(x_refs):
        x_ref[...] = put_rows(second_ref[...], d0, d1, at * cap, cap)


def gelu_both(v):
    t = pl.reciprocal(1.0 + (0.3275911 * 0.7071067811865476) * jnp.abs(v))
    e = jnp.exp(-0.5 * (v * v))
    poly = 0.5 * 1.061405429
    for coefficient in (-1.453152027, 1.421413741, -0.284496736, 0.254829592):
        poly = poly * t + 0.5 * coefficient
    tail = poly * t * e
    phi = jnp.where(v < 0.0, tail, 1.0 - tail)
    return v * phi, phi + v * e * 0.3989422804014327


def expert_kernel(local_at, groups, cap, *refs):
    take = iter(refs)
    rows_in, cots_in, slots_in, up_a, up_b, down_a, down_b = (next(take) for _ in range(7))
    reply_refs = [next(take) for _ in range(groups)]
    back_refs = [next(take) for _ in range(groups)]
    dot_refs = [next(take) for _ in range(groups)]
    ug_a, ug_b, dg_a, dg_b = (next(take) for _ in range(4))
    x_ref, xt_ref, cot_ref, gr_ref, reply_ref, back_ref = (next(take) for _ in range(6))
    up_buf, down_buf, ug_buf, dg_buf, act_ref, gh_ref = (next(take) for _ in range(6))
    in_sem, out_sem, row_sem = take
    rows, width = x_ref.shape
    slab = up_a.shape[3]
    block = up_buf.shape[2]
    per = block // slab
    half = up_a.shape[1] // per
    steps = 2 * half

    def fetches(up, down, at, slot):
        for i in range(per):
            cut = slice(i * slab, (i + 1) * slab)
            yield pltpu.make_async_copy(
                up.at[local_at, at * per + i], up_buf.at[slot, :, cut], in_sem.at[slot, i]
            )
            yield pltpu.make_async_copy(
                down.at[local_at, at * per + i], down_buf.at[slot, cut, :], in_sem.at[slot, per + i]
            )

    def stores(up, down, at, slot):
        for i in range(per):
            cut = slice(i * slab, (i + 1) * slab)
            yield pltpu.make_async_copy(
                ug_buf.at[slot, :, cut], up.at[at * per + i], out_sem.at[slot, i]
            )
            yield pltpu.make_async_copy(
                dg_buf.at[slot, cut, :], down.at[at * per + i], out_sem.at[slot, per + i]
            )

    def begin(kind, first, second, step, slot):
        @pl.when(step < half)
        def _():
            for copy in kind(*first, step, slot):
                copy.start()

        @pl.when(step >= half)
        def _():
            for copy in kind(*second, step - half, slot):
                copy.start()

    begin(fetches, (up_a, down_a), (up_b, down_b), 0, 0)
    copies = []
    for m in range(groups):
        cut = slice(m * cap, (m + 1) * cap)
        copies.append(pltpu.make_async_copy(rows_in.at[local_at, m], x_ref.at[cut, :], row_sem.at[0, m]))
        copies.append(pltpu.make_async_copy(cots_in.at[local_at, m], cot_ref.at[cut, :], row_sem.at[1, m]))
    for copy in copies:
        copy.start()
    for copy in copies:
        copy.wait()
    for m in range(groups):
        cut = slice(m * cap, (m + 1) * cap)
        slots = slots_in[m, local_at : local_at + 1, :]
        gate = jnp.transpose(jnp.broadcast_to(slots, (LANES, slots.shape[1])))[:cap, 0:1]
        gr_ref[cut, :] = (gate * cot_ref[cut, :].astype(F32)).astype(BF16)
    xt_ref[...] = jnp.transpose(x_ref[...])
    reply_ref[...] = jnp.zeros_like(reply_ref)
    back_ref[...] = jnp.zeros_like(back_ref)

    def step(at, carry):
        slot = lax.rem(at, 2)

        @pl.when(at + 1 < steps)
        def _():
            begin(fetches, (up_a, down_a), (up_b, down_b), at + 1, 1 - slot)

        for copy in fetches(up_a, down_a, 0, slot):
            copy.wait()

        @pl.when(at >= 2)
        def _():
            for copy in stores(ug_a, dg_a, 0, slot):
                copy.wait()

        chunk = 256
        for c in range(rows // chunk):
            cut = slice(c * chunk, (c + 1) * chunk)
            act, slope = gelu_both(nn(x_ref[cut, :], up_buf[slot]))
            act_ref[cut, :] = act.astype(BF16)
            grad = nt(gr_ref[cut, :], down_buf[slot])
            gh_ref[cut, :] = (grad * slope).astype(BF16)
            reply_ref[cut, :] += nn(act_ref[cut, :], down_buf[slot])
            back_ref[cut, :] += nt(gh_ref[cut, :], up_buf[slot])
        dg_buf[slot] = tn(act_ref[...], gr_ref[...]).astype(BF16)
        ug_buf[slot] = nn(xt_ref[...], gh_ref[...]).astype(BF16)
        begin(stores, (ug_a, dg_a), (ug_b, dg_b), at, slot)
        return carry

    lax.fori_loop(0, steps, step, 0)
    reply = reply_ref[...].astype(BF16)
    dots = jnp.sum(reply.astype(F32) * cot_ref[...].astype(F32), axis=1, keepdims=True)
    dots = jnp.transpose(jnp.broadcast_to(dots, (rows, LANES)))[0:8]
    for m in range(groups):
        cut = slice(m * cap, (m + 1) * cap)
        reply_refs[m][...] = reply[cut]
        back_refs[m][...] = back_ref[cut, :].astype(BF16)
        shifted = dots if m == 0 else pltpu.roll(dots, rows - m * cap, 1)
        dot_refs[m][...] = shifted[:, : dot_refs[m].shape[1]]
    for slot in range(2):
        for copy in stores(ug_a, dg_a, 0, slot):
            copy.wait()


def attend_back(after, q_ref, k_ref, v_ref, gm_ref, k_t_ref, line_ref, twice_ref, gq_t_ref, gk_ref, gv_ref, fold_ref):
    n = q_ref.shape[0]
    half = iota((1, LANES), 1) < HEAD_DIM

    def pair(hp, carry):
        lanes = pl.ds(pl.multiple_of(hp * LANES, LANES), LANES)
        kp, qp, vp, gp = k_ref[:, lanes], q_ref[:, lanes], v_ref[:, lanes], gm_ref[:, lanes]
        gk = [jnp.zeros((QBLOCK, LANES), F32) for _ in range(n // QBLOCK)]
        gv = [jnp.zeros((QBLOCK, LANES), F32) for _ in range(n // QBLOCK)]
        for side in range(2):
            toeplitz(line_ref[pl.ds(hp * 2 + side, 1), :], twice_ref)
            own = hot(half if side == 0 else ~half)
            keys, values, queries, outs = kp * own, vp * own, qp * own, gp * own
            at = pl.ds(pl.multiple_of(hp * LANES + side * HEAD_DIM, HEAD_DIM), HEAD_DIM)
            folded = jnp.zeros((LANES, n), F32)
            for block in range(n // QBLOCK):
                rows = (block + 1) * QBLOCK
                cols = slice(block * QBLOCK, rows)
                scores = nt(keys[:rows], qp[cols]) + bias_columns(twice_ref, n, block, rows)
                scores = causal(scores, block)
                top = jnp.max(scores, axis=0, keepdims=True)
                e = jnp.exp(scores - top)
                probs = e * (1.0 / jnp.sum(e, axis=0, keepdims=True))
                grad_probs = nt(values[:rows], gp[cols])
                total = jnp.sum(probs * grad_probs, axis=0, keepdims=True)
                gs = (probs * (grad_probs - total)).astype(BF16)
                low = probs.astype(BF16)
                gq_t_ref[at, cols] = (nn(k_t_ref[at, :rows], gs) * SCALE).astype(BF16)
                gk_part = nn(gs, queries[cols])
                gv_part = nn(low, outs[cols])
                for b in range(block + 1):
                    cut = slice(b * QBLOCK, (b + 1) * QBLOCK)
                    gk[b] += gk_part[cut]
                    gv[b] += gv_part[cut]
                wide = gs.astype(F32)
                for jb in range(rows // LANES):
                    piece = wide[jb * LANES : (jb + 1) * LANES]
                    parts = []
                    for lb in range(n // LANES):
                        src = (lb + jb) % (n // LANES) - block * (QBLOCK // LANES)
                        inside = 0 <= src < QBLOCK // LANES
                        parts.append(
                            piece[:, src * LANES : (src + 1) * LANES]
                            if inside
                            else jnp.zeros((LANES, LANES), F32)
                        )
                    folded += jnp.concatenate(parts, axis=1)
            size = LANES
            while size > 8:
                size //= 2
                folded = folded[:size] + pltpu.roll(folded[size : 2 * size], n - size, 1)
            fold_ref[hp * 2 + side] = folded
        for b in range(n // QBLOCK):
            cut = slice(b * QBLOCK, (b + 1) * QBLOCK)
            gk_ref[cut, lanes] = gk[b].astype(BF16)
            gv_ref[cut, lanes] = gv[b].astype(BF16)
        after(hp)
        return carry

    lax.fori_loop(0, HEADS // 2, pair, 0)


def middle_back(
    experts, local, cap, here, w_ref, routes_ref, cot_ref, middle_ref, second_ref, gates_ref, back_refs, dot_refs, gmid_ref, branch_ref
):
    n, width = cot_ref.shape
    misc = w_ref[:, 3 * width : 3 * width + LANES]
    gain = jnp.transpose(misc.astype(F32))[experts + 1 : experts + 2]
    c0_all, c1_all, oh0_all, oh1_all = places_by_row(routes_ref[...], here, local, cap)
    router_grad = jnp.zeros((width, LANES), F32)
    midnorm_grad = jnp.zeros((1, width), F32)
    for cut in chunked(n):
        c0, c1, oh0, oh1 = c0_all[cut], c1_all[cut], oh0_all[cut], oh1_all[cut]
        count = c0.shape[0]
        grad_second = jnp.zeros((count, width), F32)
        gg0 = jnp.zeros((count, 1), F32)
        gg1 = jnp.zeros((count, 1), F32)
        for at in range(experts):
            lane = iota((count, cap), 1) + at * cap
            h0, h1 = lane == c0, lane == c1
            grad_second += nn(hot(h0 | h1), back_refs[at][...])
            dots = dot_refs[at][0:1, :cap]
            gg0 += jnp.sum(jnp.where(h0, dots, 0.0), axis=1, keepdims=True)
            gg1 += jnp.sum(jnp.where(h1, dots, 0.0), axis=1, keepdims=True)
        g0, g1 = gates_ref[cut, 0:1], gates_ref[cut, 1:2]
        inner = g0 * gg0 + g1 * gg1
        grad_logits = jnp.where(oh0, g0 * (gg0 - inner), jnp.where(oh1, g1 * (gg1 - inner), 0.0))
        grad_logits = grad_logits.astype(BF16)
        grad_second += nt(grad_logits, misc)
        router_grad += tn(second_ref[cut, :], grad_logits)
        middle = middle_ref[cut, :]
        r = lax.rsqrt(jnp.mean(middle * middle, axis=-1, keepdims=True) + EPSILON)
        mr = middle * r
        midnorm_grad += jnp.sum(grad_second * mr, axis=0, keepdims=True)
        u = gain * grad_second
        gmid = cot_ref[cut, :].astype(F32) + r * (u - mr * jnp.mean(u * mr, axis=-1, keepdims=True))
        gmid_ref[cut, :] = gmid
        branch_ref[cut, :] = gmid.astype(BF16)
    return router_grad, midnorm_grad


def table_back(buckets, shards, width, bucket_ref, fold_ref):
    n = bucket_ref.shape[1]
    folded = fold_ref[...].reshape(HEADS * 8, n)
    row = iota((HEADS * 8, n), 0)
    for bit in (1, 2, 4):
        folded = jnp.where((row & bit) != 0, pltpu.roll(folded, n - bit, 1), folded)
    by_distance = jnp.sum(folded.reshape(HEADS, 8, n), axis=1)
    by_distance = jnp.concatenate([by_distance, jnp.zeros((16 - HEADS, n), F32)], axis=0)
    by_bucket = hot(iota((buckets, n), 0) == bucket_ref[...])
    table_grad = jnp.zeros((buckets, 16), F32)
    for _ in range(3):
        piece = by_distance.astype(BF16)
        table_grad += nt(by_bucket, piece)
        by_distance = by_distance - piece.astype(F32)
    spread = hot(iota((16, LANES), 1) == iota((16, LANES), 0) + TABLE_AT)
    table_grad = nn(table_grad.astype(BF16), spread).astype(BF16)
    rows, per = width // shards, buckets // shards
    b = iota((width, buckets), 1)
    select = hot(iota((width, buckets), 0) == lax.div(b, per) * rows + lax.rem(b, per))
    return nn(select, table_grad)


def inputs_back(experts, tok_ref, w_ref, gq_t_ref, gk_ref, gv_ref, gmid_ref, inputs_grad_ref):
    n, width = tok_ref.shape
    misc = w_ref[:, 3 * width : 3 * width + LANES]
    gain = jnp.transpose(misc.astype(F32))[experts : experts + 1]
    prenorm_grad = jnp.zeros((1, width), F32)
    for cut in chunked(n):
        grad_normed = nt(jnp.transpose(gq_t_ref[:, cut]), w_ref[:, :width])
        grad_normed += nt(gk_ref[cut, :], w_ref[:, width : 2 * width])
        grad_normed += nt(gv_ref[cut, :], w_ref[:, 2 * width : 3 * width])
        x = tok_ref[cut, :].astype(F32)
        q = lax.rsqrt(jnp.mean(x * x, axis=-1, keepdims=True) + EPSILON)
        xq = x * q
        prenorm_grad += jnp.sum(grad_normed * xq, axis=0, keepdims=True)
        w = gain * grad_normed
        back = q * (w - xq * jnp.mean(w * xq, axis=-1, keepdims=True))
        inputs_grad_ref[cut, :] = (gmid_ref[cut, :] + back).astype(BF16)
    return prenorm_grad


def small_grads(experts, router_grad, prenorm_grad, midnorm_grad, table):
    width = prenorm_grad.shape[1]
    tall = iota((LANES, width), 0)
    gains = jnp.where(tall == experts, prenorm_grad, jnp.where(tall == experts + 1, midnorm_grad, 0.0))
    return (router_grad + jnp.transpose(gains) + table).astype(BF16)


def backward_kernel(
    experts, local, cap, buckets, shards,
    here_ref, tok_ref, w_ref, routes_ref, bucket_ref, cot_ref, q_ref, k_ref, v_ref, normed_t_ref, merged_t_ref,
    middle_ref, second_ref, gates_ref, line_ref,
    *rest,
):
    take = iter(rest)
    back_refs = [next(take) for _ in range(experts)]
    dot_refs = [next(take) for _ in range(experts)]
    inputs_grad_ref, grads_ref = next(take), next(take)
    gm_ref, gmid_ref, k_t_ref, gq_t_ref, gk_ref, gv_ref, fold_ref, twice_ref, branch_ref = take
    width = tok_ref.shape[1]
    router_grad, midnorm_grad = middle_back(
        experts, local, cap, here_ref[0], w_ref, routes_ref, cot_ref, middle_ref, second_ref, gates_ref,
        back_refs, dot_refs, gmid_ref, branch_ref,
    )
    grads_ref[:, 3 * width + LANES :] = nn(merged_t_ref[...], branch_ref[...]).astype(BF16)
    gm_ref[...] = nt(branch_ref[...], w_ref[:, 3 * width + LANES :]).astype(BF16)
    k_t_ref[...] = jnp.transpose(k_ref[...])
    attend_back(
        lambda hp: None, q_ref, k_ref, v_ref, gm_ref, k_t_ref, line_ref, twice_ref, gq_t_ref, gk_ref, gv_ref, fold_ref
    )
    normed_t = normed_t_ref[...]
    grads_ref[:, :width] = nt(normed_t, gq_t_ref[...]).astype(BF16)
    grads_ref[:, width : 2 * width] = nn(normed_t, gk_ref[...]).astype(BF16)
    grads_ref[:, 2 * width : 3 * width] = nn(normed_t, gv_ref[...]).astype(BF16)
    prenorm_grad = inputs_back(experts, tok_ref, w_ref, gq_t_ref, gk_ref, gv_ref, gmid_ref, inputs_grad_ref)
    table = table_back(buckets, shards, width, bucket_ref, fold_ref)
    grads_ref[:, 3 * width : 3 * width + LANES] = small_grads(experts, router_grad, prenorm_grad, midnorm_grad, table)


def combine(local, cap, here, routes_ref, gates_ref, middle_ref, reply_refs, out_ref):
    n, width = middle_ref.shape
    c0, c1, _, _ = places_by_row(routes_ref[...], here, local, cap)
    for cut in chunked(n):
        picked0 = jnp.zeros((cut.stop - cut.start, width), F32)
        picked1 = jnp.zeros((cut.stop - cut.start, width), F32)
        for at, reply_ref in enumerate(reply_refs):
            lane = iota((cut.stop - cut.start, cap), 1) + at * cap
            picked0 += nn(hot(lane == c0[cut]), reply_ref[...])
            picked1 += nn(hot(lane == c1[cut]), reply_ref[...])
        out = middle_ref[cut, :] + gates_ref[cut, 0:1] * picked0 + gates_ref[cut, 1:2] * picked1
        out_ref[cut, :] = out.astype(BF16)


def combine_kernel(local, cap, here_ref, routes_ref, gates_ref, middle_ref, *rest):
    *reply_refs, out_ref = rest
    combine(local, cap, here_ref[0], routes_ref, gates_ref, middle_ref, reply_refs, out_ref)


class View:
    def __init__(self, ref, index=None):
        self.ref, self.index = ref, index

    def __getitem__(self, index):
        return View(self.ref, index)

    def cut(self):
        return self.ref if self.index is None else self.ref.at[self.index]


class Window:
    def __init__(self, ref, lead, shape):
        self.ref, self.lead, self.shape = ref, lead, shape

    def whole(self, index):
        index = () if index is Ellipsis else index if isinstance(index, tuple) else (index,)
        index += (slice(None),) * (len(self.shape) - len(index))
        limited = [slice(0, size) if i == slice(None) else i for i, size in zip(index, self.shape)]
        return (*self.lead, *limited)

    def __getitem__(self, index):
        return self.ref[self.whole(index)]

    def __setitem__(self, index, value):
        self.ref[self.whole(index)] = value

    def view(self, *index):
        return View(self.ref, self.whole(index))


class Remote:
    def __init__(self, *args):
        self.args = args

    def make(self):
        src, dst, sends, receives, at, axis, peer = self.args
        return pltpu.make_async_remote_copy(
            src_ref=src.cut(),
            dst_ref=dst.cut(),
            send_sem=sends.at[at],
            recv_sem=receives.at[at],
            device_id={axis: peer},
            device_id_type=MESH,
        )

    def start(self):
        self.make().start()

    def wait_send(self):
        self.make().wait_send()

    def wait_recv(self):
        self.make().wait_recv()

    def wait(self):
        self.wait_send()
        self.wait_recv()


class Local:
    def __init__(self, *args):
        self.args = args

    def make(self):
        src, dst, sems, at = self.args
        return pltpu.make_async_copy(src.cut(), dst.cut(), sems.at[at])

    def wait(self):
        self.make().wait()


class Links:
    def __init__(self, send_sem, recv_sem, local_sem):
        self.send_sem, self.recv_sem, self.local_sem = send_sem, recv_sem, local_sem
        self.sent = self.moved = 0
        self.open_sends = []

    def send(self, src, dst, axis, peer):
        copy = Remote(src, dst, self.send_sem, self.recv_sem, self.sent, axis, peer)
        self.sent += 1
        copy.start()
        self.open_sends.append(copy)
        return copy

    def move(self, src, dst):
        copy = Local(src, dst, self.local_sem, self.moved)
        self.moved += 1
        copy.make().start()
        return copy

    def forget(self, copies):
        self.open_sends = [other for other in self.open_sends if all(copy is not other for copy in copies)]

    def close(self):
        for copy in self.open_sends:
            copy.wait_send()


SENDS, MOVES = 144, 26


def layer_kernel(experts, local, cap, buckets, shards, names, *refs):
    r = SimpleNamespace(**dict(zip(names, refs, strict=True)))
    groups = experts // local
    me, here = lax.axis_index(DP), lax.axis_index(EXPERT)
    tok_ref, cot_ref, w_ref, routes_ref, bucket_ref = r.tok, r.cot, r.w, r.routes_by_row, r.bucket
    n, width = tok_ref.shape
    rows = r.wq.shape[0]
    slab = r.up.shape[2]
    across, along, core, diagonal = me ^ 2, me ^ 4, me ^ 1, me ^ 6
    barrier = pltpu.get_barrier_semaphore()
    for peer in (across, along, core):
        pl.semaphore_signal(barrier, inc=1, device_id={DP: peer}, device_id_type=MESH)
    for m in range(1, groups):
        pl.semaphore_signal(barrier, inc=1, device_id={EXPERT: here ^ m}, device_id_type=MESH)
    pl.semaphore_wait(barrier, 3 + groups - 1)
    links = Links(r.send_sem, r.recv_sem, r.local_sem)
    send, move = links.send, links.move

    def rows_of(owner, start=0, count=rows):
        return pl.ds(pl.multiple_of(owner * rows + start, 16), count)

    d0, d1 = places_by_lane(r.routes_t[...], here, experts, local, cap)

    z_peers = [here ^ m for m in range(groups)]
    far_first = (2, 3, 1)

    def dispatch(l, values, out_ref, in_ref):
        for m in (*far_first, 0):
            cut = slice(m * cap, (m + 1) * cap)
            target = out_ref if m else in_ref
            target[l, cut, :] = put_rows(values, d0, d1, (m * local + l) * cap, cap)

    def z_send_rows(l, m, out_ref, in_ref):
        cut = slice(m * cap, (m + 1) * cap)
        return send(View(out_ref)[l, cut, :], View(in_ref)[l, cut, :], EXPERT, z_peers[m])

    cot_copies, row_copies = {}, {}
    for l in range(local):
        dispatch(l, cot_ref[...], r.out_a, r.cots)
        for m in far_first:
            if (l, m) != (local - 1, 3):
                cot_copies[l, m] = z_send_rows(l, m, r.out_a, r.cots)
    first = 3 * width + LANES
    parts = (slice(0, first), slice(first, first + width))
    mine = rows_of(me)
    w_ref[mine, 0:width] = r.wq[...]
    w_ref[mine, width : 2 * width] = r.wk[...]
    w_ref[mine, 2 * width : 3 * width] = r.wv[...]
    r.columns[...] = jnp.zeros_like(r.columns)
    r.columns[0:experts, 0:rows] = r.router_t[...].astype(F32)
    r.columns[experts : experts + 1, 0:rows] = r.gain_one[...].astype(F32)
    r.columns[experts + 1 : experts + 2, 0:rows] = r.gain_two[...].astype(F32)
    own_rows = jnp.transpose(r.columns[...])[:rows]
    r.columns[...] = jnp.zeros_like(r.columns)
    r.columns[0 : r.table.shape[0], 0:HEADS] = r.table[...].astype(F32)
    w_ref[mine, 3 * width : first] = (own_rows + pltpu.roll(r.columns[...], TABLE_AT, 1)[:rows]).astype(BF16)
    w_ref[mine, first:] = r.wo[...]

    def w_copy(part, owner, peer, start=0, count=rows):
        view = View(w_ref)[rows_of(owner, start, count), parts[part]]
        return send(view, view, DP, peer)

    w_own = [[w_copy(part, me, peer) for peer in (across, along, core)] for part in range(2)]

    tall = iota((LANES, n), 0)
    named = jnp.where(tall == 0, r.routes_t[0:1, :], jnp.where(tall == 1, r.routes_t[1:2, :], 0))
    routes_ref[...] = jnp.transpose(named.astype(F32)).astype(I32)
    half = rows // 2
    w_passed = []
    for part in range(2):
        w_own[part][0].wait_recv()
        one = w_copy(part, across, along, 0, half)
        two = w_copy(part, across, core)
        w_own[part][1].wait_recv()
        three = w_copy(part, along, across, half, half)
        four = w_copy(part, along, core)
        w_passed.append((one, three, two, four))

    kinds = ((UP, r.up, r.up_a, r.up_b), (DOWN, r.down, r.down_a, r.down_b))
    weight_copies = {}

    def weights_out(l):
        for kind, own_ref, a_ref, b_ref in kinds:
            key = (l, kind)
            weight_copies[key, OWN] = move(View(own_ref)[l], View(a_ref)[l, 0])
            weight_copies[key, (A, 1)] = send(View(own_ref)[l], View(a_ref)[l, 1], DP, across)
            weight_copies[key, (A, 2)] = send(View(own_ref)[l], View(a_ref)[l, 2], DP, along)
            weight_copies[key, (B, 0)] = send(View(own_ref)[l], View(b_ref)[l, 0], DP, core)

    def weights_on(l):
        for kind, own_ref, a_ref, b_ref in kinds:
            key = (l, kind)
            at, peer = (1, along) if kind == UP else (2, across)
            weight_copies[key, (A, at)].wait_recv()
            weight_copies[key, (A, 3)] = send(View(a_ref)[l, at], View(a_ref)[l, 3], DP, peer)
            weight_copies[key, (B, at)] = send(View(a_ref)[l, at], View(b_ref)[l, at], DP, core)
        for kind, own_ref, a_ref, b_ref in kinds:
            key = (l, kind)
            at = 2 if kind == UP else 1
            weight_copies[key, (A, at)].wait_recv()
            weight_copies[key, (B, at)] = send(View(a_ref)[l, at], View(b_ref)[l, at], DP, core)

    def weights_last(l):
        for kind, own_ref, a_ref, b_ref in kinds:
            key = (l, kind)
            weight_copies[key, (A, 3)].wait_recv()
            weight_copies[key, (B, 3)] = send(View(a_ref)[l, 3], View(b_ref)[l, 3], DP, core)

    def weights_in(l):
        for kind, *_ in kinds:
            weight_copies[(l, kind), OWN].wait()
            for at in range(4):
                weight_copies[(l, kind), (B, at)].wait_recv()

    weights_out(0)
    v_t_ref = Window(r.gh, (), (width, n))

    def w_finish(part):
        one, three, two, four = w_passed[part]
        one.wait_recv()
        three.wait_recv()
        five = w_copy(part, diagonal, core)
        for copy in (w_own[part][2], two, four, five):
            copy.wait_recv()

    w_finish(0)

    project_inputs(
        experts, buckets, shards, tok_ref, w_ref, bucket_ref, r.q, r.k, r.v, r.normed_t, v_t_ref, r.line
    )
    attend(r.q, r.k, v_t_ref, r.line, r.twice, r.merged_t)
    w_finish(1)
    slots_out, slots_in = r.slots_out, r.slots_in
    route(
        experts, local, cap, here, tok_ref, w_ref, routes_ref, r.merged_t, r.middle, r.second, r.gates,
        [slots_out.at[m] for m in range(groups)],
    )
    slot_copies = [send(View(slots_out)[m], View(slots_in)[m], EXPERT, here ^ m) for m in range(1, groups)]
    slots_in[0] = slots_out[0]
    for l in range(local):
        dispatch(l, r.second[...], r.out_b, r.rows)
        if l == 0:
            for m in far_first:
                row_copies[l, m] = z_send_rows(l, m, r.out_b, r.rows)
    weights_on(0)
    weights_out(1)
    weights_last(0)
    for m in far_first:
        row_copies[0, m].wait_send()
    cot_copies[1, 3] = z_send_rows(1, 3, r.out_a, r.cots)
    for m in far_first:
        row_copies[1, m] = z_send_rows(1, m, r.out_b, r.rows)
    weights_in(0)
    for m in far_first:
        cot_copies[0, m].wait_recv()
        row_copies[0, m].wait_recv()
    for copy in slot_copies:
        copy.wait_recv()

    up_buf, down_buf, ug_buf, dg_buf, core_buf = r.up_buf, r.down_buf, r.ug_buf, r.dg_buf, r.core_buf
    gr_ref, act_ref, gh_ref, reply_ref, back_ref = r.gr, r.act, r.gh, r.reply, r.back
    total_rows = groups * cap
    core_sems, hop_sems = (r.core_send, r.core_recv), (r.hop_send, r.hop_recv)
    back_sems = (r.back_send, r.back_recv)
    halves = [slice(i * slab, (i + 1) * slab) for i in range(2)]

    def remote(src, dst, sems, at, axis, peer):
        return pltpu.make_async_remote_copy(
            src_ref=src, dst_ref=dst, send_sem=sems[0].at[at], recv_sem=sems[1].at[at],
            device_id={axis: peer}, device_id_type=MESH,
        )

    def fetches(l, g, a_side, wait=False):
        for i in range(2):
            at = i if wait else 2 * (3 - g) + i if a_side else 2 * g + i
            up, down = (r.up_a, r.down_a) if a_side else (r.up_b, r.down_b)
            slot = lax.rem(g, 2)
            yield pltpu.make_async_copy(up.at[l, at], up_buf.at[slot, :, halves[i]], r.fetch_sem.at[slot, i])
            yield pltpu.make_async_copy(down.at[l, at], down_buf.at[slot, halves[i], :], r.fetch_sem.at[slot, 2 + i])

    def fetch(l, g):
        for a_side in (False, True):

            @pl.when((g >= 2) == a_side)
            def _():
                for copy in fetches(l, g, a_side):
                    copy.start()

    def core_copies(l, slab_at, i, out):
        at = (l * 4 + slab_at) * 2
        yield remote(ug_buf.at[out, :, halves[i]], r.core_up.at[l, slab_at], core_sems, at, DP, core)
        yield remote(dg_buf.at[out, halves[i], :], r.core_down.at[l, slab_at], core_sems, at + 1, DP, core)

    def t_copy(l, kind, i, out, half_at):
        at = l * 4 + (0 if kind == UP else 2) + i
        if kind == UP:
            return remote(ug_buf.at[out, :, halves[half_at]], r.t_up.at[l, i], hop_sems, at, DP, along)
        return remote(dg_buf.at[out, halves[half_at], :], r.t_down.at[l, i], hop_sems, at, DP, across)

    def own_moves(l, out):
        yield pltpu.make_async_copy(ug_buf.at[out, :, halves[0]], r.own_up.at[l], r.own_sem.at[0])
        yield pltpu.make_async_copy(dg_buf.at[out, halves[0], :], r.own_down.at[l], r.own_sem.at[1])

    def kept_move(l, kind, out):
        if kind == UP:
            return pltpu.make_async_copy(ug_buf.at[out, :, halves[1]], r.keep_up.at[l], r.own_sem.at[2])
        return pltpu.make_async_copy(dg_buf.at[out, halves[0], :], r.keep_down.at[l], r.own_sem.at[3])

    def sent_from(l, g, out):
        def when(condition):
            return (lambda f: f() if condition else None) if isinstance(g, int) else pl.when(condition)

        @when(g < 2)
        def _():
            for i in range(2):
                for copy in core_copies(l, 2 * g + i, i, out):
                    copy.wait_send()

        @when(g == 2)
        def _():
            for copy in (t_copy(l, UP, 0, out, 0), t_copy(l, UP, 1, out, 1), t_copy(l, DOWN, 1, out, 1)):
                copy.wait_send()
            kept_move(l, DOWN, out).wait()

        @when(g == 3)
        def _():
            t_copy(l, DOWN, 0, out, 1).wait_send()
            for copy in (*own_moves(l, out), kept_move(l, UP, out)):
                copy.wait()

    def back_copy(l, m):
        cut = slice(m * cap, (m + 1) * cap)
        at = l * (groups - 1) + m - 1
        return remote(r.out_a.at[l, cut, :], r.backs.at[l, cut, :], back_sems, at, EXPERT, here ^ m)

    def dot_copy(l, m):
        at = (local + l) * (groups - 1) + m - 1
        return remote(r.dots_out.at[l, m], r.dots_in.at[l, m], back_sems, at, EXPERT, here ^ m)

    reply_copies = {}

    def reply_send(l, m):
        reply_copies[l, m] = z_send_rows(l, m, r.out_b, r.reply_in)

    def step(s, carry):
        l, g, out = lax.div(s, 4), lax.rem(s, 4), lax.rem(s, 3)
        slot = lax.rem(g, 2)
        x, cots = r.rows.at[l], r.cots.at[l]

        @pl.when(s == 1)
        def _():
            weights_on(1)

        @pl.when(s == 3)
        def _():
            weights_last(1)

        @pl.when(s == 4)
        def _():
            weights_in(1)
            for m in far_first:
                cot_copies[1, m].wait_recv()
                row_copies[1, m].wait_recv()

        @pl.when(s == 6)
        def _():
            for m in far_first:
                back_copy(0, m).wait_send()
            for m in (2, 1):
                reply_send(0, m)

        @pl.when(g == 0)
        def _():
            fetch(l, g)
            for m in range(groups):
                cut = slice(m * cap, (m + 1) * cap)
                slots = slots_in[m, pl.ds(l, 1), :]
                gate = jnp.transpose(jnp.broadcast_to(slots, (LANES, slots.shape[1])))[:cap, 0:1]
                gr_ref[cut, :] = (gate * cots[cut, :].astype(F32)).astype(BF16)
            core_buf[...] = jnp.zeros_like(core_buf)
            reply_ref[...] = jnp.zeros_like(reply_ref)
            back_ref[...] = jnp.zeros_like(back_ref)

        for copy in fetches(l, g, False, True):
            copy.wait()

        @pl.when(g < 3)
        def _():
            fetch(l, g + 1)

        def arrivals():
            for i in range(2):
                at = 2 * (3 - g) + i
                yield pltpu.make_async_copy(r.core_up.at[l, at], core_buf.at[0, :, halves[i]], r.add_sem.at[i])
                yield pltpu.make_async_copy(r.core_down.at[l, at], core_buf.at[1, halves[i], :], r.add_sem.at[2 + i])

        @pl.when(g >= 2)
        def _():
            for i in range(2):
                for copy in core_copies(l, 2 * (3 - g) + i, i, out):
                    copy.wait_recv()
            for copy in arrivals():
                copy.start()

        for cut in chunked(total_rows):
            act, slope = gelu_both(nn(x[cut, :], up_buf[slot]))
            act_ref[cut, :] = act.astype(BF16)
            gh_ref[cut, :] = (nt(gr_ref[cut, :], down_buf[slot]) * slope).astype(BF16)
            reply_ref[cut, :] += nn(act_ref[cut, :], down_buf[slot])
            back_ref[cut, :] += nt(gh_ref[cut, :], up_buf[slot])

        @pl.when(s >= 3)
        def _():
            sent_from(lax.div(s - 3, 4), lax.rem(s - 3, 4), out)

        @pl.when(g >= 2)
        def _():
            for copy in arrivals():
                copy.wait()

        for cut in chunked(width):
            ug = tn(x[:, cut], gh_ref[...]) + core_buf[0, cut, :].astype(F32)
            ug_buf[out, cut, :] = ug.astype(BF16)
            dg = tn(act_ref[:, cut], gr_ref[...]) + core_buf[1, cut, :].astype(F32)
            dg_buf[out, cut, :] = dg.astype(BF16)

        @pl.when(g < 2)
        def _():
            for i in range(2):
                for copy in core_copies(l, 2 * g + i, i, out):
                    copy.start()

        @pl.when(g == 2)
        def _():
            t_copy(l, UP, 0, out, 0).start()
            t_copy(l, UP, 1, out, 1).start()
            t_copy(l, DOWN, 1, out, 1).start()
            kept_move(l, DOWN, out).start()

        @pl.when(g == 3)
        def _():
            t_copy(l, DOWN, 0, out, 1).start()
            for copy in own_moves(l, out):
                copy.start()
            kept_move(l, UP, out).start()
            for which in range(local):

                @pl.when(l == which)
                def _():
                    for m in far_first:
                        cot_copies[which, m].wait_send()
                        if which:
                            row_copies[which, m].wait_send()

            for m in range(groups):
                cut = slice(m * cap, (m + 1) * cap)
                if m == 0:
                    r.backs[l, cut, :] = back_ref[cut, :].astype(BF16)
                else:
                    r.out_a[l, cut, :] = back_ref[cut, :].astype(BF16)
                    back_copy(l, m).start()
            reply = reply_ref[...].astype(BF16)
            r.out_b[l] = reply
            dots = jnp.sum(reply.astype(F32) * cots[...].astype(F32), axis=1, keepdims=True)
            dots = jnp.transpose(jnp.broadcast_to(dots, (total_rows, LANES)))[0:8]
            r.dots_in[l, 0] = dots[:, :256]
            for m in range(1, groups):
                r.dots_out[l, m] = pltpu.roll(dots, total_rows - m * cap, 1)[:, :256]
                dot_copy(l, m).start()

        return carry

    lax.fori_loop(0, 4 * local, step, 0)
    links.forget([*cot_copies.values(), *row_copies.values()])
    v_copies = {}

    def t_stage(l):
        t_copy(l, UP, 1, 0, 1).wait_recv()
        t_copy(l, DOWN, 1, 0, 1).wait_recv()
        return [
            move(View(r.t_up)[l, 1], View(up_buf)[l, :, :slab]),
            move(View(r.t_down)[l, 1], View(down_buf)[l, :slab, :]),
            move(View(r.keep_up)[l], View(up_buf)[l, :, slab:]),
            move(View(r.keep_down)[l], View(down_buf)[l, slab:, :]),
        ]

    def t_pass(l, staged):
        for copy in staged:
            copy.wait()
        up_sum = up_buf[l, :, slab:].astype(F32) + up_buf[l, :, :slab].astype(F32)
        up_buf[l, :, :slab] = up_sum.astype(BF16)
        v_copies[l, UP] = send(View(up_buf)[l, :, :slab], View(r.v_up)[l], DP, across)
        down_sum = down_buf[l, slab:, :].astype(F32) + down_buf[l, :slab, :].astype(F32)
        down_buf[l, :slab, :] = down_sum.astype(BF16)
        v_copies[l, DOWN] = send(View(down_buf)[l, :slab, :], View(r.v_down)[l], DP, along)

    t_pass(0, t_stage(0))

    for l in range(local):
        for m in range(1, groups):
            back_copy(l, m).wait_recv()
            if l:
                back_copy(l, m).wait_send()
            dot_copy(l, m).wait()
    for l, m in ((0, 3), (1, 2), (1, 3), (1, 1)):
        reply_send(l, m)
    order = [(m, l) for m in range(groups) for l in range(local)]
    gm_ref, gk_ref = Window(r.rows, (0,), (n, width)), Window(r.rows, (1,), (n, width))
    gv_ref, k_t_ref = Window(r.cots, (0,), (n, width)), v_t_ref
    gq_t_ref, gmid_ref = Window(gr_ref, (), (width, n)), Window(reply_ref, (), (n, width))
    branch_ref, normed_t = Window(act_ref, (), (n, width)), r.normed_t
    router_grad, midnorm_grad = middle_back(
        experts, local, cap, here, w_ref, routes_ref, cot_ref, r.middle, r.second, r.gates,
        [Window(r.backs.at[l, m * cap : (m + 1) * cap, :], (), (cap, width)) for m, l in order],
        [r.dots_in.at[l, m] for m, l in order],
        gmid_ref, branch_ref,
    )
    r.gain_row[0:1, :] = midnorm_grad
    r.router_grad[...] = router_grad
    part = width // 2
    chunk_at = (2, 0)
    for at in range(4 * local - 3, 4 * local):
        sent_from(at // 4, at % 4, at % 3)
    for c in range(2):
        for cut in chunked(width):
            project = nn(r.merged_t[cut, :], branch_ref[:, c * part : (c + 1) * part])
            dg_buf[chunk_at[c], cut, part:] = project.astype(BF16)
    for cut in chunked(n):
        gm_ref[cut, :] = nt(branch_ref[cut, :], w_ref[:, first:]).astype(BF16)
    k_t_ref[...] = jnp.transpose(r.k[...])

    def weight_grads(c):
        at, columns = chunk_at[c], slice(c * part, (c + 1) * part)
        for cut in chunked(width):
            ug_buf[at, cut, :part] = nt(normed_t[cut, :], gq_t_ref[columns, :]).astype(BF16)
            ug_buf[at, cut, part:] = nn(normed_t[cut, :], gk_ref[:, columns]).astype(BF16)
            dg_buf[at, cut, :part] = nn(normed_t[cut, :], gv_ref[:, columns]).astype(BF16)

    peers = [me ^ mask for mask in range(8)]
    rows_at = [rows_of(peer) for peer in peers]

    class Reduce:
        def __init__(self, pieces):
            self.pieces = pieces

        def start(self):
            self.zero = []
            for g, from_core, *_ in self.pieces:
                for i in (2, 3, 1, 0):
                    copy = send(g.view(rows_at[1 ^ (2 * i)]), from_core.view(i), DP, peers[1])
                    self.zero.append((i, g, from_core, copy))

        def one(self):
            for i, g, from_core, copy in self.zero:
                copy.wait_recv()
                at = rows_at[2 * i]
                g[at, :] = (g[at, :].astype(F32) + from_core[i].astype(F32)).astype(BF16)
            self.hops = []
            for g, _, hop_one, _, mask in self.pieces:
                for i, owner in enumerate((mask, 6)):
                    self.hops.append(send(g.view(rows_at[owner]), hop_one.view(i), DP, peers[mask]))

        def two(self):
            for copy in self.hops:
                copy.wait_recv()
            self.last = []
            for g, _, hop_one, hop_two, mask in self.pieces:
                at = rows_at[6 - mask]
                g[at, :] = (g[at, :].astype(F32) + hop_one[1].astype(F32)).astype(BF16)
                self.last.append(send(g.view(at), hop_two.view(), DP, peers[6 - mask]))

        def three(self):
            for copy in self.last:
                copy.wait_recv()
            return [
                g[rows_at[0], :].astype(F32) + hop_one[0].astype(F32) + hop_two[...].astype(F32)
                for g, _, hop_one, hop_two, _ in self.pieces
            ]

    def window(ref, *lead):
        return Window(ref, lead, ref.shape[len(lead) :])

    chunks = [
        Reduce(
            [
                (window(ug_buf, chunk_at[c]), window(r.core_a, c), window(r.hop_a, c), window(r.last_a, c), 4),
                (window(dg_buf, chunk_at[c]), window(r.core_b, c), window(r.hop_b, c), window(r.last_b, c), 2),
            ]
        )
        for c in range(2)
    ]
    little = Reduce([(window(r.little), window(r.core_c), window(r.hop_c), window(r.last_c), 4)])
    z_copies, g_copies = {}, {}
    share = pl.ds(pl.multiple_of(here * part, LANES), part)

    def z_send(c):
        a, b = chunks[c].three()
        r.sum[c, :, :width] = a.astype(BF16)
        r.sum[c, :, width:] = b.astype(BF16)
        z_copies[c] = []
        for m in range(1, groups):
            cut = pl.ds(pl.multiple_of((here ^ m) * part, LANES), part)
            z_copies[c].append(send(View(r.sum)[c, :, cut], View(r.z_in)[c, m], EXPERT, here ^ m))

    def z_gather(c):
        total = r.sum[c, :, share].astype(F32)
        for m in range(1, groups):
            z_copies[c][m - 1].wait_recv()
            total += r.z_in[c, m].astype(F32)
        r.z_sum[c] = total.astype(BF16)
        g_copies[c] = [
            send(View(r.z_sum)[c], View(r.z_all)[c, m], EXPERT, here ^ m) for m in range(1, groups)
        ]
        r.main[here, :, c * part : (c + 1) * part] = r.z_sum[c]

    def z_finish(c):
        for m in range(1, groups):
            g_copies[c][m - 1].wait_recv()
            r.main[here ^ m, :, c * part : (c + 1) * part] = r.z_all[c, m]

    def after(hp):
        @pl.when(hp == 2)
        def _():
            weight_grads(0)
            chunks[0].start()

        @pl.when(hp == 3)
        def _():
            chunks[0].one()
            t_pass(1, t_stage(1))

        @pl.when(hp == 4)
        def _():
            chunks[0].two()

    attend_back(after, r.q, r.k, r.v, gm_ref, k_t_ref, r.line, r.twice, gq_t_ref, gk_ref, gv_ref, r.fold)
    weight_grads(1)
    chunks[1].start()
    z_send(0)
    prenorm_grad = inputs_back(experts, tok_ref, w_ref, gq_t_ref, gk_ref, gv_ref, gmid_ref, gm_ref)
    results = [move(gm_ref.view(), View(r.inputs_grad))]
    chunks[1].one()
    z_gather(0)
    table = table_back(buckets, shards, width, bucket_ref, r.fold)
    r.little[...] = small_grads(
        experts, r.router_grad[...], prenorm_grad, r.gain_row[0:1, :], table
    )
    little.start()
    chunks[1].two()
    little.one()
    z_finish(0)
    z_send(1)
    layer_out_ref = Window(r.cots, (1,), (n, width))
    c0, c1, _, _ = places_by_row(routes_ref[...], here, local, cap)

    def add_replies(which, first=False, last=False):
        moves = []
        for l, m in which:
            if m:
                cut = slice(m * cap, (m + 1) * cap)
                reply_copies[l, m].wait_recv()
                moves.append(move(View(r.reply_in)[l, cut, :], View(core_buf)[l, cut, :]))
        for copy in moves:
            copy.wait()
        for cut in chunked(n):
            count = cut.stop - cut.start
            picked0 = jnp.zeros((count, width), F32)
            picked1 = jnp.zeros((count, width), F32)
            for l, m in which:
                reply = (core_buf if m else r.out_b)[l, m * cap : (m + 1) * cap, :]
                lane = iota((count, cap), 1) + (m * local + l) * cap
                picked0 += nn(hot(lane == c0[cut]), reply)
                picked1 += nn(hot(lane == c1[cut]), reply)
            total = r.gates[cut, 0:1] * picked0 + r.gates[cut, 1:2] * picked1
            total += (r.middle if first else gmid_ref)[cut, :]
            if last:
                layer_out_ref[cut, :] = total.astype(BF16)
            else:
                gmid_ref[cut, :] = total

    add_replies([(0, 0), (1, 0), (0, 2), (0, 1)], first=True)
    little.two()
    z_gather(1)
    (small_sum,) = little.three()
    r.small_z[here] = small_sum.astype(BF16)
    small_copies = [
        send(View(r.small_z)[here], View(r.small_z)[here], EXPERT, z_peers[m]) for m in range(1, groups)
    ]
    add_replies([(0, 3)])
    add_replies([(1, 2), (1, 3), (1, 1)], last=True)
    results.append(move(layer_out_ref.view(), View(r.layer_out)))
    z_finish(1)
    for copy in small_copies:
        copy.wait_recv()
    total = r.small_z[0].astype(F32)
    for m in range(1, groups):
        total += r.small_z[m].astype(F32)
    turned = jnp.transpose(jnp.concatenate([total, jnp.zeros((LANES - rows, LANES), F32)], axis=0))
    r.router_out[...] = turned[0:experts, :rows]
    r.gains_out[...] = turned[experts : experts + 2, :rows]
    r.table_out[...] = pltpu.roll(total, LANES - TABLE_AT, 1)[0 : r.table.shape[0], 0:HEADS]
    for l in range(local):
        for kind in (UP, DOWN):
            t_copy(l, kind, 0, 0, 0).wait_recv()
            v_copies[l, kind].wait_recv()
    for copy in results:
        copy.wait()
    links.close()


def whole_layer(
    tokens, query_weight, key_weight, value_weight, project_weight, router_weight, prenorm_gain, midnorm_gain, bias_table,
    up_weight, down_weight, routes, bucket_row, cotangent,
):
    experts, table_rows_own = router_weight.shape[1], bias_table.shape[0]
    n, width = tokens.shape
    shards, groups = lax.axis_size(DP), lax.axis_size(EXPERT)
    local, _, slab = up_weight.shape
    buckets = table_rows_own * shards
    cap = 3 * n // experts
    rows = query_weight.shape[0]
    total = groups * cap
    vmem, hbm = pl.BlockSpec(memory_space=pltpu.VMEM), pl.BlockSpec(memory_space=pl.ANY)

    def array(*s, dtype=BF16):
        return jax.ShapeDtypeStruct(s, dtype)

    inputs = dict(
        tok=tokens, wq=query_weight, wk=key_weight, wv=value_weight, wo=project_weight,
        router_t=router_weight.T, gain_one=prenorm_gain[None, :], gain_two=midnorm_gain[None, :], table=bias_table,
        routes_t=routes.T, bucket=bucket_row, cot=cotangent, up=up_weight, down=down_weight,
    )
    near = dict(
        main=array(4, rows, width),
        router_out=array(experts, rows, dtype=F32),
        gains_out=array(2, rows, dtype=F32),
        table_out=array(table_rows_own, HEADS, dtype=F32),
    )
    far = dict(
        layer_out=array(n, width),
        inputs_grad=array(n, width),
        own_up=array(local, width, slab),
        own_down=array(local, slab, width),
        keep_up=array(local, width, slab),
        keep_down=array(local, slab, width),
        t_up=array(local, 2, width, slab),
        t_down=array(local, 2, slab, width),
        v_up=array(local, width, slab),
        v_down=array(local, slab, width),
        up_a=array(local, 4, width, slab),
        up_b=array(local, 4, width, slab),
        down_a=array(local, 4, slab, width),
        down_b=array(local, 4, slab, width),
        core_up=array(local, 4, width, slab),
        core_down=array(local, 4, slab, width),
        reply_in=array(local, total, width),
    )
    v, part = pltpu.VMEM, width // 2
    scratch = dict(
        w=v((width, 4 * width + LANES), BF16),
        out_a=v((local, total, width), BF16),
        out_b=v((local, total, width), BF16),
        rows=v((local, total, width), BF16),
        cots=v((local, total, width), BF16),
        backs=v((local, total, width), BF16),
        slots_out=v((groups, 8, 256), F32),
        slots_in=v((groups, 8, 256), F32),
        dots_out=v((local, groups, 8, 256), F32),
        dots_in=v((local, groups, 8, 256), F32),
        q=v((n, width), BF16),
        k=v((n, width), BF16),
        v=v((n, width), BF16),
        normed_t=v((width, n), BF16),
        second=v((n, width), BF16),
        merged_t=v((width, n), BF16),
        middle=v((n, width), F32),
        gates=v((n, LANES), F32),
        routes_by_row=v((n, LANES), I32),
        columns=v((LANES, LANES), F32),
        line=v((16, n), F32),
        twice=v((LANES, 2 * n), F32),
        fold=v((HEADS, 8, n), F32),
        gr=v((total, width), BF16),
        act=v((total, width), BF16),
        gh=v((total, width), BF16),
        reply=v((total, width), F32),
        back=v((total, width), F32),
        up_buf=v((2, width, width), BF16),
        down_buf=v((2, width, width), BF16),
        ug_buf=v((3, width, width), BF16),
        dg_buf=v((3, width, width), BF16),
        core_buf=v((2, width, width), BF16),
        core_a=v((2, 4, rows, width), BF16),
        core_b=v((2, 4, rows, width), BF16),
        hop_a=v((2, 2, rows, width), BF16),
        hop_b=v((2, 2, rows, width), BF16),
        last_a=v((2, rows, width), BF16),
        last_b=v((2, rows, width), BF16),
        sum=v((2, rows, 2 * width), BF16),
        z_in=v((2, groups, rows, part), BF16),
        z_sum=v((2, rows, part), BF16),
        z_all=v((2, groups, rows, part), BF16),
        little=v((width, LANES), BF16),
        gain_row=v((8, width), F32),
        router_grad=v((width, LANES), F32),
        core_c=v((4, rows, LANES), BF16),
        hop_c=v((2, rows, LANES), BF16),
        last_c=v((rows, LANES), BF16),
        small_z=v((groups, rows, LANES), BF16),
        send_sem=pltpu.SemaphoreType.DMA((SENDS,)),
        recv_sem=pltpu.SemaphoreType.DMA((SENDS,)),
        local_sem=pltpu.SemaphoreType.DMA((MOVES,)),
        fetch_sem=pltpu.SemaphoreType.DMA((2, 4)),
        add_sem=pltpu.SemaphoreType.DMA((4,)),
        own_sem=pltpu.SemaphoreType.DMA((4,)),
        core_send=pltpu.SemaphoreType.DMA((8 * local,)),
        core_recv=pltpu.SemaphoreType.DMA((8 * local,)),
        hop_send=pltpu.SemaphoreType.DMA((4 * local,)),
        hop_recv=pltpu.SemaphoreType.DMA((4 * local,)),
        back_send=pltpu.SemaphoreType.DMA((2 * local * (groups - 1),)),
        back_recv=pltpu.SemaphoreType.DMA((2 * local * (groups - 1),)),
    )
    names = [*inputs, *near, *far, *scratch]
    outs = pl.pallas_call(
        functools.partial(layer_kernel, experts, local, cap, buckets, shards, names),
        name="layer",
        out_shape=[*near.values(), *far.values()],
        in_specs=[vmem] * (len(inputs) - 2) + [hbm] * 2,
        out_specs=[vmem] * len(near) + [hbm] * len(far),
        scratch_shapes=[*scratch.values()],
        compiler_params=pltpu.CompilerParams(
            vmem_limit_bytes=LAYER_VMEM, collective_id=0, has_side_effects=True
        ),
        cost_estimate=pl.CostEstimate(flops=60 * 10**9, bytes_accessed=400 * 10**6, transcendentals=0),
    )(*inputs.values())
    o = SimpleNamespace(**dict(zip([*near, *far], outs)))

    def total_of(own, first_hop, last_hop):
        return own.astype(F32) + first_hop[:, 0].astype(F32) + last_hop.astype(F32)

    return (
        o.layer_out,
        o.inputs_grad,
        o.main[0].astype(F32),
        o.main[1].astype(F32),
        o.main[2].astype(F32),
        o.main[3].astype(F32),
        o.router_out.T,
        o.gains_out[0],
        o.gains_out[1],
        o.table_out,
        total_of(o.own_up, o.t_up, o.v_up),
        total_of(o.own_down, o.t_down, o.v_down),
    )


def swap(value, axis, bit):
    return lax.ppermute(value, axis, [(i, i ^ bit) for i in range(lax.axis_size(axis))])


def swap_all(values):
    return [v if m == 0 else swap(v, EXPERT, m) for m, v in enumerate(values)]


def body(
    tokens,
    query_weight,
    key_weight,
    value_weight,
    project_weight,
    router_weight,
    prenorm_gain,
    midnorm_gain,
    bias_table,
    up_weight,
    down_weight,
    routes,
    bucket_index,
    cotangent,
):
    n, width = tokens.shape
    experts = router_weight.shape[1]
    shards, groups = lax.axis_size(DP), lax.axis_size(EXPERT)
    local, _, slab = up_weight.shape
    cap = 3 * n // experts
    buckets = bias_table.shape[0] * shards
    own_rows = query_weight.shape[0]
    hidden = slab * shards
    direct = slab % LANES == 0 and shards == 8
    here = lax.axis_index(EXPERT).astype(I32).reshape(1)
    smem = pl.BlockSpec(memory_space=pltpu.SMEM)
    vmem = pl.BlockSpec(memory_space=pltpu.VMEM)
    hbm = pl.BlockSpec(memory_space=pl.ANY)
    routes_t = routes.T
    bucket_row = bucket_index[None, :]

    def shape(s, dtype=BF16):
        return jax.ShapeDtypeStruct(s, dtype)

    if direct:
        return whole_layer(
            tokens, query_weight, key_weight, value_weight, project_weight, router_weight, prenorm_gain, midnorm_gain,
            bias_table, up_weight, down_weight, routes, bucket_row, cotangent,
        )
    small = jnp.concatenate(
        [
            router_weight,
            prenorm_gain[:, None],
            midnorm_gain[:, None],
            jnp.zeros((own_rows, TABLE_AT - experts - 2), BF16),
            jnp.pad(bias_table, ((0, own_rows - bias_table.shape[0]), (0, 0))),
            jnp.zeros((own_rows, LANES - TABLE_AT - HEADS), BF16),
        ],
        axis=1,
    )
    packed_width = 4 * width + LANES
    slots_shape = (groups, 8, 256)
    kept = [shape((n, width))] * 3 + [
        shape((width, n)),
        shape((width, n)),
        shape((n, width), F32),
        shape((n, width)),
        shape((n, LANES), F32),
        shape((16, n), F32),
    ]
    packed = jnp.concatenate(
        [query_weight, key_weight, value_weight, small, project_weight], axis=1
    )
    full = lax.all_gather(packed, DP, axis=0, tiled=True)
    cot_out = vmem_call(
        functools.partial(scatter_kernel, experts, local, cap),
        "send_cotangent",
        [shape((cap, width))] * experts,
        specs=[smem, vmem, vmem],
    )(here, routes_t, cotangent)
    up_all = lax.all_gather(up_weight, DP, axis=2, tiled=True)
    down_all = lax.all_gather(down_weight, DP, axis=1, tiled=True)
    up_all = up_all.reshape(local, width, hidden // width, width).transpose(0, 2, 1, 3)
    down_all = down_all.reshape(local, hidden // width, width, width)
    cut = hidden // width // 2
    weights = (up_all[:, :cut], up_all[:, cut:], down_all[:, :cut], down_all[:, cut:])
    forward = vmem_call(
        functools.partial(forward_kernel, experts, local, cap, buckets, shards),
        "attention_forward",
        kept + [shape((cap, width))] * experts + [shape((8, 256), F32)] * groups,
        scratch=[pltpu.VMEM((width, n), BF16), pltpu.VMEM((LANES, 2 * n), F32)],
        specs=[smem] + [vmem] * 5,
    )(here, tokens, full, routes, routes_t, bucket_row)
    q, k, v, normed, merged_t, middle, second, gates, line = forward[:9]
    x_out, slots_out = forward[9 : 9 + experts], forward[9 + experts :]
    slots_in = jnp.stack(swap_all(slots_out))
    x_in = jnp.stack([jnp.stack(swap_all(x_out[l::local])) for l in range(local)])
    cot_in = jnp.stack([jnp.stack(swap_all(cot_out[l::local])) for l in range(local)])

    rows = groups * cap
    replies, backs, dots, up_grads, down_grads = [], [], [], [], []
    for l in range(local):
        count, slab_width = weights[0].shape[1], weights[0].shape[3]
        per = width // slab_width
        outs = pl.pallas_call(
            functools.partial(expert_kernel, l, groups, cap),
            name=EXPERT,
            out_shape=[shape((cap, width))] * (2 * groups)
            + [shape((8, 256), F32)] * groups
            + [shape((count, width, slab_width))] * 2
            + [shape((count, slab_width, width))] * 2,
            in_specs=[hbm, hbm, vmem] + [hbm] * 4,
            out_specs=[vmem] * (3 * groups) + [hbm] * 4,
            scratch_shapes=[
                pltpu.VMEM((rows, width), BF16),
                pltpu.VMEM((width, rows), BF16),
                pltpu.VMEM((rows, width), BF16),
                pltpu.VMEM((rows, width), BF16),
                pltpu.VMEM((rows, width), F32),
                pltpu.VMEM((rows, width), F32),
                pltpu.VMEM((2, width, width), BF16),
                pltpu.VMEM((2, width, width), BF16),
                pltpu.VMEM((2, width, width), BF16),
                pltpu.VMEM((2, width, width), BF16),
                pltpu.VMEM((rows, width), BF16),
                pltpu.VMEM((rows, width), BF16),
                pltpu.SemaphoreType.DMA((2, 2 * per)),
                pltpu.SemaphoreType.DMA((2, 2 * per)),
                pltpu.SemaphoreType.DMA((2, groups)),
            ],
            compiler_params=pltpu.CompilerParams(vmem_limit_bytes=VMEM_LIMIT),
            cost_estimate=pl.CostEstimate(
                flops=12 * rows * width * hidden, bytes_accessed=40 * 10**6, transcendentals=0
            ),
        )(x_in, cot_in, slots_in, *weights)
        replies.append(outs[:groups])
        backs.append(swap_all(outs[groups : 2 * groups]))
        dots.append(swap_all(outs[2 * groups : 3 * groups]))
        ug, dg = outs[3 * groups : 3 * groups + 2], outs[3 * groups + 2 :]
        ug = jnp.concatenate(ug, axis=0).transpose(1, 0, 2).reshape(width, hidden)
        dg = jnp.concatenate(dg, axis=0).reshape(hidden, width)
        up_grads.append(lax.psum_scatter(ug, DP, scatter_dimension=1, tiled=True).astype(F32))
        down_grads.append(lax.psum_scatter(dg, DP, scatter_dimension=0, tiled=True).astype(F32))

    flat = lambda parts: [parts[l][m] for m in range(groups) for l in range(local)]
    inputs_grad, grads = vmem_call(
        functools.partial(backward_kernel, experts, local, cap, buckets, shards),
        "attention_backward",
        [shape((n, width)), shape((width, packed_width))],
        scratch=[
            pltpu.VMEM((n, width), BF16),
            pltpu.VMEM((n, width), F32),
            pltpu.VMEM((width, n), BF16),
            pltpu.VMEM((width, n), BF16),
            pltpu.VMEM((n, width), BF16),
            pltpu.VMEM((n, width), BF16),
            pltpu.VMEM((HEADS, 8, n), F32),
            pltpu.VMEM((LANES, 2 * n), F32),
            pltpu.VMEM((n, width), BF16),
        ],
        specs=[smem] + [vmem] * (14 + 2 * experts),
        flops=40 * 10**9,
        moved=30 * 10**6,
    )(
        here,
        tokens,
        full,
        routes,
        bucket_row,
        cotangent,
        q,
        k,
        v,
        normed,
        merged_t,
        middle,
        second,
        gates,
        line,
        *flat(backs),
        *flat(dots),
    )
    shares = lax.psum_scatter(grads, DP, scatter_dimension=0, tiled=True)
    totals = lax.psum(shares, EXPERT).astype(F32)

    replies = flat([swap_all(r) for r in replies])
    layer_out = vmem_call(
        functools.partial(combine_kernel, local, cap),
        "layer_out",
        shape((n, width)),
        specs=[smem] + [vmem] * (3 + experts),
        flops=4 * n * experts * cap * width,
        moved=6 * 10**6,
    )(here, routes, gates, middle, *replies)

    at = 3 * width
    return (
        layer_out,
        inputs_grad,
        totals[:, :width],
        totals[:, width : 2 * width],
        totals[:, 2 * width : 3 * width],
        totals[:, at + LANES :],
        totals[:, at : at + experts],
        totals[:, at + experts],
        totals[:, at + experts + 1],
        totals[: bias_table.shape[0], at + TABLE_AT : at + TABLE_AT + HEADS],
        jnp.stack(up_grads),
        jnp.stack(down_grads),
    )


def solution(mesh):
    both, first = P((DP, EXPERT), None), P(DP, None)
    up, down = P(EXPERT, None, DP), P(EXPERT, DP, None)
    return jax.shard_map(
        body,
        mesh=mesh,
        in_specs=(both,)
        + (first,) * 5
        + (P(DP), P(DP), first, up, down, both, P(), both),
        out_specs=(both, both) + (first,) * 5 + (P(DP), P(DP), first, up, down),
        check_vma=False,
    )
```
